256 devices in a mesh: blk: 64 (over y, z, core), sub: 4 (over x).
Axes of the slice: x: 4, y: 4, z: 8, core: 2. Of those that a mesh axis runs over, the one named last changes fastest.
Arguments:
- solution: float32 [5, 64, 32, 512], P(None, 'blk', 'sub'), may hold values from -6 to 6
- right_side: float32 [5, 64, 32, 512], P(None, 'blk', 'sub'), may hold values from -6 to 6
- couple: float32 [3, 7, 5, 5], replicated, may hold values from -0.06 to 1.1, as said below
- partner: int32 [64], replicated, may hold values from 0 to 63, each once
- orient: int32 [64], replicated, may hold values from 0 to 3
- owner_one: int32 [64], replicated, may hold values from 0 to 63, each once
- owner_two: int32 [64], replicated, may hold values from 0 to 63, each once
Outputs:
- corrected: float32 [5, 64, 32, 512], P(None, 'blk', 'sub')
- coarse_one: float32 [5, 64, 16, 128], P(None, 'blk', 'sub')
- coarse_two: float32 [5, 64, 8, 32], P(None, 'blk', 'sub')
- norms: float32 [3], replicated
The draws below stay inside these ranges and needn't reach their ends.
Inputs may be any that keep to these rules, and one draw needn't show every extreme that they name: `couple`: each level's centre matrix has diagonal entries of 0.9 to 1.1 and off-diagonal entries of magnitude 0.06 or less; every coupling's entries lie in the stated range. `partner`: A permutation of the 64 blocks. `owner_one`: A permutation of the 64 blocks. `owner_two`: A permutation of the 64 blocks.
All inputs are finite; a program needn't handle non-finite values.
Results may differ from the reference program's by a relative error of at most 0.00025.
Values sent between devices are 32-bit elements; how exact they have to be, the bound alone decides.
No kernel may reach another device: no remote copies, remote signals or barrier semaphores. Data moves between devices by JAX's collectives and lax.ppermute only.
A program may use at most 64 MiB of HBM per device.

```python
import jax
import jax.numpy as jnp
from jax import lax

NV = 5
BI = 32
BJ = 16
SWEEPS_FINE = 2
SWEEPS_MID = 2
SWEEPS_COARSE = 4
NB = 64
K0 = 32
PL0 = 512


def draw_couple(key, part):
    jitter = jax.random.uniform(key, (3, 7, NV, NV), jnp.float32, -1.0, 1.0)
    diagonal = jnp.array([1.0, 0.015, 0.015, 0.015, 0.015, 0.8, 0.04], jnp.float32)
    spread = jnp.array([0.06, 0.006, 0.006, 0.006, 0.006, 0.05, 0.012], jnp.float32)
    identity = jnp.eye(NV, dtype=jnp.float32)
    leading = diagonal[None, :, None, None] * (1.0 + 0.1 * jitter)
    lateral = spread[None, :, None, None] * jitter
    return identity * leading + (1.0 - identity) * lateral


def set_ends(values, key, least, largest):
    place = [jax.random.randint(jax.random.fold_in(key, axis), (), 0, length) for axis, length in enumerate(values.shape)]
    widest = values.shape.index(max(values.shape))
    next_to = place[:widest] + [(place[widest] + 1) % values.shape[widest]] + place[widest + 1:]
    return values.at[tuple(place)].set(least).at[tuple(next_to)].set(largest)


def levels(stream_key, dims, pieces, smallest, top_value):
    def one(dim, shards_of):
        steps = jax.random.uniform(jax.random.fold_in(jax.random.fold_in(stream_key, 6), dim), (shards_of,), jnp.float32, smallest / len(pieces), top_value / len(pieces))
        return jnp.repeat(jnp.exp(steps), dims[dim] // shards_of).reshape((-1,) + (1,) * (len(dims) - dim - 1))

    gain = one(*pieces[0])
    for cut in pieces[1:]:
        gain = gain * one(*cut)
    return gain


def noise(own_key, dims, deviation, bound, split=(), kind=jnp.bfloat16):
    factor_of = levels(own_key, dims, split, -0.22, 0.18) if split else 1.0
    result = jax.random.normal(own_key, dims, jnp.float32) * deviation * factor_of
    return jnp.minimum(jnp.maximum(result, -bound), bound).astype(kind)


def setup_inputs(seed: int = 0) -> dict:
    streams_of = jax.random.split(jax.random.key(seed), 8)
    return {
        "solution": noise(streams_of[0], (NV, NB, K0, PL0), 1.0, 6.0, ((1, 64), (2, 4)), jnp.float32),
        "right_side": noise(streams_of[1], (NV, NB, K0, PL0), 1.0, 6.0, ((1, 64), (2, 4)), jnp.float32),
        "couple": draw_couple(jax.random.fold_in(streams_of[7], 71), 0),
        "partner": jax.random.permutation(streams_of[3], NB).astype(jnp.int32),
        "orient": set_ends(jax.random.randint(streams_of[4], (NB,), 0, 4), jax.random.fold_in(streams_of[4], 1), 0, 3).astype(jnp.int32),
        "owner_one": jax.random.permutation(streams_of[5], NB).astype(jnp.int32),
        "owner_two": jax.random.permutation(streams_of[6], NB).astype(jnp.int32),
    }


PRECISE = lax.Precision.HIGHEST

def apply_matrix(matrix, values):
    return jnp.einsum('ab,b...->a...', matrix, values, precision=PRECISE)

def invert(matrix):
    identity = jnp.eye(matrix.shape[0], dtype=matrix.dtype)
    approx = identity
    for repeat in range(6):
        approx = jnp.dot(approx, 2.0 * identity - jnp.dot(matrix, approx, precision=PRECISE), precision=PRECISE)
    return approx

def level_matrices(couple, level):
    center = couple[level, 0]
    inverse = invert(center)
    lateral = (couple[level, 1], couple[level, 2], couple[level, 3], couple[level, 4])
    below_coupling = couple[level, 5]
    above_coupling = couple[level, 6]
    forward = jnp.dot(inverse, below_coupling, precision=PRECISE)
    backward = jnp.dot(inverse, above_coupling, precision=PRECISE)
    return (center, inverse, lateral, below_coupling, above_coupling, forward, backward)

def in_plane(lateral, values, rows_i, rows_j):
    shaped = values.reshape(values.shape[:-1] + (rows_i, rows_j))
    pad_widths = [(0, 0)] * (shaped.ndim - 2) + [(1, 1), (1, 1)]
    padded = jnp.pad(shaped, pad_widths)
    summed = apply_matrix(lateral[0], padded[..., :-2, 1:-1]) + apply_matrix(lateral[1], padded[..., 2:, 1:-1])
    summed = summed + apply_matrix(lateral[2], padded[..., 1:-1, :-2]) + apply_matrix(lateral[3], padded[..., 1:-1, 2:])
    return summed.reshape(values.shape)

def flip_planes(planes, codes, rows_i, rows_j):
    shaped = planes.reshape(planes.shape[:-1] + (rows_i, rows_j))
    first_flip = jnp.where((codes % 2 == 1)[None, :, None, None], shaped[..., ::-1, :], shaped)
    both_flips = jnp.where((codes // 2 == 1)[None, :, None, None], first_flip[..., ::-1], first_flip)
    return both_flips.reshape(planes.shape)

def inverse_map(mapping):
    indices = jnp.arange(mapping.shape[0], dtype=jnp.int32)
    return lax.optimization_barrier(jnp.sum(jnp.where(mapping[None, :] == indices[:, None], indices[None, :], 0), axis=1)).astype(jnp.int32)

def interfaces(iterate, partner, orient, rows_i, rows_j):
    down_map = inverse_map(partner)
    below = flip_planes(iterate[:, down_map, -1, :], orient[down_map], rows_i, rows_j)
    above = flip_planes(iterate[:, partner, 0, :], orient, rows_i, rows_j)
    return (below, above)

def residual_of(iterate, source_term, matrices, partner, orient, rows_i, rows_j):
    center, inverse, lateral, below_coupling, above_coupling, forward, backward = matrices
    below, above = interfaces(iterate, partner, orient, rows_i, rows_j)
    lower = jnp.concatenate([below[:, :, None], iterate[:, :, :-1]], axis=2)
    upper = jnp.concatenate([iterate[:, :, 1:], above[:, :, None]], axis=2)
    image = apply_matrix(center, iterate) - in_plane(lateral, iterate, rows_i, rows_j)
    image = image - apply_matrix(below_coupling, lower) - apply_matrix(above_coupling, upper)
    return source_term - image

def sweep_of(iterate, source_term, matrices, partner, orient, rows_i, rows_j):
    center, inverse, lateral, below_coupling, above_coupling, forward, backward = matrices
    below, above = interfaces(iterate, partner, orient, rows_i, rows_j)
    planes_count = iterate.shape[2]
    upper = jnp.concatenate([iterate[:, :, 1:], above[:, :, None]], axis=2)
    source = source_term + in_plane(lateral, iterate, rows_i, rows_j) + apply_matrix(above_coupling, upper)
    scaled = apply_matrix(inverse, source)
    previous = below
    stacked = []
    for position in range(planes_count):
        previous = scaled[:, :, position] + apply_matrix(forward, previous)
        stacked.append(previous)
    forward_field = jnp.stack(stacked, axis=2)
    lower = jnp.concatenate([below[:, :, None], forward_field[:, :, :-1]], axis=2)
    source_back = source_term + in_plane(lateral, forward_field, rows_i, rows_j) + apply_matrix(below_coupling, lower)
    scaled_back = apply_matrix(inverse, source_back)
    following = above
    stacked_back = []
    for position in range(planes_count - 1, -1, -1):
        following = scaled_back[:, :, position] + apply_matrix(backward, following)
        stacked_back.append(following)
    return jnp.stack(stacked_back[::-1], axis=2)

def restrict(values, rows_i, rows_j):
    shape_in = values.shape
    shaped = values.reshape(shape_in[0], shape_in[1], shape_in[2] // 2, 2, rows_i // 2, 2, rows_j // 2, 2)
    averaged = lax.optimization_barrier(jnp.mean(shaped, axis=(3, 5, 7)))
    return averaged.reshape(shape_in[0], shape_in[1], shape_in[2] // 2, shape_in[3] // 4)

def prolong(values, rows_i, rows_j):
    shape_in = values.shape
    shaped = values.reshape(shape_in[0], shape_in[1], shape_in[2], 1, rows_i, 1, rows_j, 1)
    spread_out = jnp.broadcast_to(shaped, (shape_in[0], shape_in[1], shape_in[2], 2, rows_i, 2, rows_j, 2))
    return spread_out.reshape(shape_in[0], shape_in[1], shape_in[2] * 2, shape_in[3] * 4)

def reference(solution, right_side, couple, partner, orient, owner_one, owner_two):
    matrices = [level_matrices(couple, level) for level in range(3)]
    iterate = solution
    for repeat in range(SWEEPS_FINE):
        iterate = sweep_of(iterate, right_side, matrices[0], partner, orient, BI, BJ)
    residual_zero = residual_of(iterate, right_side, matrices[0], partner, orient, BI, BJ)
    source_one = restrict(residual_zero, BI, BJ)
    iterate_one = jnp.zeros_like(source_one)
    for repeat in range(SWEEPS_MID):
        iterate_one = sweep_of(iterate_one, source_one, matrices[1], partner, orient, BI // 2, BJ // 2)
    residual_one = residual_of(iterate_one, source_one, matrices[1], partner, orient, BI // 2, BJ // 2)
    source_two = restrict(residual_one, BI // 2, BJ // 2)
    iterate_two = jnp.zeros_like(source_two)
    for repeat in range(SWEEPS_COARSE):
        iterate_two = sweep_of(iterate_two, source_two, matrices[2], partner, orient, BI // 4, BJ // 4)
    residual_two = residual_of(iterate_two, source_two, matrices[2], partner, orient, BI // 4, BJ // 4)
    norms = jnp.stack([jnp.sqrt(jnp.mean(residual_zero * residual_zero)), jnp.sqrt(jnp.mean(residual_one * residual_one)), jnp.sqrt(jnp.mean(residual_two * residual_two))])
    iterate_one = iterate_one + prolong(iterate_two, BI // 4, BJ // 4)
    corrected = iterate + prolong(iterate_one, BI // 2, BJ // 2)
    coarse_one = iterate_one[:, inverse_map(owner_one)]
    coarse_two = iterate_two[:, inverse_map(owner_two)]
    return (corrected, coarse_one, coarse_two, norms)
```

```python
import functools

import jax
import jax.numpy as jnp
from jax import lax
from jax.experimental import pallas as pl
from jax.experimental.pallas import tpu as pltpu
from jax.sharding import Mesh
from jax.sharding import PartitionSpec as P

NV = 5
LANES = 128
CHIPS = 32
BLK = ("blk_0", "blk_1", "blk_2")
CHIP = ("blk_0", "blk_1")
PRECISE = lax.Precision.HIGHEST

CINV, SIDE, FORWARD, BACKWARD, CENTER, LATERAL, BELOW, ABOVE = 0, 1, 5, 10, 15, 16, 20, 21
MATRICES = 22

SUB, CHIP_DN, REL_DN, CHIP_UP, REL_UP, CODE_DN, CODE_UP, POS_OWN, POS_ONE, POS_TWO, CHIP_ONE, REL_ONE = range(12)

VMEM = pl.BlockSpec(memory_space=pltpu.VMEM)
SMEM = pl.BlockSpec(memory_space=pltpu.SMEM)


def call(kernel, out_shapes, in_specs, scratch=()):
    return pl.pallas_call(
        kernel,
        out_shape=tuple(jax.ShapeDtypeStruct(shape, jnp.float32) for shape in out_shapes),
        in_specs=in_specs,
        out_specs=tuple(VMEM for _ in out_shapes),
        scratch_shapes=list(scratch),
        compiler_params=pltpu.CompilerParams(vmem_limit_bytes=40 * 1024 * 1024),
    )


def iota(shape, dim):
    return lax.broadcasted_iota(jnp.int32, shape, dim)


def dot(a, b):
    return lax.dot_general(
        a, b, (((1,), (0,)), ((), ())), precision=PRECISE, preferred_element_type=jnp.float32
    )


def dot_nt(a, b):
    return lax.dot_general(
        a, b, (((1,), (1,)), ((), ())), precision=PRECISE, preferred_element_type=jnp.float32
    )


def times(coef, place, values, start=None):
    out = list(start) if start is not None else [None] * NV
    for a in range(NV):
        for b in range(NV):
            term = coef[place * 25 + a * NV + b] * values[b]
            out[a] = term if out[a] is None else out[a] + term
    return out


def summed(coef, terms, start):
    width = start[0].shape[1]
    parts = []
    for at in range(0, width, LANES):
        out = [x[:, at : at + LANES] for x in start]
        for place, values in terms:
            out = times(coef, place, [x[:, at : at + LANES] for x in values], out)
        parts.append(out)
    if len(parts) == 1:
        return parts[0]
    return [jnp.concatenate([part[a] for part in parts], axis=1) for a in range(NV)]


def beside(values, columns):
    shape = values[0].shape
    width = shape[1]
    lane = iota(shape, 1)
    column = lane & (columns - 1)
    cases = (
        (columns, lane >= columns),
        (width - columns, lane < width - columns),
        (1, column != 0),
        (width - 1, column != columns - 1),
    )
    return [
        [jnp.where(mask, pltpu.roll(x, shift, 1), 0.0) for x in values] for shift, mask in cases
    ]


def moved_up(x, by):
    return jnp.where(iota(x.shape, 0) >= by, pltpu.roll(x, by, 0), 0.0)


def moved_down(x, by):
    count = x.shape[0]
    return jnp.where(iota(x.shape, 0) < count - by, pltpu.roll(x, count - by, 0), 0.0)


def recurrence(coef, values, forward):
    by, place = 1, FORWARD if forward else BACKWARD
    move = moved_up if forward else moved_down
    while by < values[0].shape[0]:
        values = summed(coef, [(place, [move(x, by) for x in values])], values)
        by, place = 2 * by, place + 1
    return values


def at_ends(low, high, count):
    out = []
    for a, b in zip(low, high):
        shape = (count, a.shape[1])
        row = iota(shape, 0)
        out.append(
            jnp.where(
                row == 0,
                jnp.broadcast_to(a, shape),
                jnp.where(row == count - 1, jnp.broadcast_to(b, shape), 0.0),
            )
        )
    return out


def sweep(coef, scaled, ends, values, columns):
    base = scaled
    if ends is not None:
        low = times(coef, FORWARD, ends[0])
        high = times(coef, BACKWARD, ends[1])
        base = [x + e for x, e in zip(base, at_ends(low, high, base[0].shape[0]))]
    source = base
    if values is not None:
        terms = [(SIDE + n, x) for n, x in enumerate(beside(values, columns))]
        terms.append((BACKWARD, [moved_down(x, 1) for x in values]))
        source = summed(coef, terms, base)
    first = recurrence(coef, source, True)
    terms = [(SIDE + n, x) for n, x in enumerate(beside(first, columns))]
    terms.append((FORWARD, [moved_up(x, 1) for x in first]))
    return recurrence(coef, summed(coef, terms, base), False)


def zeros_like(values):
    return [jnp.zeros_like(x) for x in values]


def scaled_source(coef, source):
    return summed(coef, [(CINV, source)], zeros_like(source))


def residual(coef, values, source, ends, columns):
    terms = [(LATERAL + n, x) for n, x in enumerate(beside(values, columns))]
    terms.append((BELOW, [moved_up(x, 1) for x in values]))
    terms.append((ABOVE, [moved_down(x, 1) for x in values]))
    image = summed(coef, [(CENTER, values)], zeros_like(values))
    out = summed(coef, terms, [g - x for g, x in zip(source, image)])
    if ends is not None:
        low = times(coef, BELOW, ends[0])
        high = times(coef, ABOVE, ends[1])
        out = [x + e for x, e in zip(out, at_ends(low, high, out[0].shape[0]))]
    return out


def lanes_crossed(x, bits):
    width, dim = x.shape[-1], x.ndim - 1
    lane = iota(x.shape, dim)
    for bit in bits:
        step = 1 << bit
        x = jnp.where(
            (lane & step) != 0, pltpu.roll(x, step, dim), pltpu.roll(x, width - step, dim)
        )
    return x


def flipped(x, code, columns):
    code = jnp.broadcast_to(code, x.shape) if getattr(code, "ndim", 0) else jnp.full(x.shape, code, jnp.int32)
    width = x.shape[-1]
    along_j = columns.bit_length() - 1
    x = jnp.where((code & 1) == 1, lanes_crossed(x, range(along_j, width.bit_length() - 1)), x)
    return jnp.where((code & 2) == 2, lanes_crossed(x, range(along_j)), x)


def block_of(same, other, chip, rel):
    a, b = same[chip], other[chip]
    return jnp.where(jnp.full(a.shape, rel, jnp.int32) == 0, a, b)


def plane_rows(rows, chunks):
    parts = [rows[c * NV : (c + 1) * NV] for c in range(chunks)]
    return parts[0] if chunks == 1 else jnp.concatenate(parts, axis=1)


def received_ends(idx, same, other, columns):
    rows = same.shape[1] // 2
    chunks = rows // NV
    last = block_of(same, other, idx[CHIP_DN], idx[REL_DN])[rows:]
    first = block_of(same, other, idx[CHIP_UP], idx[REL_UP])[:rows]
    below = flipped(plane_rows(last, chunks), idx[CODE_DN], columns)
    above = flipped(plane_rows(first, chunks), idx[CODE_UP], columns)
    return [below[a : a + 1] for a in range(NV)], [above[a : a + 1] for a in range(NV)]


def store_ends(out, values, at=0):
    count, width = values[0].shape
    for row in (0, count - 1):
        for c in range(width // LANES):
            for a in range(NV):
                out[at : at + 1, :] = values[a][row : row + 1, c * LANES : (c + 1) * LANES]
                at += 1


def whole(ref):
    return [jnp.concatenate([ref[q, a] for q in range(4)], axis=0) for a in range(NV)]


def store_whole(ref, values):
    for a in range(NV):
        for q in range(4):
            ref[q, a] = values[a][8 * q : 8 * q + 8]


def squares(values):
    total = None
    for x in values:
        for at in range(0, x.shape[1], LANES):
            part = x[:, at : at + LANES] * x[:, at : at + LANES]
            total = part if total is None else total + part
    return jnp.sum(total, axis=0, keepdims=True)


def join_kernel(idx, p0, p1, p2, p3, field, source, ends):
    for d, piece in enumerate((p0, p1, p2, p3)):
        q = (idx[SUB] + d) & 3
        for a in range(NV):
            field[q, a] = piece[a]
            source[q, a] = piece[NV + a]
    store_ends(ends, whole(field))


def fine_kernel(coef, idx, field, source, same, other, out, ends):
    scaled = scaled_source(coef, whole(source))
    near = received_ends(idx, same, other, 16)
    values = sweep(coef, scaled, near, whole(field), 16)
    store_whole(out, values)
    store_ends(ends, values)


def first_mid_kernel(coef, coef_mid, idx, field, source, same, other, out, right, ends, total):
    near = received_ends(idx, same, other, 16)
    left = residual(coef, whole(field), whole(source), near, 16)
    total[...] = jnp.broadcast_to(squares(left), (8, LANES))
    cell, coarse = iota((512, LANES), 0), iota((512, LANES), 1)
    match = ((cell >> 5) == (coarse >> 3)) & (((cell & 15) >> 1) == (coarse & 7))
    plane_mean = jnp.where(match, 0.25, 0.0)
    pair = jnp.where((iota((16, 32), 1) >> 1) == iota((16, 32), 0), 0.5, 0.0)
    mean = dot(jnp.concatenate(left, axis=0), plane_mean)
    source_mid = [dot(pair, mean[32 * a : 32 * a + 32]) for a in range(NV)]
    values = sweep(coef_mid, scaled_source(coef_mid, source_mid), None, None, 8)
    for a in range(NV):
        out[a] = values[a]
        right[a] = source_mid[a]
    store_ends(ends, values)


def second_mid_kernel(coef, idx, field, source, same, other, total, quarter, doubled, send):
    right = [source[a] for a in range(NV)]
    near = received_ends(idx, same, other, 8)
    values = sweep(coef, scaled_source(coef, right), near, [field[a] for a in range(NV)], 8)
    for a in range(NV):
        for k in range(16):
            row = values[a][k : k + 1]
            quarter[k // 4, a * 4 + k % 4 : a * 4 + k % 4 + 1, :] = row
            at = a * 8 + 2 * (k % 4)
            doubled[k // 4, at : at + 1, :] = row
            doubled[k // 4, at + 1 : at + 2, :] = row
    left = residual(coef, values, right, None, 8)
    pair = jnp.where((iota((8, 16), 1) >> 1) == iota((8, 16), 0), 0.5, 0.0)
    mean = jnp.concatenate([dot(pair, x) for x in left], axis=0)
    cell, place = iota((LANES, LANES), 0), iota((LANES, LANES), 1)
    match_i = (cell >> 4) == (place & 7)
    column = (cell & 7) >> 1
    own_plane = (iota((8, LANES), 1) >> 4) == iota((8, LANES), 0)
    for half in range(2):
        match = match_i & (column == 2 * half + ((place >> 3) & 1))
        spread = dot(mean, jnp.where(match, 0.25, 0.0))
        for a in range(NV):
            kept = jnp.where(own_plane, spread[8 * a : 8 * a + 8], 0.0)
            at = half * NV + a
            send[at : at + 1, :] = jnp.sum(kept, axis=0, keepdims=True)
    store_ends(send, values, 10)
    store_ends(send, left, 20)
    send[30:31, :] = total[0:1]
    inner = (iota((16, LANES), 0) > 0) & (iota((16, LANES), 0) < 15)
    send[31:32, :] = squares([jnp.where(inner, x, 0.0) for x in left])


def coarse_kernel(coef, coef_mid, idx, lanes, rows, same, other, out, norms):
    groups = ((8, 8, LANES))
    lane3 = iota(groups, 2)
    side3 = iota(groups, 1)

    def sent(r):
        return jnp.concatenate(
            [ref[pl.ds(r, CHIPS, stride=32), :] for ref in (same, other)], axis=0
        )

    row = iota((LANES, LANES), 0)
    from_down = jnp.where(row == lanes[0:1, :], 1.0, 0.0)
    from_up = jnp.where(row == lanes[1:2, :], 1.0, 0.0)
    code_down, code_up = lanes[2:3, :], lanes[3:4, :]

    def flip_planes(x, code):
        code = jnp.broadcast_to(code, (8, LANES))
        side = iota((8, LANES), 0)
        out_planes = []
        for pair in x:
            turned = []
            for p in pair:
                q = pltpu.roll(p, 4, 0)
                q = jnp.where((side & 2) != 0, pltpu.roll(q, 2, 0), pltpu.roll(q, 6, 0))
                q = jnp.where((side & 1) != 0, pltpu.roll(q, 1, 0), pltpu.roll(q, 7, 0))
                turned.append(jnp.where((code & 1) == 1, q, p))
            swapped = [pltpu.roll(p, 64, 1) for p in turned[::-1]]
            out_planes.append(
                [jnp.where((code & 2) == 2, s, p) for s, p in zip(swapped, turned)]
            )
        return out_planes

    def mapped(planes, chosen, code):
        got = dot(planes, chosen)
        pairs = [
            [got[16 * a + 8 * p : 16 * a + 8 * p + 8] for p in range(2)] for a in range(NV)
        ]
        return flip_planes(pairs, code)

    source = []
    for a in range(NV):
        both = jnp.concatenate([sent(a), sent(NV + a)], axis=0)
        turned = both.T.reshape(8, 2, 8, LANES)
        source.append([turned[:, 0], turned[:, 1]])
    cell = iota((32, LANES), 1)
    place = iota((32, LANES), 0)
    match = ((cell >> 4) == (place & 7)) & (((cell & 7) >> 1) == (place >> 3))
    mean = jnp.where(match, 0.25, 0.0)

    def restricted(first_row):
        out_rows = []
        for a in range(NV):
            got = dot_nt(mean, sent(first_row + a))
            out_rows.append(jnp.concatenate([got[:16], got[16:]], axis=1))
        return jnp.concatenate(out_rows, axis=0)

    mid_below = mapped(restricted(15), from_down, code_down)
    mid_above = mapped(restricted(10), from_up, code_up)
    for p in range(2):
        low = times(coef_mid, BELOW, [0.5 * x[p] for x in mid_below])
        high = times(coef_mid, ABOVE, [0.5 * x[p] for x in mid_above])
        for a in range(NV):
            g = source[a][p]
            source[a][p] = jnp.concatenate(
                [g[:1] + low[a][None], g[1:7], g[7:] + high[a][None]], axis=0
            )

    block_row, block_lane = rows[...], iota((64, 64), 1)
    total_zero = sent(30)
    total_one = sent(31)
    for first_row, end_row, place_at, matrix in ((15, 20, 0, BELOW), (10, 25, 1, ABOVE)):
        chosen = jnp.where(block_row[place_at][:, :64] == block_lane, 1.0, 0.0)
        got = dot(chosen, jnp.concatenate([sent(first_row + a) for a in range(NV)], axis=1))
        got = [got[:, a * LANES : (a + 1) * LANES] for a in range(NV)]
        got = [flipped(x, block_row[2 + place_at], 8) for x in got]
        for x in times(coef_mid, matrix, got, [sent(end_row + a) for a in range(NV)]):
            total_one = total_one + x * x

    def pairwise(terms, start):
        out_pairs = [[None, None] for _ in range(NV)]
        for p in range(2):
            got = [x[p] for x in start]
            for place_of, values in terms:
                got = times(coef, place_of, [x[p] for x in values], got)
            for a in range(NV):
                out_pairs[a][p] = got[a]
        return out_pairs

    def beside_coarse(values):
        low = [[jnp.where(side3 > 0, pltpu.roll(x, 1, 1), 0.0) for x in pair] for pair in values]
        high = [[jnp.where(side3 < 7, pltpu.roll(x, 7, 1), 0.0) for x in pair] for pair in values]
        left = [
            [jnp.where(lane3 >= 64, pltpu.roll(pair[1], 64, 2), 0.0), pair[0]] for pair in values
        ]
        right = [
            [pair[1], jnp.where(lane3 < 64, pltpu.roll(pair[0], 64, 2), 0.0)] for pair in values
        ]
        return [low, high, left, right]

    def lifted(values, ghost):
        return [
            [jnp.concatenate([g[None], x[:7]], axis=0) for g, x in zip(gp, pair)]
            for gp, pair in zip(ghost, values)
        ]

    def lowered(values, ghost):
        return [
            [jnp.concatenate([x[1:], g[None]], axis=0) for g, x in zip(gp, pair)]
            for gp, pair in zip(ghost, values)
        ]

    def carried(values, ghost, forward):
        place_of = FORWARD if forward else BACKWARD
        out_pairs = [[None, None] for _ in range(NV)]
        for p in range(2):
            before = None if ghost is None else [x[p] for x in ghost]
            planes = [None] * 8
            for k in range(8) if forward else range(7, -1, -1):
                own = [x[p][k] for x in values]
                before = own if before is None else times(coef, place_of, before, own)
                planes[k] = before
            for a in range(NV):
                out_pairs[a][p] = jnp.stack([planes[k][a] for k in range(8)], axis=0)
        return out_pairs

    def edge(values, k):
        return jnp.concatenate([x[p][k] for x in values for p in range(2)], axis=0)

    def neighbours(values):
        below = mapped(edge(values, 7), from_down, code_down)
        above = mapped(edge(values, 0), from_up, code_up)
        return below, above

    nothing = [[jnp.zeros((8, LANES), jnp.float32)] * 2 for _ in range(NV)]
    empty = [[jnp.zeros(groups, jnp.float32)] * 2 for _ in range(NV)]
    scaled = pairwise([(CINV, source)], empty)
    values = None
    for _ in range(4):
        start = scaled
        below = above = None
        if values is not None:
            below, above = neighbours(values)
            terms = [(SIDE + n, x) for n, x in enumerate(beside_coarse(values))]
            terms.append((BACKWARD, lowered(values, above)))
            start = pairwise(terms, scaled)
        first = carried(start, below, True)
        terms = [(SIDE + n, x) for n, x in enumerate(beside_coarse(first))]
        terms.append((FORWARD, lifted(first, nothing if below is None else below)))
        values = carried(pairwise(terms, scaled), above, False)

    below, above = neighbours(values)
    image = pairwise([(CENTER, values)], empty)
    terms = [(LATERAL + n, x) for n, x in enumerate(beside_coarse(values))]
    terms += [(BELOW, lifted(values, below)), (ABOVE, lowered(values, above))]
    start = [[g - x for g, x in zip(gp, pair)] for gp, pair in zip(source, image)]
    total_two = None
    for pair in pairwise(terms, start):
        for x in pair:
            part = jnp.sum(x * x, axis=0)
            total_two = part if total_two is None else total_two + part

    lane = iota((8, LANES), 1)
    result = jnp.zeros((8, LANES), jnp.float32)
    sizes = (NV * 64 * 32 * 512, NV * 64 * 16 * 128, NV * 64 * 8 * 32)
    for level, total in enumerate((total_zero, total_one, total_two)):
        total = jnp.sum(jnp.sum(total, axis=0, keepdims=True), axis=1, keepdims=True)
        root = jnp.sqrt(jnp.broadcast_to(total, (8, LANES)) / float(sizes[level]))
        result = jnp.where(lane == level, root, result)
    norms[...] = result

    which = iota((8, LANES), 0)
    wanted = jnp.where(
        which < 2,
        jnp.full((8, LANES), idx[POS_OWN], jnp.int32),
        jnp.where(
            which < 4,
            jnp.full((8, LANES), idx[POS_ONE], jnp.int32),
            jnp.full((8, LANES), idx[POS_TWO], jnp.int32),
        ),
    )
    chosen = jnp.where(lane == wanted + 64 * (which & 1), 1.0, 0.0)
    for a in range(NV):
        laid = jnp.stack(values[a], axis=1).reshape(LANES, LANES)
        out[a] = dot_nt(chosen, laid)


def last_kernel(idx, field, doubled, same, other, coarse, corrected, one, two):
    s = idx[SUB]
    row = iota((2 * LANES, LANES), 0)
    cell = iota((2 * LANES, LANES), 1)
    half, inner_j, inner_i = row >> 7, (row >> 3) & 1, row & 7
    fits = (inner_i == (cell >> 4)) & (2 * half + inner_j == ((cell & 7) >> 1))
    to_mid = jnp.where(fits, 1.0, 0.0)
    fits = (inner_i == (cell >> 2)) & (2 * half + inner_j == (cell & 3)) & (cell < 32)
    to_cells = jnp.where(fits, 1.0, 0.0)

    def laid(which, count, shift):
        parts = []
        shape = (count, 2 * LANES)
        plane = (iota(shape, 1) >> 4) & 7
        wanted = 2 * s + (iota(shape, 0) >> shift)
        for a in range(NV):
            pair = jnp.concatenate(
                [coarse[a, 2 * which : 2 * which + 1, :], coarse[a, 2 * which + 1 : 2 * which + 2, :]], axis=1
            )
            parts.append(jnp.where(plane == wanted, jnp.broadcast_to(pair, shape), 0.0))
        return parts

    x_one = doubled[s] + dot(jnp.concatenate(laid(0, 8, 2), axis=0), to_mid)
    mid, fine = iota((LANES, 512), 0), iota((LANES, 512), 1)
    fits = ((fine >> 5) == (mid >> 3)) & (((fine & 15) >> 1) == (mid & 7))
    spread = dot(x_one, jnp.where(fits, 1.0, 0.0))
    for a in range(NV):
        corrected[a] = field[s, a] + spread[8 * a : 8 * a + 8]
    held = block_of(same, other, idx[CHIP_ONE], idx[REL_ONE])
    for a, part in enumerate(laid(1, 8, 1)):
        got = dot(part, to_mid)
        one[a] = held[4 * a : 4 * a + 4] + got[:4]
    for a, part in enumerate(laid(2, 8, 0)):
        two[a] = dot(part, to_cells)[:2, :32]


def product(a, b):
    return jnp.einsum("...ab,...bc->...ac", a, b, precision=PRECISE)


def coefficients(couple):
    center = couple[:, 0]
    identity = jnp.broadcast_to(jnp.eye(NV, dtype=jnp.float32), center.shape)
    inverse = identity
    for _ in range(6):
        inverse = product(inverse, 2.0 * identity - product(center, inverse))
    scaled = product(inverse[:, None], couple[:, 1:])
    powers = [scaled[:, 4:]]
    for _ in range(4):
        powers.append(product(powers[-1], powers[-1]))
    powers = jnp.stack(powers, axis=2).reshape(3, 10, NV, NV)
    listed = jnp.concatenate([inverse[:, None], scaled[:, :4], powers, couple], axis=1)
    return listed.reshape(3, MATRICES * 25)


def inverse_map(mapping):
    slots = jnp.arange(mapping.shape[0], dtype=jnp.int32)
    return jnp.sum(jnp.where(mapping[None, :] == slots[:, None], slots[None, :], 0), axis=1)


def gathered(payload):
    copies = jnp.broadcast_to(payload, (CHIPS, *payload.shape))
    same = lax.all_to_all(copies, CHIP, split_axis=0, concat_axis=0, tiled=True)
    other = lax.ppermute(same, "blk_2", [(0, 1), (1, 0)])
    return same, other


def shards(solution, right_side, couple, partner, orient, owner_one, owner_two):
    core = lax.axis_index("blk_2")
    device = lax.axis_index(BLK)
    sub = lax.axis_index("sub")

    own = jnp.concatenate([solution[:, 0], right_side[:, 0]], axis=0)
    pieces = [own]
    for d in range(1, 4):
        pieces.append(lax.ppermute(own, "sub", [((i + d) % 4, i) for i in range(4)]))

    coef = coefficients(couple)
    slots = jnp.arange(64, dtype=jnp.int32)
    down_map = inverse_map(partner)
    held_one = inverse_map(owner_one)[device]
    held_two = inverse_map(owner_two)[device]

    def chip(b):
        return b // 2

    def rel(b):
        return (b % 2) ^ core

    def pos(b):
        return rel(b) * CHIPS + chip(b)

    down, up = down_map[device], partner[device]
    idx = jnp.stack(
        [sub, chip(down), rel(down), chip(up), rel(up), orient[down], orient[device]]
        + [pos(device), pos(held_one), pos(held_two), chip(held_one), rel(held_one)]
    ).astype(jnp.int32)
    listed = (slots % CHIPS) * 2 + ((slots // CHIPS) ^ core)
    down_of, up_of = down_map[listed], partner[listed]
    table = jnp.stack([pos(down_of), pos(up_of), orient[down_of], orient[listed]])
    halves = jnp.array([0, 64], jnp.int32)[None, :, None] * jnp.array([1, 1, 0, 0], jnp.int32)[:, None, None]
    lanes = (table[:, None] + halves).reshape(4, LANES)
    lanes = jnp.concatenate([lanes, jnp.zeros_like(lanes)], axis=0)
    rows = jnp.broadcast_to(table[:, :, None], (4, 64, LANES))

    whole_shape, ends_shape = (4, NV, 8, 512), (40, LANES)
    mid_shape = (NV, 16, LANES)
    field, source, ends = call(
        join_kernel, [whole_shape, whole_shape, ends_shape], [SMEM] + [VMEM] * 4
    )(idx, *pieces)
    fine = call(fine_kernel, [whole_shape, ends_shape], [SMEM, SMEM] + [VMEM] * 4)
    for _ in range(2):
        field, ends = fine(coef[0], idx, field, source, *gathered(ends))
    x_one, source_one, ends, total = call(
        first_mid_kernel,
        [mid_shape, mid_shape, (10, LANES), (8, LANES)],
        [SMEM] * 3 + [VMEM] * 4,
    )(coef[0], coef[1], idx, field, source, *gathered(ends))
    quarter, doubled, send = call(
        second_mid_kernel,
        [(4, 20, LANES), (4, 40, LANES), (32, LANES)],
        [SMEM] * 2 + [VMEM] * 5,
    )(coef[1], idx, x_one, source_one, *gathered(ends), total)
    got = [x.reshape(CHIPS * 32, LANES) for x in gathered(send)]
    held = gathered(lax.dynamic_index_in_dim(quarter, sub, 0, keepdims=False))
    coarse, norms = call(
        coarse_kernel, [(NV, 8, LANES), (8, LANES)], [SMEM] * 3 + [VMEM] * 4
    )(coef[2], coef[1], idx, lanes, rows, *got)
    corrected, one, two = call(
        last_kernel, [(NV, 8, 512), (NV, 4, LANES), (NV, 2, 32)], [SMEM] + [VMEM] * 5
    )(idx, field, doubled, *held, coarse)
    return (corrected[:, None], one[:, None], two[:, None], norms[0, :3])


def solution(mesh):
    torus = Mesh(
        mesh.devices.reshape(4, 8, 2, mesh.shape["sub"]), ("blk_0", "blk_1", "blk_2", "sub")
    )
    split = P(None, BLK, "sub", None)
    return jax.shard_map(
        shards,
        mesh=torus,
        in_specs=(split, split, P(), P(), P(), P(), P()),
        out_specs=(split, split, split, P()),
        check_vma=False,
    )
```

```python
import functools

import jax
import jax.numpy as jnp
from jax import lax
from jax.experimental import pallas as pl
from jax.experimental.pallas import tpu as pltpu
from jax.sharding import Mesh
from jax.sharding import PartitionSpec as P

NV = 5
LANES = 128
CHIPS = 32
BLK = ("blk_0", "blk_1", "blk_2")
CHIP = ("blk_0", "blk_1")
PRECISE = lax.Precision.HIGHEST

CINV, SIDE, FORWARD, BACKWARD, CENTER, LATERAL, BELOW, ABOVE = 0, 1, 5, 10, 15, 16, 20, 21
MATRICES = 22

SUB, CORE, POS_OWN, POS_ONE, POS_TWO, CHIP_ONE, REL_ONE = range(7)
DOWN, UP, DOWN_TWO, UP_TWO = 8, 11, 14, 17
PLACES = 20

END_ROWS, LEFT_ROWS, TOTAL_ROW, QUARTER_ROWS, SENT_ROWS = 10, 20, 30, 31, 56

VMEM = pl.BlockSpec(memory_space=pltpu.VMEM)
SMEM = pl.BlockSpec(memory_space=pltpu.SMEM)


def call(kernel, out_shapes, in_specs, scratch=()):
    return pl.pallas_call(
        kernel,
        out_shape=tuple(jax.ShapeDtypeStruct(shape, jnp.float32) for shape in out_shapes),
        in_specs=in_specs,
        out_specs=tuple(VMEM for _ in out_shapes),
        scratch_shapes=list(scratch),
        compiler_params=pltpu.CompilerParams(vmem_limit_bytes=40 * 1024 * 1024),
    )


def iota(shape, dim):
    return lax.broadcasted_iota(jnp.int32, shape, dim)


def dot(a, b):
    return lax.dot_general(
        a, b, (((1,), (0,)), ((), ())), precision=PRECISE, preferred_element_type=jnp.float32
    )


def dot_nt(a, b):
    return lax.dot_general(
        a, b, (((1,), (1,)), ((), ())), precision=PRECISE, preferred_element_type=jnp.float32
    )


def times(coef, place, values, start=None):
    out = list(start) if start is not None else [None] * NV
    for a in range(NV):
        for b in range(NV):
            term = coef[place * 25 + a * NV + b] * values[b]
            out[a] = term if out[a] is None else out[a] + term
    return out


def summed(coef, terms, start):
    width = start[0].shape[1]
    parts = []
    for at in range(0, width, LANES):
        out = [x[:, at : at + LANES] for x in start]
        for place, values in terms:
            out = times(coef, place, [x[:, at : at + LANES] for x in values], out)
        parts.append(out)
    if len(parts) == 1:
        return parts[0]
    return [jnp.concatenate([part[a] for part in parts], axis=1) for a in range(NV)]


def beside(values, columns, cells):
    shape = values[0].shape
    width = shape[1]
    cell = iota(shape, 1) & (cells - 1)
    column = cell & (columns - 1)
    cases = (
        (columns, cell >= columns),
        (width - columns, cell < cells - columns),
        (1, column != 0),
        (width - 1, column != columns - 1),
    )
    return [
        [jnp.where(mask, pltpu.roll(x, shift, 1), 0.0) for x in values] for shift, mask in cases
    ]


def moved_up(x, by):
    return jnp.where(iota(x.shape, 0) >= by, pltpu.roll(x, by, 0), 0.0)


def moved_down(x, by):
    count = x.shape[0]
    return jnp.where(iota(x.shape, 0) < count - by, pltpu.roll(x, count - by, 0), 0.0)


def recurrence(coef, values, forward):
    by, place = 1, FORWARD if forward else BACKWARD
    move = moved_up if forward else moved_down
    while by < values[0].shape[0]:
        values = summed(coef, [(place, [move(x, by) for x in values])], values)
        by, place = 2 * by, place + 1
    return values


def at_ends(low, high, count):
    out = []
    for a, b in zip(low, high):
        shape = (count, a.shape[1])
        row = iota(shape, 0)
        out.append(
            jnp.where(
                row == 0,
                jnp.broadcast_to(a, shape),
                jnp.where(row == count - 1, jnp.broadcast_to(b, shape), 0.0),
            )
        )
    return out


def sweep(coef, scaled, ends, values, columns, cells):
    base = scaled
    if ends is not None:
        low = times(coef, FORWARD, ends[0])
        high = times(coef, BACKWARD, ends[1])
        base = [x + e for x, e in zip(base, at_ends(low, high, base[0].shape[0]))]
    source = base
    if values is not None:
        terms = [(SIDE + n, x) for n, x in enumerate(beside(values, columns, cells))]
        terms.append((BACKWARD, [moved_down(x, 1) for x in values]))
        source = summed(coef, terms, base)
    first = recurrence(coef, source, True)
    terms = [(SIDE + n, x) for n, x in enumerate(beside(first, columns, cells))]
    terms.append((FORWARD, [moved_up(x, 1) for x in first]))
    return recurrence(coef, summed(coef, terms, base), False)


def zeros_like(values):
    return [jnp.zeros_like(x) for x in values]


def scaled_source(coef, source):
    return summed(coef, [(CINV, source)], zeros_like(source))


def local_residual(coef, values, source, columns, cells):
    terms = [(LATERAL + n, x) for n, x in enumerate(beside(values, columns, cells))]
    terms.append((BELOW, [moved_up(x, 1) for x in values]))
    terms.append((ABOVE, [moved_down(x, 1) for x in values]))
    image = summed(coef, [(CENTER, values)], zeros_like(values))
    return summed(coef, terms, [g - x for g, x in zip(source, image)])


def lanes_crossed(x, bits):
    width, dim = x.shape[-1], x.ndim - 1
    lane = iota(x.shape, dim)
    for bit in bits:
        step = 1 << bit
        x = jnp.where(
            (lane & step) != 0, pltpu.roll(x, step, dim), pltpu.roll(x, width - step, dim)
        )
    return x


def flipped(x, code, columns):
    code = jnp.broadcast_to(code, x.shape) if getattr(code, "ndim", 0) else jnp.full(x.shape, code, jnp.int32)
    width = x.shape[-1]
    along_j = columns.bit_length() - 1
    x = jnp.where((code & 1) == 1, lanes_crossed(x, range(along_j, width.bit_length() - 1)), x)
    return jnp.where((code & 2) == 2, lanes_crossed(x, range(along_j)), x)


def block_of(same, other, chip, rel):
    a, b = same[chip], other[chip]
    return jnp.where(jnp.full(a.shape, rel, jnp.int32) == 0, a, b)


def plane_rows(rows, chunks):
    parts = [rows[c * NV : (c + 1) * NV] for c in range(chunks)]
    return parts[0] if chunks == 1 else jnp.concatenate(parts, axis=1)


def sent_by(idx, same, other, place):
    return block_of(same, other, idx[place], idx[place + 1])


def listed_rows(x):
    return [x[a : a + 1] for a in range(NV)]


def received_ends(idx, same, other):
    below = flipped(plane_rows(sent_by(idx, same, other, DOWN)[20:40], 4), idx[DOWN + 2], 16)
    above = flipped(plane_rows(sent_by(idx, same, other, UP)[:20], 4), idx[UP + 2], 16)
    return listed_rows(below), listed_rows(above)


def store_ends(out, values, at=0):
    count, width = values[0].shape
    for row in (0, count - 1):
        for c in range(width // LANES):
            for a in range(NV):
                out[at : at + 1, :] = values[a][row : row + 1, c * LANES : (c + 1) * LANES]
                at += 1


def whole(ref):
    return [jnp.concatenate([ref[q, a] for q in range(4)], axis=0) for a in range(NV)]


def store_whole(ref, values):
    for a in range(NV):
        for q in range(4):
            ref[q, a] = values[a][8 * q : 8 * q + 8]


def squares(values):
    total = None
    for x in values:
        for at in range(0, x.shape[1], LANES):
            part = x[:, at : at + LANES] * x[:, at : at + LANES]
            total = part if total is None else total + part
    return jnp.sum(total, axis=0, keepdims=True)


def index_kernel(partner, orient, owner_one, owner_two, idx):
    device = lax.axis_index(BLK)
    core = lax.axis_index("blk_2")
    idx[SUB] = lax.axis_index("sub")
    idx[CORE] = core

    def find(j, found):
        down, one, two = found
        return (
            jnp.where(partner[j] == device, j, down),
            jnp.where(owner_one[j] == device, j, one),
            jnp.where(owner_two[j] == device, j, two),
        )

    zero = jnp.int32(0)
    down, one, two = lax.fori_loop(0, 64, find, (zero, zero, zero), unroll=8)
    down_two = lax.fori_loop(
        0, 64, lambda j, found: jnp.where(partner[j] == down, j, found), zero, unroll=8
    )
    up = partner[device]
    up_two = partner[up]
    for place, block in ((POS_OWN, device), (POS_ONE, one), (POS_TWO, two)):
        idx[place] = ((block & 1) ^ core) * CHIPS + (block >> 1)
    idx[CHIP_ONE] = one >> 1
    idx[REL_ONE] = (one & 1) ^ core
    places = ((DOWN, down, down), (UP, up, device), (DOWN_TWO, down_two, down_two), (UP_TWO, up_two, up))
    for place, block, crossing in places:
        idx[place] = block >> 1
        idx[place + 1] = (block & 1) ^ core
        idx[place + 2] = orient[crossing]
    idx[7] = zero


def pick_kernel(idx, same, other, out):
    lowest = idx[SUB] == 0
    chip = jnp.where(lowest, idx[UP], idx[DOWN])
    rel = jnp.where(lowest, idx[UP + 1], idx[DOWN + 1])
    out[...] = block_of(same, other, chip, rel)


def first_fine_kernel(coef, idx, p0, p1, p2, p3, e0, e1, e2, e3, out, source, ends, field):
    for d, piece in enumerate((p0, p1, p2, p3)):
        q = (idx[SUB] + d) & 3
        for a in range(NV):
            field[q, a] = piece[a]
            source[q, a] = piece[NV + a]
    below = above = e0[...]
    for d, end in ((1, e1), (2, e2), (3, e3)):
        q = jnp.full(below.shape, (idx[SUB] + d) & 3, jnp.int32)
        above = jnp.where(q == 0, end[...], above)
        below = jnp.where(q == 3, end[...], below)
    near = (
        listed_rows(flipped(plane_rows(below, 4), idx[DOWN + 2], 16)),
        listed_rows(flipped(plane_rows(above, 4), idx[UP + 2], 16)),
    )
    values = sweep(coef, scaled_source(coef, whole(source)), near, whole(field), 16, 512)
    store_whole(out, values)
    store_ends(ends, values)


def plane_mean():
    cell, coarse = iota((512, LANES), 0), iota((512, LANES), 1)
    match = ((cell >> 5) == (coarse >> 3)) & (((cell & 15) >> 1) == (coarse & 7))
    return jnp.where(match, 0.25, 0.0)


def second_fine_kernel(
    coef, coef_mid, idx, field, source, same, other, out, edges, total, mid, right, send
):
    near = received_ends(idx, same, other)
    given = whole(source)
    values = sweep(coef, scaled_source(coef, given), near, whole(field), 16, 512)
    store_whole(out, values)
    left = local_residual(coef, values, given, 16, 512)
    edges[...] = jnp.zeros((16, 512), jnp.float32)
    for a in range(NV):
        edges[a : a + 1, :] = left[a][:1]
        edges[8 + a : 9 + a, :] = left[a][31:]
    row = iota((32, 512), 0)
    inner = (row > 0) & (row < 31)
    total[...] = jnp.broadcast_to(squares([jnp.where(inner, x, 0.0) for x in left]), (8, LANES))
    pair = jnp.where((iota((16, 32), 1) >> 1) == iota((16, 32), 0), 0.5, 0.0)
    mean = dot(jnp.concatenate(left, axis=0), plane_mean())
    source_mid = [dot(pair, mean[32 * a : 32 * a + 32]) for a in range(NV)]
    reply = sweep(coef_mid, scaled_source(coef_mid, source_mid), None, None, 8, LANES)
    for a in range(NV):
        mid[a] = reply[a]
        right[a] = source_mid[a]
    store_ends(send, values)
    store_ends(send, reply, 40)


def mid_kernel(
    coef_fine, coef, idx, same, other, sent, edges, total, mid, right, doubled, send, quarter
):
    down, up = sent_by(idx, same, other, DOWN), sent_by(idx, same, other, UP)
    down_two, up_two = sent_by(idx, same, other, DOWN_TWO), sent_by(idx, same, other, UP_TWO)
    own = sent[...]
    first, last = slice(0, 20), slice(20, 40)
    below = flipped(plane_rows(down[last], 4), idx[DOWN + 2], 16)
    above = flipped(plane_rows(up[first], 4), idx[UP + 2], 16)

    low = times(coef_fine, BELOW, listed_rows(below), [edges[a : a + 1, :] for a in range(NV)])
    high = times(coef_fine, ABOVE, listed_rows(above), [edges[8 + a : 9 + a, :] for a in range(NV)])
    total_zero = total[:1] + squares(low) + squares(high)

    gap = jnp.zeros((3, 512), jnp.float32)
    planes = [below, plane_rows(own[last], 4), plane_rows(down_two[last], 4)]
    planes += [above, plane_rows(up_two[first], 4), plane_rows(own[first], 4)]
    stacked = jnp.concatenate([part for x in planes for part in (x, gap)], axis=0)
    mean = dot(stacked, plane_mean())
    mean = [mean[8 * n : 8 * n + NV] for n in range(6)]
    codes = (idx[UP + 2], idx[DOWN_TWO + 2], idx[UP_TWO + 2], idx[DOWN + 2])
    for n, code in zip((1, 2, 4, 5), codes):
        mean[n] = flipped(mean[n], code, 8)
    lows = listed_rows(0.5 * jnp.concatenate(mean[:3], axis=1))
    highs = listed_rows(0.5 * jnp.concatenate(mean[3:], axis=1))
    added = at_ends(times(coef_fine, BELOW, lows), times(coef_fine, ABOVE, highs), 16)
    reply = sweep(coef, scaled_source(coef, added), None, None, 8, LANES)

    field = [mid[a] + reply[a][:, :LANES] for a in range(NV)]
    source = [right[a] + added[a][:, :LANES] for a in range(NV)]
    above = [up[40 + a : 41 + a] + reply[a][:1, LANES : 2 * LANES] for a in range(NV)]
    below = [down[45 + a : 46 + a] + reply[a][15:, 2 * LANES :] for a in range(NV)]
    near = (
        listed_rows(flipped(jnp.concatenate(below, axis=0), idx[DOWN + 2], 8)),
        listed_rows(flipped(jnp.concatenate(above, axis=0), idx[UP + 2], 8)),
    )
    values = sweep(coef, scaled_source(coef, source), near, field, 8, LANES)
    left = local_residual(coef, values, source, 8, LANES)
    pair = jnp.where((iota((8, 16), 1) >> 1) == iota((8, 16), 0), 0.5, 0.0)
    mean = jnp.concatenate([dot(pair, x) for x in left], axis=0)
    cell, place = iota((LANES, LANES), 0), iota((LANES, LANES), 1)
    match_i = (cell >> 4) == (place & 7)
    column = (cell & 7) >> 1
    own_plane = (iota((8, LANES), 1) >> 4) == iota((8, LANES), 0)
    for half in range(2):
        match = match_i & (column == 2 * half + ((place >> 3) & 1))
        spread = dot(mean, jnp.where(match, 0.25, 0.0))
        for a in range(NV):
            kept = jnp.where(own_plane, spread[8 * a : 8 * a + 8], 0.0)
            at = half * NV + a
            send[at : at + 1, :] = jnp.sum(kept, axis=0, keepdims=True)
    store_ends(send, values, END_ROWS)
    store_ends(send, left, LEFT_ROWS)
    row = iota((16, LANES), 0)
    inner = (row > 0) & (row < 15)
    total_one = squares([jnp.where(inner, x, 0.0) for x in left])
    total_zero = total_zero + pltpu.roll(total_zero, 64, 1)
    total_one = total_one + pltpu.roll(total_one, 64, 1)
    send[TOTAL_ROW : TOTAL_ROW + 1, :] = jnp.where(iota((1, LANES), 1) < 64, total_zero, total_one)
    for a in range(NV):
        for k in range(16):
            line = values[a][k : k + 1]
            quarter[k // 4, a * 4 + k % 4 : a * 4 + k % 4 + 1, :] = line
            at = a * 8 + 2 * (k % 4)
            doubled[k // 4, at : at + 1, :] = line
            doubled[k // 4, at + 1 : at + 2, :] = line
    send[QUARTER_ROWS : QUARTER_ROWS + 20, :] = quarter[idx[SUB]]
    send[QUARTER_ROWS + 20 :, :] = jnp.zeros((SENT_ROWS - QUARTER_ROWS - 20, LANES), jnp.float32)


def coarse_kernel(coef, coef_mid, idx, lanes, same, other, out, norms):
    groups = ((8, 8, LANES))
    lane3 = iota(groups, 2)
    side3 = iota(groups, 1)

    def sent(r):
        return jnp.concatenate(
            [ref[pl.ds(r, CHIPS, stride=SENT_ROWS), :] for ref in (same, other)], axis=0
        )

    square = (LANES, LANES)
    row, column = iota(square, 0), iota(square, 1)

    def block_at(x):
        return 2 * (x & 31) + (((x >> 5) & 1) ^ idx[CORE])

    alike = (row >> 6) == (column >> 6)
    beyond = jnp.broadcast_to(lanes[0:1, :], square)
    beyond_of_row = beyond.T
    at_row, at_column = block_at(row).astype(jnp.float32), block_at(column).astype(jnp.float32)
    from_down = jnp.where(alike & (beyond_of_row == at_column), 1.0, 0.0)
    from_up = jnp.where(alike & (at_row == beyond), 1.0, 0.0)
    code_up = jnp.broadcast_to(lanes[1:2, :], (8, LANES))
    code_down = dot(code_up, from_down)

    def as_rows(x):
        return (jnp.broadcast_to(x[:1], square).T[:64] + 0.5).astype(jnp.int32)

    row_codes = (as_rows(code_down), as_rows(code_up))
    row_maps = (from_down.T[:64, :64], from_up.T[:64, :64])
    code_up = (code_up + 0.5).astype(jnp.int32)
    code_down = (code_down + 0.5).astype(jnp.int32)

    def flip_planes(x, code):
        side = iota((8, LANES), 0)
        out_planes = []
        for pair in x:
            turned = []
            for p in pair:
                q = pltpu.roll(p, 4, 0)
                q = jnp.where((side & 2) != 0, pltpu.roll(q, 2, 0), pltpu.roll(q, 6, 0))
                q = jnp.where((side & 1) != 0, pltpu.roll(q, 1, 0), pltpu.roll(q, 7, 0))
                turned.append(jnp.where((code & 1) == 1, q, p))
            swapped = [pltpu.roll(p, 64, 1) for p in turned[::-1]]
            out_planes.append(
                [jnp.where((code & 2) == 2, s, p) for s, p in zip(swapped, turned)]
            )
        return out_planes

    def mapped(planes, chosen, code):
        got = dot(planes, chosen)
        pairs = [
            [got[16 * a + 8 * p : 16 * a + 8 * p + 8] for p in range(2)] for a in range(NV)
        ]
        return flip_planes(pairs, code)

    source = []
    for a in range(NV):
        both = jnp.concatenate([sent(a), sent(NV + a)], axis=0)
        turned = both.T.reshape(8, 2, 8, LANES)
        source.append([turned[:, 0], turned[:, 1]])
    cell = iota((32, LANES), 1)
    place = iota((32, LANES), 0)
    match = ((cell >> 4) == (place & 7)) & (((cell & 7) >> 1) == (place >> 3))
    mean = jnp.where(match, 0.25, 0.0)

    def restricted(first_row):
        out_rows = []
        for a in range(NV):
            got = dot_nt(mean, sent(first_row + a))
            out_rows.append(jnp.concatenate([got[:16], got[16:]], axis=1))
        return jnp.concatenate(out_rows, axis=0)

    mid_below = mapped(restricted(END_ROWS + NV), from_down, code_down)
    mid_above = mapped(restricted(END_ROWS), from_up, code_up)
    for p in range(2):
        low = times(coef_mid, BELOW, [0.5 * x[p] for x in mid_below])
        high = times(coef_mid, ABOVE, [0.5 * x[p] for x in mid_above])
        for a in range(NV):
            g = source[a][p]
            source[a][p] = jnp.concatenate(
                [g[:1] + low[a][None], g[1:7], g[7:] + high[a][None]], axis=0
            )

    totals = sent(TOTAL_ROW)
    low_lane = iota(totals.shape, 1) < 64
    total_zero = jnp.where(low_lane, totals, 0.0)
    total_one = jnp.where(low_lane, 0.0, totals)
    for first_row, end_row, side, matrix in (
        (END_ROWS + NV, LEFT_ROWS, 0, BELOW),
        (END_ROWS, LEFT_ROWS + NV, 1, ABOVE),
    ):
        got = dot(row_maps[side], jnp.concatenate([sent(first_row + a) for a in range(NV)], axis=1))
        got = [got[:, a * LANES : (a + 1) * LANES] for a in range(NV)]
        got = [flipped(x, row_codes[side], 8) for x in got]
        for x in times(coef_mid, matrix, got, [sent(end_row + a) for a in range(NV)]):
            total_one = total_one + x * x

    def pairwise(terms, start):
        out_pairs = [[None, None] for _ in range(NV)]
        for p in range(2):
            got = [x[p] for x in start]
            for place_of, values in terms:
                got = times(coef, place_of, [x[p] for x in values], got)
            for a in range(NV):
                out_pairs[a][p] = got[a]
        return out_pairs

    def beside_coarse(values):
        low = [[jnp.where(side3 > 0, pltpu.roll(x, 1, 1), 0.0) for x in pair] for pair in values]
        high = [[jnp.where(side3 < 7, pltpu.roll(x, 7, 1), 0.0) for x in pair] for pair in values]
        left = [
            [jnp.where(lane3 >= 64, pltpu.roll(pair[1], 64, 2), 0.0), pair[0]] for pair in values
        ]
        right = [
            [pair[1], jnp.where(lane3 < 64, pltpu.roll(pair[0], 64, 2), 0.0)] for pair in values
        ]
        return [low, high, left, right]

    def lifted(values, ghost):
        return [
            [jnp.concatenate([g[None], x[:7]], axis=0) for g, x in zip(gp, pair)]
            for gp, pair in zip(ghost, values)
        ]

    def lowered(values, ghost):
        return [
            [jnp.concatenate([x[1:], g[None]], axis=0) for g, x in zip(gp, pair)]
            for gp, pair in zip(ghost, values)
        ]

    def carried(values, ghost, forward):
        place_of = FORWARD if forward else BACKWARD
        out_pairs = [[None, None] for _ in range(NV)]
        for p in range(2):
            before = None if ghost is None else [x[p] for x in ghost]
            planes = [None] * 8
            for k in range(8) if forward else range(7, -1, -1):
                own = [x[p][k] for x in values]
                before = own if before is None else times(coef, place_of, before, own)
                planes[k] = before
            for a in range(NV):
                out_pairs[a][p] = jnp.stack([planes[k][a] for k in range(8)], axis=0)
        return out_pairs

    def edge(values, k):
        return jnp.concatenate([x[p][k] for x in values for p in range(2)], axis=0)

    def neighbours(values):
        below = mapped(edge(values, 7), from_down, code_down)
        above = mapped(edge(values, 0), from_up, code_up)
        return below, above

    nothing = [[jnp.zeros((8, LANES), jnp.float32)] * 2 for _ in range(NV)]
    empty = [[jnp.zeros(groups, jnp.float32)] * 2 for _ in range(NV)]
    scaled = pairwise([(CINV, source)], empty)
    values = None
    for _ in range(4):
        start = scaled
        below = above = None
        if values is not None:
            below, above = neighbours(values)
            terms = [(SIDE + n, x) for n, x in enumerate(beside_coarse(values))]
            terms.append((BACKWARD, lowered(values, above)))
            start = pairwise(terms, scaled)
        first = carried(start, below, True)
        terms = [(SIDE + n, x) for n, x in enumerate(beside_coarse(first))]
        terms.append((FORWARD, lifted(first, nothing if below is None else below)))
        values = carried(pairwise(terms, scaled), above, False)

    below, above = neighbours(values)
    image = pairwise([(CENTER, values)], empty)
    terms = [(LATERAL + n, x) for n, x in enumerate(beside_coarse(values))]
    terms += [(BELOW, lifted(values, below)), (ABOVE, lowered(values, above))]
    start = [[g - x for g, x in zip(gp, pair)] for gp, pair in zip(source, image)]
    total_two = None
    for pair in pairwise(terms, start):
        for x in pair:
            part = jnp.sum(x * x, axis=0)
            total_two = part if total_two is None else total_two + part

    lane = iota((8, LANES), 1)
    result = jnp.zeros((8, LANES), jnp.float32)
    sizes = (NV * 64 * 32 * 512, NV * 64 * 16 * 128, NV * 64 * 8 * 32)
    for level, total in enumerate((total_zero, total_one, total_two)):
        total = jnp.sum(jnp.sum(total, axis=0, keepdims=True), axis=1, keepdims=True)
        root = jnp.sqrt(jnp.broadcast_to(total, (8, LANES)) / float(sizes[level]))
        result = jnp.where(lane == level, root, result)
    norms[...] = result

    which = iota((8, LANES), 0)
    wanted = jnp.where(
        which < 2,
        jnp.full((8, LANES), idx[POS_OWN], jnp.int32),
        jnp.where(
            which < 4,
            jnp.full((8, LANES), idx[POS_ONE], jnp.int32),
            jnp.full((8, LANES), idx[POS_TWO], jnp.int32),
        ),
    )
    chosen = jnp.where(lane == wanted + 64 * (which & 1), 1.0, 0.0)
    for a in range(NV):
        laid = jnp.stack(values[a], axis=1).reshape(LANES, LANES)
        out[a] = dot_nt(chosen, laid)


def last_kernel(idx, field, doubled, same, other, coarse, corrected, one, two):
    s = idx[SUB]
    row = iota((2 * LANES, LANES), 0)
    cell = iota((2 * LANES, LANES), 1)
    half, inner_j, inner_i = row >> 7, (row >> 3) & 1, row & 7
    fits = (inner_i == (cell >> 4)) & (2 * half + inner_j == ((cell & 7) >> 1))
    to_mid = jnp.where(fits, 1.0, 0.0)
    fits = (inner_i == (cell >> 2)) & (2 * half + inner_j == (cell & 3)) & (cell < 32)
    to_cells = jnp.where(fits, 1.0, 0.0)

    def laid(which, count, shift):
        parts = []
        shape = (count, 2 * LANES)
        plane = (iota(shape, 1) >> 4) & 7
        wanted = 2 * s + (iota(shape, 0) >> shift)
        for a in range(NV):
            pair = jnp.concatenate(
                [coarse[a, 2 * which : 2 * which + 1, :], coarse[a, 2 * which + 1 : 2 * which + 2, :]], axis=1
            )
            parts.append(jnp.where(plane == wanted, jnp.broadcast_to(pair, shape), 0.0))
        return parts

    x_one = doubled[s] + dot(jnp.concatenate(laid(0, 8, 2), axis=0), to_mid)
    mid, fine = iota((LANES, 512), 0), iota((LANES, 512), 1)
    fits = ((fine >> 5) == (mid >> 3)) & (((fine & 15) >> 1) == (mid & 7))
    spread = dot(x_one, jnp.where(fits, 1.0, 0.0))
    for a in range(NV):
        corrected[a] = field[s, a] + spread[8 * a : 8 * a + 8]
    held = sent_by(idx, same, other, CHIP_ONE)[QUARTER_ROWS : QUARTER_ROWS + 20]
    for a, part in enumerate(laid(1, 8, 1)):
        got = dot(part, to_mid)
        one[a] = held[4 * a : 4 * a + 4] + got[:4]
    for a, part in enumerate(laid(2, 8, 0)):
        two[a] = dot(part, to_cells)[:2, :32]


def product(a, b):
    return jnp.einsum("...ab,...bc->...ac", a, b, precision=PRECISE)


def coefficients(couple):
    center = couple[:, 0]
    identity = jnp.broadcast_to(jnp.eye(NV, dtype=jnp.float32), center.shape)
    inverse = identity
    for _ in range(6):
        inverse = product(inverse, 2.0 * identity - product(center, inverse))
    scaled = product(inverse[:, None], couple[:, 1:])
    powers = [scaled[:, 4:]]
    for _ in range(4):
        powers.append(product(powers[-1], powers[-1]))
    powers = jnp.stack(powers, axis=2).reshape(3, 10, NV, NV)
    listed = jnp.concatenate([inverse[:, None], scaled[:, :4], powers, couple], axis=1)
    return listed.reshape(3, MATRICES * 25)


def gathered(payload):
    copies = jnp.broadcast_to(payload, (CHIPS, *payload.shape))
    same = lax.all_to_all(copies, CHIP, split_axis=0, concat_axis=0, tiled=True)
    other = lax.ppermute(same, "blk_2", [(0, 1), (1, 0)])
    return same, other


def around(piece):
    moves = [[((i + d) % 4, i) for i in range(4)] for d in range(1, 4)]
    return [piece] + [lax.ppermute(piece, "sub", move) for move in moves]


def shards(solution, right_side, couple, partner, orient, owner_one, owner_two):
    core = lax.axis_index("blk_2")
    sub = lax.axis_index("sub")

    end = jnp.where(sub == 0, solution[:, 0, 0], solution[:, 0, -1])
    ends = gathered(end.reshape(NV, 4, LANES).transpose(1, 0, 2).reshape(20, LANES))
    pieces = around(jnp.concatenate([solution[:, 0], right_side[:, 0]], axis=0))

    idx = pl.pallas_call(
        index_kernel,
        out_shape=jax.ShapeDtypeStruct((PLACES,), jnp.int32),
        in_specs=[SMEM] * 4,
        out_specs=SMEM,
    )(partner, orient, owner_one, owner_two)
    coef = coefficients(couple)
    lanes = jnp.stack([partner, orient]).reshape(2, CHIPS, 2).transpose(0, 2, 1)
    lanes = jnp.where(core == 0, lanes, lanes[:, ::-1]).reshape(2, 64).astype(jnp.float32)
    lanes = jnp.concatenate([lanes, lanes], axis=1)

    whole_shape, ends_shape = (4, NV, 8, 512), (40, LANES)
    mid_shape = (NV, 16, LANES)
    (picked,) = call(pick_kernel, [(20, LANES)], [SMEM] + [VMEM] * 2)(idx, *ends)
    field, source, ends = call(
        first_fine_kernel,
        [whole_shape, whole_shape, ends_shape],
        [SMEM] * 2 + [VMEM] * 8,
        [pltpu.VMEM(whole_shape, jnp.float32)],
    )(coef[0], idx, *pieces, *around(picked))
    field, edges, total, mid, right, sent = call(
        second_fine_kernel,
        [whole_shape, (16, 512), (8, LANES), mid_shape, mid_shape, (50, LANES)],
        [SMEM] * 3 + [VMEM] * 4,
    )(coef[0], coef[1], idx, field, source, *gathered(ends))
    doubled, sent = call(
        mid_kernel,
        [(4, 40, LANES), (SENT_ROWS, LANES)],
        [SMEM] * 3 + [VMEM] * 7,
        [pltpu.VMEM((4, 20, LANES), jnp.float32)],
    )(coef[0], coef[1], idx, *gathered(sent), sent, edges, total, mid, right)
    got = gathered(sent)
    coarse, norms = call(
        coarse_kernel, [(NV, 8, LANES), (8, LANES)], [SMEM] * 3 + [VMEM] * 3
    )(coef[2], coef[1], idx, lanes, *[x.reshape(CHIPS * SENT_ROWS, LANES) for x in got])
    corrected, one, two = call(
        last_kernel, [(NV, 8, 512), (NV, 4, LANES), (NV, 2, 32)], [SMEM] + [VMEM] * 5
    )(idx, field, doubled, *got, coarse)
    return (corrected[:, None], one[:, None], two[:, None], norms[0, :3])


def solution(mesh):
    torus = Mesh(
        mesh.devices.reshape(4, 8, 2, mesh.shape["sub"]), ("blk_0", "blk_1", "blk_2", "sub")
    )
    split = P(None, BLK, "sub", None)
    return jax.shard_map(
        shards,
        mesh=torus,
        in_specs=(split, split, P(), P(), P(), P(), P()),
        out_specs=(split, split, split, P()),
        check_vma=False,
    )
```

```python
import functools

import jax
import jax.numpy as jnp
from jax import lax
from jax.experimental import pallas as pl
from jax.experimental.pallas import tpu as pltpu
from jax.sharding import Mesh
from jax.sharding import PartitionSpec as P

NV = 5
LANES = 128
CHIPS = 32
BLK = ("blk_0", "blk_1", "blk_2")
CHIP = ("blk_0", "blk_1")
PRECISE = lax.Precision.HIGHEST

CINV, SIDE, FORWARD, BACKWARD, CENTER, LATERAL, BELOW, ABOVE = 0, 1, 5, 9, 13, 14, 18, 19
MATRICES = 20

SUB, CORE, POS_OWN, POS_ONE, POS_TWO, CHIP_ONE, REL_ONE = range(7)
DOWN, UP, DOWN_TWO, UP_TWO = 8, 11, 14, 17
PLACES = 20

END_ROWS, LEFT_ROWS, TOTAL_ROW, QUARTER_ROWS, SENT_ROWS = 10, 20, 30, 31, 56

VMEM = pl.BlockSpec(memory_space=pltpu.VMEM)
SMEM = pl.BlockSpec(memory_space=pltpu.SMEM)


def call(kernel, out_shapes, in_specs, scratch=()):
    return pl.pallas_call(
        kernel,
        out_shape=tuple(jax.ShapeDtypeStruct(shape, jnp.float32) for shape in out_shapes),
        in_specs=in_specs,
        out_specs=tuple(VMEM for _ in out_shapes),
        scratch_shapes=list(scratch),
        compiler_params=pltpu.CompilerParams(vmem_limit_bytes=40 * 1024 * 1024),
    )


def iota(shape, dim):
    return lax.broadcasted_iota(jnp.int32, shape, dim)


def dot(a, b):
    return lax.dot_general(
        a, b, (((1,), (0,)), ((), ())), precision=PRECISE, preferred_element_type=jnp.float32
    )


def dot_nt(a, b):
    return lax.dot_general(
        a, b, (((1,), (1,)), ((), ())), precision=PRECISE, preferred_element_type=jnp.float32
    )


def times(coef, place, values, start=None):
    out = list(start) if start is not None else [None] * NV
    for a in range(NV):
        for b in range(NV):
            term = coef[place * 25 + a * NV + b] * values[b]
            out[a] = term if out[a] is None else out[a] + term
    return out


def summed(coef, terms, start):
    width = start[0].shape[1]
    parts = []
    for at in range(0, width, LANES):
        out = [x[:, at : at + LANES] for x in start]
        for place, values in terms:
            out = times(coef, place, [x[:, at : at + LANES] for x in values], out)
        parts.append(out)
    if len(parts) == 1:
        return parts[0]
    return [jnp.concatenate([part[a] for part in parts], axis=1) for a in range(NV)]


def beside(values, columns, cells):
    shape = values[0].shape
    width = shape[1]
    cell = iota(shape, 1) & (cells - 1)
    column = cell & (columns - 1)
    cases = (
        (columns, cell >= columns),
        (width - columns, cell < cells - columns),
        (1, column != 0),
        (width - 1, column != columns - 1),
    )
    return [
        [jnp.where(mask, pltpu.roll(x, shift, 1), 0.0) for x in values] for shift, mask in cases
    ]


def moved_up(x, by):
    return jnp.where(iota(x.shape, 0) >= by, pltpu.roll(x, by, 0), 0.0)


def moved_down(x, by):
    count = x.shape[0]
    return jnp.where(iota(x.shape, 0) < count - by, pltpu.roll(x, count - by, 0), 0.0)


def tiles_of(values):
    return [[x[at : at + 8] for x in values] for at in range(0, values[0].shape[0], 8)]


def joined(tiles):
    return [jnp.concatenate([tile[a] for tile in tiles], axis=0) for a in range(NV)]


def recurrence(coef, values, forward):
    place = FORWARD if forward else BACKWARD
    move = moved_up if forward else moved_down
    for n in range(3):
        values = summed(coef, [(place + n, [move(x, 1 << n) for x in values])], values)
    tiles = tiles_of(values)
    count = len(tiles)
    for n in range(1, count):
        at, before = (n, n - 1) if forward else (count - 1 - n, count - n)
        tiles[at] = summed(coef, [(place + 3, tiles[before])], tiles[at])
    return joined(tiles)


def response(coef, low, high, count, columns, kept):
    width = low[0].shape[1]
    row = iota((8, width), 0)
    tile = [jnp.where(row == 0, jnp.broadcast_to(x, (8, width)), 0.0) for x in low]
    for n in range(3):
        tile = summed(coef, [(FORWARD + n, [moved_up(x, 1 << n) for x in tile])], tile)
    tiles = [tile]
    for _ in range(1, count // 8):
        tiles.append(summed(coef, [(FORWARD + 3, tiles[-1])], zeros_like(tile)))
    tiles[-1] = [
        x + jnp.where(row == 7, jnp.broadcast_to(h, (8, width)), 0.0)
        for x, h in zip(tiles[-1], high)
    ]
    if kept == "last":
        end = tiles[-1]
        terms = [(SIDE + n, x) for n, x in enumerate(beside(end, columns, width))]
        terms.append((FORWARD, [moved_up(x, 1) for x in end]))
        end = summed(coef, terms, zeros_like(end))
        return [x[7:] + h for x, h in zip(end, high)]
    first = joined(tiles)
    terms = [(SIDE + n, x) for n, x in enumerate(beside(first, columns, width))]
    terms.append((FORWARD, [moved_up(x, 1) for x in first]))
    source = summed(coef, terms, at_ends(low, high, count))
    if kept == "all":
        return recurrence(coef, source, False)
    tiles = tiles_of(source)
    end = tiles[-1]
    for tile in tiles[-2::-1]:
        end = summed(coef, [(BACKWARD + 3, end)], tile)
    for n in range(3):
        end = summed(coef, [(BACKWARD + n, [moved_down(x, 1 << n) for x in end])], end)
    return [x[:1] for x in end]


def at_ends(low, high, count):
    out = []
    for a, b in zip(low, high):
        shape = (count, a.shape[1])
        row = iota(shape, 0)
        out.append(
            jnp.where(
                row == 0,
                jnp.broadcast_to(a, shape),
                jnp.where(row == count - 1, jnp.broadcast_to(b, shape), 0.0),
            )
        )
    return out


def sweep(coef, scaled, ends, values, columns, cells):
    base = scaled
    if ends is not None:
        low = times(coef, FORWARD, ends[0])
        high = times(coef, BACKWARD, ends[1])
        base = [x + e for x, e in zip(base, at_ends(low, high, base[0].shape[0]))]
    source = base
    if values is not None:
        terms = [(SIDE + n, x) for n, x in enumerate(beside(values, columns, cells))]
        terms.append((BACKWARD, [moved_down(x, 1) for x in values]))
        source = summed(coef, terms, base)
    first = recurrence(coef, source, True)
    terms = [(SIDE + n, x) for n, x in enumerate(beside(first, columns, cells))]
    terms.append((FORWARD, [moved_up(x, 1) for x in first]))
    return recurrence(coef, summed(coef, terms, base), False)


def zeros_like(values):
    return [jnp.zeros_like(x) for x in values]


def scaled_source(coef, source):
    return summed(coef, [(CINV, source)], zeros_like(source))


def local_residual(coef, values, source, columns, cells):
    terms = [(LATERAL + n, x) for n, x in enumerate(beside(values, columns, cells))]
    terms.append((BELOW, [moved_up(x, 1) for x in values]))
    terms.append((ABOVE, [moved_down(x, 1) for x in values]))
    image = summed(coef, [(CENTER, values)], zeros_like(values))
    return summed(coef, terms, [g - x for g, x in zip(source, image)])


def lanes_crossed(x, bits):
    width, dim = x.shape[-1], x.ndim - 1
    lane = iota(x.shape, dim)
    for bit in bits:
        step = 1 << bit
        x = jnp.where(
            (lane & step) != 0, pltpu.roll(x, step, dim), pltpu.roll(x, width - step, dim)
        )
    return x


def flipped(x, code, columns):
    code = jnp.broadcast_to(code, x.shape) if getattr(code, "ndim", 0) else jnp.full(x.shape, code, jnp.int32)
    width = x.shape[-1]
    along_j = columns.bit_length() - 1
    x = jnp.where((code & 1) == 1, lanes_crossed(x, range(along_j, width.bit_length() - 1)), x)
    return jnp.where((code & 2) == 2, lanes_crossed(x, range(along_j)), x)


def block_of(same, other, chip, rel):
    a, b = same[chip], other[chip]
    return jnp.where(jnp.full(a.shape, rel, jnp.int32) == 0, a, b)


def sent_by(idx, same, other, place):
    return block_of(same, other, idx[place], idx[place + 1])


def listed_rows(x):
    return [x[a : a + 1] for a in range(NV)]


def plane_of(ref, row):
    return jnp.concatenate([ref[c, row : row + NV, :] for c in range(4)], axis=1)


def ordered(idx, pieces, ref):
    for d, piece in enumerate(pieces):
        ref[(idx[SUB] + d) & 3] = piece[...]


def near_planes(idx, found, own):
    down, up, down_two, up_two = (idx[place + 2] for place in (DOWN, UP, DOWN_TWO, UP_TWO))
    first, last = plane_of(own, 0), plane_of(own, NV)
    return (
        ((plane_of(found, 5), down), (plane_of(found, 0), up)),
        ((last, up), (plane_of(found, 10), up_two)),
        ((plane_of(found, 15), down_two), (first, down)),
    )


def store_end_chunks(out, values, at):
    count = values[0].shape[0]
    for c in range(4):
        for a in range(NV):
            line = values[a][:, c * LANES : (c + 1) * LANES]
            out[c, at + a : at + a + 1, :] = line[:1]
            out[c, at + NV + a : at + NV + a + 1, :] = line[count - 1 :]


def store_ends(out, values, at):
    count = values[0].shape[0]
    for a in range(NV):
        out[at + a : at + a + 1, :] = values[a][:1]
        out[at + NV + a : at + NV + a + 1, :] = values[a][count - 1 :]


def whole(ref):
    return [jnp.concatenate([ref[q, a] for q in range(4)], axis=0) for a in range(NV)]


def store_whole(ref, values):
    for a in range(NV):
        for q in range(4):
            ref[q, a] = values[a][8 * q : 8 * q + 8]


def squares(values):
    total = None
    for x in values:
        for at in range(0, x.shape[1], LANES):
            part = x[:, at : at + LANES] * x[:, at : at + LANES]
            total = part if total is None else total + part
    return jnp.sum(total, axis=0, keepdims=True)


def index_kernel(partner, orient, owner_one, owner_two, idx):
    device = lax.axis_index(BLK)
    core = lax.axis_index("blk_2")
    idx[SUB] = lax.axis_index("sub")
    idx[CORE] = core

    def find(j, found):
        down, one, two = found
        return (
            jnp.where(partner[j] == device, j, down),
            jnp.where(owner_one[j] == device, j, one),
            jnp.where(owner_two[j] == device, j, two),
        )

    zero = jnp.int32(0)
    down, one, two = lax.fori_loop(0, 64, find, (zero, zero, zero), unroll=8)
    down_two = lax.fori_loop(
        0, 64, lambda j, found: jnp.where(partner[j] == down, j, found), zero, unroll=8
    )
    up = partner[device]
    up_two = partner[up]
    for place, block in ((POS_OWN, device), (POS_ONE, one), (POS_TWO, two)):
        idx[place] = ((block & 1) ^ core) * CHIPS + (block >> 1)
    idx[CHIP_ONE] = one >> 1
    idx[REL_ONE] = (one & 1) ^ core
    places = ((DOWN, down, down), (UP, up, device), (DOWN_TWO, down_two, down_two), (UP_TWO, up_two, up))
    for place, block, crossing in places:
        idx[place] = block >> 1
        idx[place + 1] = (block & 1) ^ core
        idx[place + 2] = orient[crossing]
    idx[7] = zero


def pick_kernel(last_extra, idx, same, other, out):
    up, down = sent_by(idx, same, other, UP), sent_by(idx, same, other, DOWN)
    out[0:5, :] = up[0:5]
    out[5:10, :] = down[5:10]
    out[10:15, :] = sent_by(idx, same, other, UP_TWO)[0:5]
    out[15:20, :] = sent_by(idx, same, other, DOWN_TWO)[5:10]
    out[20:25, :] = up[10:15]
    out[25:30, :] = down[last_extra : last_extra + 5]
    out[30:32, :] = jnp.zeros((2, LANES), jnp.float32)


def local_kernel(coef, idx, p0, p1, p2, p3, source, local, own, send, field):
    for d, piece in enumerate((p0, p1, p2, p3)):
        q = (idx[SUB] + d) & 3
        for a in range(NV):
            field[q, a] = piece[a]
            source[q, a] = piece[NV + a]
    given = whole(field)
    own[...] = jnp.zeros(own.shape, jnp.float32)
    store_end_chunks(own, given, 0)
    values = sweep(coef, scaled_source(coef, whole(source)), None, given, 16, 512)
    store_whole(local, values)
    store_end_chunks(own, values, 10)
    send[...] = own[idx[SUB]]


def plane_mean():
    cell, coarse = iota((512, LANES), 0), iota((512, LANES), 1)
    match = ((cell >> 5) == (coarse >> 3)) & (((cell & 15) >> 1) == (coarse & 7))
    return jnp.where(match, 0.25, 0.0)


def fine_kernel(
    coef, coef_mid, idx, e0, e1, e2, e3, own, source, local, out, edges, total, mid, right, own_ends, send, found
):
    ordered(idx, (e0, e1, e2, e3), found)
    replies = []
    for kept, pair in zip(("all", "first", "last"), near_planes(idx, found, own)):
        below, above = (listed_rows(flipped(plane, code, 16)) for plane, code in pair)
        low, high = times(coef, FORWARD, below), times(coef, BACKWARD, above)
        replies.append(response(coef, low, high, 32, 16, kept))
    field = [x + y for x, y in zip(whole(local), replies[0])]
    above = plane_of(found, 20) + jnp.concatenate(replies[1], axis=0)
    below = plane_of(found, 25) + jnp.concatenate(replies[2], axis=0)
    near = (
        listed_rows(flipped(below, idx[DOWN + 2], 16)),
        listed_rows(flipped(above, idx[UP + 2], 16)),
    )
    given = whole(source)
    values = sweep(coef, scaled_source(coef, given), near, field, 16, 512)
    store_whole(out, values)
    left = local_residual(coef, values, given, 16, 512)
    edges[...] = jnp.zeros((16, 512), jnp.float32)
    for a in range(NV):
        edges[a : a + 1, :] = left[a][:1]
        edges[8 + a : 9 + a, :] = left[a][31:]
    row = iota((32, 512), 0)
    inner = (row > 0) & (row < 31)
    total[...] = jnp.broadcast_to(squares([jnp.where(inner, x, 0.0) for x in left]), (8, LANES))
    pair = jnp.where((iota((16, 32), 1) >> 1) == iota((16, 32), 0), 0.5, 0.0)
    mean = dot(jnp.concatenate(left, axis=0), plane_mean())
    source_mid = [dot(pair, mean[32 * a : 32 * a + 32]) for a in range(NV)]
    reply = sweep(coef_mid, scaled_source(coef_mid, source_mid), None, None, 8, LANES)
    own_ends[...] = jnp.zeros(own_ends.shape, jnp.float32)
    store_end_chunks(own_ends, values, 0)
    for a in range(NV):
        mid[a] = reply[a]
        right[a] = source_mid[a]
        for c in range(4):
            line = reply[a][15:] if c & 1 else reply[a][:1]
            own_ends[c, 10 + a : 11 + a, :] = line
    send[...] = own_ends[idx[SUB]]


def mid_kernel(
    coef_fine, coef, idx, e0, e1, e2, e3, own, edges, total, mid, right, doubled, send, quarter, found
):
    ordered(idx, (e0, e1, e2, e3), found)
    pairs = near_planes(idx, found, own)
    below, above = (flipped(plane, code, 16) for plane, code in pairs[0])

    low = times(coef_fine, BELOW, listed_rows(below), [edges[a : a + 1, :] for a in range(NV)])
    high = times(coef_fine, ABOVE, listed_rows(above), [edges[8 + a : 9 + a, :] for a in range(NV)])
    total_zero = total[:1] + squares(low) + squares(high)

    gap = jnp.zeros((3, 512), jnp.float32)
    stacked = jnp.concatenate([part for pair in pairs for plane, _ in pair for part in (plane, gap)], axis=0)
    mean = dot(stacked, plane_mean())
    replies = []
    for n, (kept, pair) in enumerate(zip(("all", "first", "last"), pairs)):
        planes = [
            flipped(0.5 * mean[8 * m : 8 * m + NV], code, 8)
            for m, (_, code) in zip((2 * n, 2 * n + 1), pair)
        ]
        low = times(coef_fine, BELOW, listed_rows(planes[0]))
        high = times(coef_fine, ABOVE, listed_rows(planes[1]))
        if n == 0:
            added = at_ends(low, high, 16)
        low, high = times(coef, CINV, low), times(coef, CINV, high)
        replies.append(response(coef, low, high, 16, 8, kept))
    field = [mid[a] + replies[0][a] for a in range(NV)]
    source = [right[a] + added[a] for a in range(NV)]
    above = found[0, 20:25, :] + jnp.concatenate(replies[1], axis=0)
    below = found[1, 25:30, :] + jnp.concatenate(replies[2], axis=0)
    near = (
        listed_rows(flipped(below, idx[DOWN + 2], 8)),
        listed_rows(flipped(above, idx[UP + 2], 8)),
    )
    values = sweep(coef, scaled_source(coef, source), near, field, 8, LANES)
    left = local_residual(coef, values, source, 8, LANES)
    pair = jnp.where((iota((8, 16), 1) >> 1) == iota((8, 16), 0), 0.5, 0.0)
    mean = jnp.concatenate([dot(pair, x) for x in left], axis=0)
    cell, place = iota((LANES, LANES), 0), iota((LANES, LANES), 1)
    match_i = (cell >> 4) == (place & 7)
    column = (cell & 7) >> 1
    own_plane = (iota((8, LANES), 1) >> 4) == iota((8, LANES), 0)
    for half in range(2):
        match = match_i & (column == 2 * half + ((place >> 3) & 1))
        spread = dot(mean, jnp.where(match, 0.25, 0.0))
        for a in range(NV):
            kept = jnp.where(own_plane, spread[8 * a : 8 * a + 8], 0.0)
            at = half * NV + a
            send[at : at + 1, :] = jnp.sum(kept, axis=0, keepdims=True)
    store_ends(send, values, END_ROWS)
    store_ends(send, left, LEFT_ROWS)
    row = iota((16, LANES), 0)
    inner = (row > 0) & (row < 15)
    total_one = squares([jnp.where(inner, x, 0.0) for x in left])
    total_zero = total_zero + pltpu.roll(total_zero, 64, 1)
    total_one = total_one + pltpu.roll(total_one, 64, 1)
    send[TOTAL_ROW : TOTAL_ROW + 1, :] = jnp.where(iota((1, LANES), 1) < 64, total_zero, total_one)
    for a in range(NV):
        for k in range(16):
            line = values[a][k : k + 1]
            quarter[k // 4, a * 4 + k % 4 : a * 4 + k % 4 + 1, :] = line
            at = a * 8 + 2 * (k % 4)
            doubled[k // 4, at : at + 1, :] = line
            doubled[k // 4, at + 1 : at + 2, :] = line
    send[QUARTER_ROWS : QUARTER_ROWS + 20, :] = quarter[idx[SUB]]
    send[QUARTER_ROWS + 20 :, :] = jnp.zeros((SENT_ROWS - QUARTER_ROWS - 20, LANES), jnp.float32)


def coarse_kernel(coef, coef_mid, idx, lanes, same, other, out, norms):
    groups = ((8, 8, LANES))
    lane3 = iota(groups, 2)
    side3 = iota(groups, 1)

    def sent(r):
        return jnp.concatenate(
            [ref[pl.ds(r, CHIPS, stride=SENT_ROWS), :] for ref in (same, other)], axis=0
        )

    square = (LANES, LANES)
    row, column = iota(square, 0), iota(square, 1)

    def block_at(x):
        return 2 * (x & 31) + (((x >> 5) & 1) ^ idx[CORE])

    alike = (row >> 6) == (column >> 6)
    beyond = jnp.broadcast_to(lanes[0:1, :], square)
    beyond_of_row = beyond.T
    at_row, at_column = block_at(row).astype(jnp.float32), block_at(column).astype(jnp.float32)
    from_down = jnp.where(alike & (beyond_of_row == at_column), 1.0, 0.0)
    from_up = jnp.where(alike & (at_row == beyond), 1.0, 0.0)
    code_up = jnp.broadcast_to(lanes[1:2, :], (8, LANES))
    code_down = dot(code_up, from_down)

    def as_rows(x):
        return (jnp.broadcast_to(x[:1], square).T[:64] + 0.5).astype(jnp.int32)

    row_codes = (as_rows(code_down), as_rows(code_up))
    row_maps = (from_down.T[:64, :64], from_up.T[:64, :64])
    code_up = (code_up + 0.5).astype(jnp.int32)
    code_down = (code_down + 0.5).astype(jnp.int32)

    def flip_planes(x, code):
        side = iota((8, LANES), 0)
        out_planes = []
        for pair in x:
            turned = []
            for p in pair:
                q = pltpu.roll(p, 4, 0)
                q = jnp.where((side & 2) != 0, pltpu.roll(q, 2, 0), pltpu.roll(q, 6, 0))
                q = jnp.where((side & 1) != 0, pltpu.roll(q, 1, 0), pltpu.roll(q, 7, 0))
                turned.append(jnp.where((code & 1) == 1, q, p))
            swapped = [pltpu.roll(p, 64, 1) for p in turned[::-1]]
            out_planes.append(
                [jnp.where((code & 2) == 2, s, p) for s, p in zip(swapped, turned)]
            )
        return out_planes

    def mapped(planes, chosen, code):
        got = dot(planes, chosen)
        pairs = [
            [got[16 * a + 8 * p : 16 * a + 8 * p + 8] for p in range(2)] for a in range(NV)
        ]
        return flip_planes(pairs, code)

    source = []
    for a in range(NV):
        both = jnp.concatenate([sent(a), sent(NV + a)], axis=0)
        turned = both.T.reshape(8, 2, 8, LANES)
        source.append([turned[:, 0], turned[:, 1]])
    cell = iota((32, LANES), 1)
    place = iota((32, LANES), 0)
    match = ((cell >> 4) == (place & 7)) & (((cell & 7) >> 1) == (place >> 3))
    mean = jnp.where(match, 0.25, 0.0)

    def restricted(first_row):
        out_rows = []
        for a in range(NV):
            got = dot_nt(mean, sent(first_row + a))
            out_rows.append(jnp.concatenate([got[:16], got[16:]], axis=1))
        return jnp.concatenate(out_rows, axis=0)

    mid_below = mapped(restricted(END_ROWS + NV), from_down, code_down)
    mid_above = mapped(restricted(END_ROWS), from_up, code_up)
    for p in range(2):
        low = times(coef_mid, BELOW, [0.5 * x[p] for x in mid_below])
        high = times(coef_mid, ABOVE, [0.5 * x[p] for x in mid_above])
        for a in range(NV):
            g = source[a][p]
            source[a][p] = jnp.concatenate(
                [g[:1] + low[a][None], g[1:7], g[7:] + high[a][None]], axis=0
            )

    totals = sent(TOTAL_ROW)
    low_lane = iota(totals.shape, 1) < 64
    total_zero = jnp.where(low_lane, totals, 0.0)
    total_one = jnp.where(low_lane, 0.0, totals)
    for first_row, end_row, side, matrix in (
        (END_ROWS + NV, LEFT_ROWS, 0, BELOW),
        (END_ROWS, LEFT_ROWS + NV, 1, ABOVE),
    ):
        got = dot(row_maps[side], jnp.concatenate([sent(first_row + a) for a in range(NV)], axis=1))
        got = [got[:, a * LANES : (a + 1) * LANES] for a in range(NV)]
        got = [flipped(x, row_codes[side], 8) for x in got]
        for x in times(coef_mid, matrix, got, [sent(end_row + a) for a in range(NV)]):
            total_one = total_one + x * x

    def pairwise(terms, start):
        out_pairs = [[None, None] for _ in range(NV)]
        for p in range(2):
            got = [x[p] for x in start]
            for place_of, values in terms:
                got = times(coef, place_of, [x[p] for x in values], got)
            for a in range(NV):
                out_pairs[a][p] = got[a]
        return out_pairs

    def beside_coarse(values):
        low = [[jnp.where(side3 > 0, pltpu.roll(x, 1, 1), 0.0) for x in pair] for pair in values]
        high = [[jnp.where(side3 < 7, pltpu.roll(x, 7, 1), 0.0) for x in pair] for pair in values]
        left = [
            [jnp.where(lane3 >= 64, pltpu.roll(pair[1], 64, 2), 0.0), pair[0]] for pair in values
        ]
        right = [
            [pair[1], jnp.where(lane3 < 64, pltpu.roll(pair[0], 64, 2), 0.0)] for pair in values
        ]
        return [low, high, left, right]

    def lifted(values, ghost):
        return [
            [jnp.concatenate([g[None], x[:7]], axis=0) for g, x in zip(gp, pair)]
            for gp, pair in zip(ghost, values)
        ]

    def lowered(values, ghost):
        return [
            [jnp.concatenate([x[1:], g[None]], axis=0) for g, x in zip(gp, pair)]
            for gp, pair in zip(ghost, values)
        ]

    def carried(values, ghost, forward):
        place_of = FORWARD if forward else BACKWARD
        out_pairs = [[None, None] for _ in range(NV)]
        for p in range(2):
            before = None if ghost is None else [x[p] for x in ghost]
            planes = [None] * 8
            for k in range(8) if forward else range(7, -1, -1):
                own = [x[p][k] for x in values]
                before = own if before is None else times(coef, place_of, before, own)
                planes[k] = before
            for a in range(NV):
                out_pairs[a][p] = jnp.stack([planes[k][a] for k in range(8)], axis=0)
        return out_pairs

    def edge(values, k):
        return jnp.concatenate([x[p][k] for x in values for p in range(2)], axis=0)

    def neighbours(values):
        below = mapped(edge(values, 7), from_down, code_down)
        above = mapped(edge(values, 0), from_up, code_up)
        return below, above

    nothing = [[jnp.zeros((8, LANES), jnp.float32)] * 2 for _ in range(NV)]
    empty = [[jnp.zeros(groups, jnp.float32)] * 2 for _ in range(NV)]
    scaled = pairwise([(CINV, source)], empty)
    values = None
    for _ in range(4):
        start = scaled
        below = above = None
        if values is not None:
            below, above = neighbours(values)
            terms = [(SIDE + n, x) for n, x in enumerate(beside_coarse(values))]
            terms.append((BACKWARD, lowered(values, above)))
            start = pairwise(terms, scaled)
        first = carried(start, below, True)
        terms = [(SIDE + n, x) for n, x in enumerate(beside_coarse(first))]
        terms.append((FORWARD, lifted(first, nothing if below is None else below)))
        values = carried(pairwise(terms, scaled), above, False)

    below, above = neighbours(values)
    image = pairwise([(CENTER, values)], empty)
    terms = [(LATERAL + n, x) for n, x in enumerate(beside_coarse(values))]
    terms += [(BELOW, lifted(values, below)), (ABOVE, lowered(values, above))]
    start = [[g - x for g, x in zip(gp, pair)] for gp, pair in zip(source, image)]
    total_two = None
    for pair in pairwise(terms, start):
        for x in pair:
            part = jnp.sum(x * x, axis=0)
            total_two = part if total_two is None else total_two + part

    lane = iota((8, LANES), 1)
    result = jnp.zeros((8, LANES), jnp.float32)
    sizes = (NV * 64 * 32 * 512, NV * 64 * 16 * 128, NV * 64 * 8 * 32)
    for level, total in enumerate((total_zero, total_one, total_two)):
        total = jnp.sum(jnp.sum(total, axis=0, keepdims=True), axis=1, keepdims=True)
        root = jnp.sqrt(jnp.broadcast_to(total, (8, LANES)) / float(sizes[level]))
        result = jnp.where(lane == level, root, result)
    norms[...] = result

    which = iota((8, LANES), 0)
    wanted = jnp.where(
        which < 2,
        jnp.full((8, LANES), idx[POS_OWN], jnp.int32),
        jnp.where(
            which < 4,
            jnp.full((8, LANES), idx[POS_ONE], jnp.int32),
            jnp.full((8, LANES), idx[POS_TWO], jnp.int32),
        ),
    )
    chosen = jnp.where(lane == wanted + 64 * (which & 1), 1.0, 0.0)
    for a in range(NV):
        laid = jnp.stack(values[a], axis=1).reshape(LANES, LANES)
        out[a] = dot_nt(chosen, laid)


def last_kernel(idx, field, doubled, same, other, coarse, corrected, one, two):
    s = idx[SUB]
    row = iota((2 * LANES, LANES), 0)
    cell = iota((2 * LANES, LANES), 1)
    half, inner_j, inner_i = row >> 7, (row >> 3) & 1, row & 7
    fits = (inner_i == (cell >> 4)) & (2 * half + inner_j == ((cell & 7) >> 1))
    to_mid = jnp.where(fits, 1.0, 0.0)
    fits = (inner_i == (cell >> 2)) & (2 * half + inner_j == (cell & 3)) & (cell < 32)
    to_cells = jnp.where(fits, 1.0, 0.0)

    def laid(which, count, shift):
        parts = []
        shape = (count, 2 * LANES)
        plane = (iota(shape, 1) >> 4) & 7
        wanted = 2 * s + (iota(shape, 0) >> shift)
        for a in range(NV):
            pair = jnp.concatenate(
                [coarse[a, 2 * which : 2 * which + 1, :], coarse[a, 2 * which + 1 : 2 * which + 2, :]], axis=1
            )
            parts.append(jnp.where(plane == wanted, jnp.broadcast_to(pair, shape), 0.0))
        return parts

    x_one = doubled[s] + dot(jnp.concatenate(laid(0, 8, 2), axis=0), to_mid)
    mid, fine = iota((LANES, 512), 0), iota((LANES, 512), 1)
    fits = ((fine >> 5) == (mid >> 3)) & (((fine & 15) >> 1) == (mid & 7))
    spread = dot(x_one, jnp.where(fits, 1.0, 0.0))
    for a in range(NV):
        corrected[a] = field[s, a] + spread[8 * a : 8 * a + 8]
    held = sent_by(idx, same, other, CHIP_ONE)[QUARTER_ROWS : QUARTER_ROWS + 20]
    for a, part in enumerate(laid(1, 8, 1)):
        got = dot(part, to_mid)
        one[a] = held[4 * a : 4 * a + 4] + got[:4]
    for a, part in enumerate(laid(2, 8, 0)):
        two[a] = dot(part, to_cells)[:2, :32]


def product(a, b):
    return jnp.einsum("...ab,...bc->...ac", a, b, precision=PRECISE)


def coefficients(couple):
    center = couple[:, 0]
    identity = jnp.broadcast_to(jnp.eye(NV, dtype=jnp.float32), center.shape)
    inverse = identity
    for _ in range(6):
        inverse = product(inverse, 2.0 * identity - product(center, inverse))
    scaled = product(inverse[:, None], couple[:, 1:])
    powers = [scaled[:, 4:]]
    for _ in range(3):
        powers.append(product(powers[-1], powers[-1]))
    powers = jnp.stack(powers, axis=2).reshape(3, 8, NV, NV)
    listed = jnp.concatenate([inverse[:, None], scaled[:, :4], powers, couple], axis=1)
    return listed.reshape(3, MATRICES * 25)


def gathered(payload):
    copies = jnp.broadcast_to(payload, (CHIPS, *payload.shape))
    same = lax.all_to_all(copies, CHIP, split_axis=0, concat_axis=0, tiled=True)
    other = lax.ppermute(same, "blk_2", [(0, 1), (1, 0)])
    return same, other


def around(piece):
    moves = [[((i + d) % 4, i) for i in range(4)] for d in range(1, 4)]
    return [piece] + [lax.ppermute(piece, "sub", move) for move in moves]


def shards(solution, right_side, couple, partner, orient, owner_one, owner_two):
    core = lax.axis_index("blk_2")

    pieces = around(jnp.concatenate([solution[:, 0], right_side[:, 0]], axis=0))

    idx = pl.pallas_call(
        index_kernel,
        out_shape=jax.ShapeDtypeStruct((PLACES,), jnp.int32),
        in_specs=[SMEM] * 4,
        out_specs=SMEM,
        cost_estimate=pl.CostEstimate(flops=0, bytes_accessed=4_000_000, transcendentals=0),
    )(partner, orient, owner_one, owner_two)
    coef = coefficients(couple)
    lanes = jnp.stack([partner, orient]).reshape(2, CHIPS, 2).transpose(0, 2, 1)
    lanes = jnp.where(core == 0, lanes, lanes[:, ::-1]).reshape(2, 64).astype(jnp.float32)
    lanes = jnp.concatenate([lanes, lanes], axis=1)

    whole_shape = (4, NV, 8, 512)
    mid_shape = (NV, 16, LANES)
    found = pltpu.VMEM((4, 32, LANES), jnp.float32)

    def picked(sent, last_extra):
        kernel = functools.partial(pick_kernel, last_extra)
        (rows,) = call(kernel, [(32, LANES)], [SMEM] + [VMEM] * 2)(idx, *gathered(sent))
        return around(rows)

    source, local, own, sent = call(
        local_kernel,
        [whole_shape, whole_shape, (4, 24, LANES), (24, LANES)],
        [SMEM] * 2 + [VMEM] * 4,
        [pltpu.VMEM(whole_shape, jnp.float32)],
    )(coef[0], idx, *pieces)
    field, edges, total, mid, right, own, sent = call(
        fine_kernel,
        [whole_shape, (16, 512), (8, LANES), mid_shape, mid_shape, (4, 16, LANES), (16, LANES)],
        [SMEM] * 3 + [VMEM] * 7,
        [found],
    )(coef[0], coef[1], idx, *picked(sent, 15), own, source, local)
    doubled, sent = call(
        mid_kernel,
        [(4, 40, LANES), (SENT_ROWS, LANES)],
        [SMEM] * 3 + [VMEM] * 9,
        [pltpu.VMEM((4, 20, LANES), jnp.float32), found],
    )(coef[0], coef[1], idx, *picked(sent, 10), own, edges, total, mid, right)
    got = gathered(sent)
    coarse, norms = call(
        coarse_kernel, [(NV, 8, LANES), (8, LANES)], [SMEM] * 3 + [VMEM] * 3
    )(coef[2], coef[1], idx, lanes, *[x.reshape(CHIPS * SENT_ROWS, LANES) for x in got])
    corrected, one, two = call(
        last_kernel, [(NV, 8, 512), (NV, 4, LANES), (NV, 2, 32)], [SMEM] + [VMEM] * 5
    )(idx, field, doubled, *got, coarse)
    return (corrected[:, None], one[:, None], two[:, None], norms[0, :3])


def solution(mesh):
    torus = Mesh(
        mesh.devices.reshape(4, 8, 2, mesh.shape["sub"]), ("blk_0", "blk_1", "blk_2", "sub")
    )
    split = P(None, BLK, "sub", None)
    return jax.shard_map(
        shards,
        mesh=torus,
        in_specs=(split, split, P(), P(), P(), P(), P()),
        out_specs=(split, split, split, P()),
        check_vma=False,
    )
```

```python
import jax
import jax.numpy as jnp
from jax import lax
from jax.experimental import pallas as pl
from jax.experimental.pallas import tpu as pltpu
from jax.sharding import Mesh
from jax.sharding import PartitionSpec as P

NV = 5
LANES = 128
CHIPS = 32
BLK = ("blk_0", "blk_1", "blk_2")
CHIP = ("blk_0", "blk_1")
PRECISE = lax.Precision.HIGHEST

CINV, SIDE, FORWARD, BACKWARD, CENTER, LATERAL, BELOW, ABOVE = 0, 1, 5, 9, 13, 14, 18, 19
MATRICES = 20

SUB, CORE, POS_OWN, POS_ONE, POS_TWO, CHIP_ONE, REL_ONE = range(7)
DOWN, UP, DOWN_TWO, UP_TWO, DOWN_THREE, UP_THREE = 8, 11, 14, 17, 20, 23

TOTAL_ROW, QUARTER_ROWS, SENT_ROWS = 10, 11, 32

VMEM = pl.BlockSpec(memory_space=pltpu.VMEM)
SMEM = pl.BlockSpec(memory_space=pltpu.SMEM)


def call(kernel, out_shapes, in_specs, scratch=()):
    return pl.pallas_call(
        kernel,
        out_shape=tuple(jax.ShapeDtypeStruct(shape, jnp.float32) for shape in out_shapes),
        in_specs=in_specs,
        out_specs=tuple(VMEM for _ in out_shapes),
        scratch_shapes=list(scratch),
        compiler_params=pltpu.CompilerParams(vmem_limit_bytes=40 * 1024 * 1024),
    )


def iota(shape, dim):
    return lax.broadcasted_iota(jnp.int32, shape, dim)


def parts_of(x):
    high = x.astype(jnp.bfloat16)
    rest = x - high.astype(jnp.float32)
    middle = rest.astype(jnp.bfloat16)
    return high, middle, (rest - middle.astype(jnp.float32)).astype(jnp.bfloat16)


def contracted(a, b, dims):
    return lax.dot_general(a, b, (dims, ((), ())), preferred_element_type=jnp.float32)


def dot(values, exact):
    exact = exact.astype(jnp.bfloat16)
    high, middle, low = (contracted(x, exact, ((1,), (0,))) for x in parts_of(values))
    return high + (middle + low)


def dot_left(exact, values):
    exact = exact.astype(jnp.bfloat16)
    high, middle, low = (contracted(exact, x, ((1,), (0,))) for x in parts_of(values))
    return high + (middle + low)


def dot_nt(exact, values):
    exact = exact.astype(jnp.bfloat16)
    high, middle, low = (contracted(exact, x, ((1,), (1,))) for x in parts_of(values))
    return high + (middle + low)


def times(coef, place, values, start=None):
    out = list(start) if start is not None else [None] * NV
    for a in range(NV):
        for b in range(NV):
            term = coef[place * 25 + a * NV + b] * values[b]
            out[a] = term if out[a] is None else out[a] + term
    return out


def summed(coef, terms, start):
    width = start[0].shape[1]
    parts = []
    for at in range(0, width, LANES):
        out = [x[:, at : at + LANES] for x in start]
        for place, values in terms:
            out = times(coef, place, [x[:, at : at + LANES] for x in values], out)
        parts.append(out)
    if len(parts) == 1:
        return parts[0]
    return [jnp.concatenate([part[a] for part in parts], axis=1) for a in range(NV)]


def beside(values, columns, cells):
    shape = values[0].shape
    width = shape[1]
    cell = iota(shape, 1) & (cells - 1)
    column = cell & (columns - 1)
    cases = (
        (columns, cell >= columns),
        (width - columns, cell < cells - columns),
        (1, column != 0),
        (width - 1, column != columns - 1),
    )
    return [
        [jnp.where(mask, pltpu.roll(x, shift, 1), 0.0) for x in values] for shift, mask in cases
    ]


def moved_up(x, by):
    return jnp.where(iota(x.shape, 0) >= by, pltpu.roll(x, by, 0), 0.0)


def moved_down(x, by):
    count = x.shape[0]
    return jnp.where(iota(x.shape, 0) < count - by, pltpu.roll(x, count - by, 0), 0.0)


def tiles_of(values):
    return [[x[at : at + 8] for x in values] for at in range(0, values[0].shape[0], 8)]


def joined(tiles):
    return [jnp.concatenate([tile[a] for tile in tiles], axis=0) for a in range(NV)]


def recurrence(coef, values, forward):
    place = FORWARD if forward else BACKWARD
    move = moved_up if forward else moved_down
    for n in range(3):
        values = summed(coef, [(place + n, [move(x, 1 << n) for x in values])], values)
    tiles = tiles_of(values)
    count = len(tiles)
    for n in range(1, count):
        at, before = (n, n - 1) if forward else (count - 1 - n, count - n)
        tiles[at] = summed(coef, [(place + 3, tiles[before])], tiles[at])
    return joined(tiles)


def response(coef, low, high, count, columns, kept):
    width = low[0].shape[1]
    row = iota((8, width), 0)
    tile = [jnp.where(row == 0, jnp.broadcast_to(x, (8, width)), 0.0) for x in low]
    for n in range(3):
        tile = summed(coef, [(FORWARD + n, [moved_up(x, 1 << n) for x in tile])], tile)
    tiles = [tile]
    for _ in range(1, count // 8):
        tiles.append(summed(coef, [(FORWARD + 3, tiles[-1])], zeros_like(tile)))
    tiles[-1] = [
        x + jnp.where(row == 7, jnp.broadcast_to(h, (8, width)), 0.0)
        for x, h in zip(tiles[-1], high)
    ]
    if kept == "last":
        end = sides(coef, SIDE, tiles[-1], columns, width, tiles[-1])
        return [x[7:] for x in end]
    first = joined(tiles)
    source = sides(coef, SIDE, first, columns, width, first)
    if kept == "all":
        second = recurrence(coef, source, False)
        return second, [z - y for z, y in zip(second, first)]
    tiles = tiles_of(source)
    end = tiles[-1]
    for tile in tiles[-2::-1]:
        end = summed(coef, [(BACKWARD + 3, end)], tile)
    for n in range(3):
        end = summed(coef, [(BACKWARD + n, [moved_down(x, 1 << n) for x in end])], end)
    return [x[:1] for x in end]


def at_ends(low, high, count):
    out = []
    for a, b in zip(low, high):
        shape = (count, a.shape[1])
        row = iota(shape, 0)
        out.append(
            jnp.where(
                row == 0,
                jnp.broadcast_to(a, shape),
                jnp.where(row == count - 1, jnp.broadcast_to(b, shape), 0.0),
            )
        )
    return out


def sides(coef, place, values, columns, cells, start):
    return summed(coef, [(place + n, x) for n, x in enumerate(beside(values, columns, cells))], start)


def sweep(coef, scaled, values, columns, cells):
    source = scaled
    if values is not None:
        source = summed(coef, [(BACKWARD, [moved_down(x, 1) for x in values])], scaled)
        source = sides(coef, SIDE, values, columns, cells, source)
    first = recurrence(coef, source, True)
    start = first
    if values is not None:
        start = [g + (y - s) for g, y, s in zip(scaled, first, source)]
    second = recurrence(coef, sides(coef, SIDE, first, columns, cells, start), False)
    return second, [z - y for z, y in zip(second, first)]


def next_sweep(coef, gap, low, high, columns, cells):
    drive = sides(coef, SIDE, gap, columns, cells, gap)
    begin = drive
    if low is not None:
        begin = [x + e for x, e in zip(drive, at_ends(low, high, gap[0].shape[0]))]
    first = recurrence(coef, begin, True)
    start = [x - q for x, q in zip(first, drive)]
    return first, recurrence(coef, sides(coef, SIDE, first, columns, cells, start), False)


def zeros_like(values):
    return [jnp.zeros_like(x) for x in values]


def scaled_source(coef, source):
    return summed(coef, [(CINV, source)], zeros_like(source))


def residual(coef, gap, ends, columns, cells):
    low = times(coef, BELOW, listed_rows(ends[0]))
    high = times(coef, ABOVE, listed_rows(ends[1]))
    start = summed(coef, [(BELOW, [moved_up(x, 1) for x in gap])], at_ends(low, high, gap[0].shape[0]))
    return sides(coef, LATERAL, gap, columns, cells, start)


def lanes_crossed(x, bits):
    width, dim = x.shape[-1], x.ndim - 1
    lane = iota(x.shape, dim)
    for bit in bits:
        step = 1 << bit
        x = jnp.where(
            (lane & step) != 0, pltpu.roll(x, step, dim), pltpu.roll(x, width - step, dim)
        )
    return x


def flipped(x, code, columns):
    code = jnp.broadcast_to(code, x.shape) if getattr(code, "ndim", 0) else jnp.full(x.shape, code, jnp.int32)
    width = x.shape[-1]
    along_j = columns.bit_length() - 1
    x = jnp.where((code & 1) == 1, lanes_crossed(x, range(along_j, width.bit_length() - 1)), x)
    return jnp.where((code & 2) == 2, lanes_crossed(x, range(along_j)), x)


def block_of(same, other, chip, rel):
    a, b = same[chip], other[chip]
    return jnp.where(jnp.full(a.shape, rel, jnp.int32) == 0, a, b)


def sent_by(idx, same, other, place):
    return block_of(same, other, idx[0, place], idx[0, place + 1])


def listed_rows(x):
    return [x[a : a + 1] for a in range(NV)]


def plane_of(ref, row):
    return jnp.concatenate([ref[c, row : row + NV, :] for c in range(4)], axis=1)


def ordered(idx, pieces, ref):
    for d, piece in enumerate(pieces):
        ref[(idx[0, SUB] + d) & 3] = piece[...]


def near_planes(idx, found, own):
    down, up, down_two, up_two = (idx[0, place + 2] for place in (DOWN, UP, DOWN_TWO, UP_TWO))
    first, last = plane_of(own, 0), plane_of(own, NV)
    return (
        ((plane_of(found, 5), down), (plane_of(found, 0), up)),
        ((last, up), (plane_of(found, 10), up_two)),
        ((plane_of(found, 15), down_two), (first, down)),
    )


def store_end_chunks(out, values, at):
    count = values[0].shape[0]
    for c in range(4):
        for a in range(NV):
            line = values[a][:, c * LANES : (c + 1) * LANES]
            out[c, at + a : at + a + 1, :] = line[:1]
            out[c, at + NV + a : at + NV + a + 1, :] = line[count - 1 :]


def whole(ref):
    return [jnp.concatenate([ref[q, a] for q in range(4)], axis=0) for a in range(NV)]


def store_whole(ref, values):
    for a in range(NV):
        for q in range(4):
            ref[q, a] = values[a][8 * q : 8 * q + 8]


def squares(values):
    total = None
    for x in values:
        for at in range(0, x.shape[1], LANES):
            part = x[:, at : at + LANES] * x[:, at : at + LANES]
            total = part if total is None else total + part
    return jnp.sum(total, axis=0, keepdims=True)


def index_kernel(partner, orient, owner_one, owner_two, out):
    device = lax.axis_index(BLK)
    core = lax.axis_index("blk_2")
    idx = {SUB: lax.axis_index("sub"), CORE: core}

    def find(j, found):
        down, one, two = found
        return (
            jnp.where(partner[j] == device, j, down),
            jnp.where(owner_one[j] == device, j, one),
            jnp.where(owner_two[j] == device, j, two),
        )

    zero = jnp.int32(0)
    down, one, two = lax.fori_loop(0, 64, find, (zero, zero, zero), unroll=8)

    def below_of(block):
        return lax.fori_loop(
            0, 64, lambda j, found: jnp.where(partner[j] == block, j, found), zero, unroll=8
        )

    down_two = below_of(down)
    down_three = below_of(down_two)
    up = partner[device]
    up_two = partner[up]
    up_three = partner[up_two]
    for place, block in ((POS_OWN, device), (POS_ONE, one), (POS_TWO, two)):
        idx[place] = ((block & 1) ^ core) * CHIPS + (block >> 1)
    idx[CHIP_ONE] = one >> 1
    idx[REL_ONE] = (one & 1) ^ core
    places = ((DOWN, down, down), (UP, up, device), (DOWN_TWO, down_two, down_two), (UP_TWO, up_two, up))
    places += ((DOWN_THREE, down_three, down_three), (UP_THREE, up_three, up_two))
    for place, block, crossing in places:
        idx[place] = block >> 1
        idx[place + 1] = (block & 1) ^ core
        idx[place + 2] = orient[crossing]
    lane = iota((1, LANES), 1)
    listed = jnp.zeros((1, LANES), jnp.int32)
    for place, value in idx.items():
        listed = jnp.where(lane == place, jnp.full((1, LANES), value, jnp.int32), listed)
    out[...] = listed


def pick_kernel(idx, same, other, out):
    up, down = sent_by(idx, same, other, UP), sent_by(idx, same, other, DOWN)
    out[0:5, :] = up[0:5]
    out[5:10, :] = down[5:10]
    out[10:15, :] = sent_by(idx, same, other, UP_TWO)[0:5]
    out[15:20, :] = sent_by(idx, same, other, DOWN_TWO)[5:10]
    out[20:25, :] = up[10:15]
    out[25:30, :] = down[15:20]
    out[30:32, :] = jnp.zeros((2, LANES), jnp.float32)


def pick_mid_kernel(idx, same, other, out):
    up, down = sent_by(idx, same, other, UP), sent_by(idx, same, other, DOWN)
    up_two, down_two = sent_by(idx, same, other, UP_TWO), sent_by(idx, same, other, DOWN_TWO)
    out[0:5, :] = up[0:5]
    out[5:10, :] = down[5:10]
    out[10:15, :] = up_two[0:5]
    out[15:20, :] = down_two[5:10]
    for n, block in enumerate((up, down, up_two, down_two)):
        out[20 + 5 * n : 25 + 5 * n, :] = block[10:15]
    out[40:45, :] = up[5:10]
    out[45:50, :] = down[0:5]
    out[50:55, :] = sent_by(idx, same, other, UP_THREE)[0:5]
    out[55:60, :] = sent_by(idx, same, other, DOWN_THREE)[5:10]
    out[60:64, :] = jnp.zeros((4, LANES), jnp.float32)


def local_kernel(coef, idx, p0, p1, p2, p3, local, gap, own, send, field, source):
    for d, piece in enumerate((p0, p1, p2, p3)):
        q = (idx[0, SUB] + d) & 3
        for a in range(NV):
            field[q, a] = piece[a]
            source[q, a] = piece[NV + a]
    given = whole(field)
    own[...] = jnp.zeros(own.shape, jnp.float32)
    store_end_chunks(own, given, 0)
    values, rest = sweep(coef, scaled_source(coef, whole(source)), given, 16, 512)
    store_whole(local, values)
    store_whole(gap, rest)
    store_end_chunks(own, values, 10)
    send[...] = own[idx[0, SUB]]


def plane_mean():
    cell, coarse = iota((512, LANES), 0), iota((512, LANES), 1)
    match = ((cell >> 5) == (coarse >> 3)) & (((cell & 15) >> 1) == (coarse & 7))
    return jnp.where(match, 0.25, 0.0)


def fine_kernel(
    coef, coef_mid, idx, e0, e1, e2, e3, own, local, gap, out, edges, total, mid, mid_gap, own_ends, send, found
):
    ordered(idx, (e0, e1, e2, e3), found)
    replies, before = [], None
    for kept, pair in zip(("all", "first", "last"), near_planes(idx, found, own)):
        below, above = (flipped(plane, code, 16) for plane, code in pair)
        before = (below, above) if before is None else before
        low = times(coef, FORWARD, listed_rows(below))
        high = times(coef, BACKWARD, listed_rows(above))
        replies.append(response(coef, low, high, 32, 16, kept))
    above = plane_of(found, 20) + jnp.concatenate(replies[1], axis=0)
    below = plane_of(found, 25) + jnp.concatenate(replies[2], axis=0)
    below, above = flipped(below, idx[0, DOWN + 2], 16), flipped(above, idx[0, UP + 2], 16)
    low = times(coef, FORWARD, listed_rows(below - before[0]))
    high = times(coef, BACKWARD, listed_rows(above - before[1]))
    rest = [x + y for x, y in zip(whole(gap), replies[0][1])]
    first, second = next_sweep(coef, rest, low, high, 16, 512)
    values = [x + y + z for x, y, z in zip(whole(local), replies[0][0], second)]
    store_whole(out, values)
    rest = [x + (z - y) for x, y, z in zip(rest, first, second)]
    left = residual(coef, rest, (-below, -above), 16, 512)
    edges[...] = jnp.zeros((16, 512), jnp.float32)
    for a in range(NV):
        edges[a : a + 1, :] = left[a][:1]
        edges[8 + a : 9 + a, :] = left[a][31:]
    row = iota((32, 512), 0)
    inner = (row > 0) & (row < 31)
    total[...] = jnp.broadcast_to(squares([jnp.where(inner, x, 0.0) for x in left]), (8, LANES))
    pair = jnp.where((iota((16, 32), 1) >> 1) == iota((16, 32), 0), 0.5, 0.0)
    mean = dot(jnp.concatenate(left, axis=0), plane_mean())
    source_mid = [dot_left(pair, mean[32 * a : 32 * a + 32]) for a in range(NV)]
    reply, rest = sweep(coef_mid, scaled_source(coef_mid, source_mid), None, 8, LANES)
    twice = next_sweep(coef_mid, rest, None, None, 8, LANES)[1]
    twice = [x + y for x, y in zip(reply, twice)]
    own_ends[...] = jnp.zeros(own_ends.shape, jnp.float32)
    store_end_chunks(own_ends, values, 0)
    for a in range(NV):
        mid[a] = reply[a]
        mid_gap[a] = rest[a]
        lines = (reply[a][:1], reply[a][15:], twice[a][:1], twice[a][15:])
        for c, line in enumerate(lines):
            own_ends[c, 10 + a : 11 + a, :] = line
    send[...] = own_ends[idx[0, SUB]]


def mid_kernel(
    coef_fine, coef, idx, e0, e1, e2, e3, own, edges, total, mid, mid_gap, doubled, send, quarter, found
):
    ordered(idx, (e0, e1, e2, e3), found)
    pairs = list(near_planes(idx, found, own))
    below, above = (flipped(plane, code, 16) for plane, code in pairs[0])
    up_two, down_two = idx[0, UP_TWO + 2], idx[0, DOWN_TWO + 2]
    pairs.append(((plane_of(found, 40), up_two), (plane_of(found, 50), idx[0, UP_THREE + 2])))
    pairs.append(((plane_of(found, 55), idx[0, DOWN_THREE + 2]), (plane_of(found, 45), down_two)))

    low = times(coef_fine, BELOW, listed_rows(below), [edges[a : a + 1, :] for a in range(NV)])
    high = times(coef_fine, ABOVE, listed_rows(above), [edges[8 + a : 9 + a, :] for a in range(NV)])
    total_zero = total[:1] + squares(low) + squares(high)

    gap = jnp.zeros((3, 512), jnp.float32)
    stacked = jnp.concatenate([part for pair in pairs for plane, _ in pair for part in (plane, gap)], axis=0)
    mean = dot(stacked, plane_mean())
    replies = []
    for n, (kept, pair) in enumerate(zip(("all", "all", "all", "first", "last"), pairs)):
        planes = [
            flipped(0.5 * mean[8 * m : 8 * m + NV], code, 8)
            for m, (_, code) in zip((2 * n, 2 * n + 1), pair)
        ]
        low = times(coef_fine, BELOW, listed_rows(planes[0]))
        high = times(coef_fine, ABOVE, listed_rows(planes[1]))
        low, high = times(coef, CINV, low), times(coef, CINV, high)
        replies.append(response(coef, low, high, 16, 8, kept))
    (own_reply, own_gap), (up_reply, up_gap), (down_reply, down_gap) = replies[:3]

    def row_of(values, k):
        return jnp.concatenate([x[k : k + 1] for x in values], axis=0)

    def driven(gap, below, above):
        low = times(coef, FORWARD, listed_rows(below))
        return next_sweep(coef, gap, low, times(coef, BACKWARD, listed_rows(above)), 8, LANES)

    down, up = idx[0, DOWN + 2], idx[0, UP + 2]
    field = [mid[a] + own_reply[a] for a in range(NV)]
    below = flipped(found[1, 25:30, :] + row_of(down_reply, 15), down, 8)
    above = flipped(found[0, 20:25, :] + row_of(up_reply, 0), up, 8)
    above_up = flipped(found[0, 30:35, :] + jnp.concatenate(replies[3], axis=0), up_two, 8)
    below_down = flipped(found[1, 35:40, :] + jnp.concatenate(replies[4], axis=0), down_two, 8)
    rest = [mid_gap[a] + own_gap[a] for a in range(NV)]
    first, second = driven(rest, below, above)
    values = [x + y for x, y in zip(field, second)]
    rest = [x + (z - y) for x, y, z in zip(rest, first, second)]
    up_second = driven(up_gap, flipped(row_of(field, 15), up, 8), above_up)[1]
    down_second = driven(down_gap, below_down, flipped(row_of(field, 0), down, 8))[1]
    new_above = found[2, 20:25, :] + row_of(up_reply, 0) + row_of(up_second, 0)
    new_below = found[3, 25:30, :] + row_of(down_reply, 15) + row_of(down_second, 15)
    change = (flipped(new_below, down, 8) - below, flipped(new_above, up, 8) - above)
    left = residual(coef, rest, change, 8, LANES)
    pair = jnp.where((iota((8, 16), 1) >> 1) == iota((8, 16), 0), 0.5, 0.0)
    mean = jnp.concatenate([dot_left(pair, x) for x in left], axis=0)
    cell, place = iota((LANES, LANES), 0), iota((LANES, LANES), 1)
    match_i = (cell >> 4) == (place & 7)
    column = (cell & 7) >> 1
    own_plane = (iota((8, LANES), 1) >> 4) == iota((8, LANES), 0)
    for half in range(2):
        match = match_i & (column == 2 * half + ((place >> 3) & 1))
        spread = dot(mean, jnp.where(match, 0.25, 0.0))
        for a in range(NV):
            kept = jnp.where(own_plane, spread[8 * a : 8 * a + 8], 0.0)
            at = half * NV + a
            send[at : at + 1, :] = jnp.sum(kept, axis=0, keepdims=True)
    total_one = squares(left)
    total_zero = total_zero + pltpu.roll(total_zero, 64, 1)
    total_one = total_one + pltpu.roll(total_one, 64, 1)
    send[TOTAL_ROW : TOTAL_ROW + 1, :] = jnp.where(iota((1, LANES), 1) < 64, total_zero, total_one)
    for a in range(NV):
        for k in range(16):
            line = values[a][k : k + 1]
            quarter[k // 4, a * 4 + k % 4 : a * 4 + k % 4 + 1, :] = line
            at = a * 8 + 2 * (k % 4)
            doubled[k // 4, at : at + 1, :] = line
            doubled[k // 4, at + 1 : at + 2, :] = line
    send[QUARTER_ROWS : QUARTER_ROWS + 20, :] = quarter[idx[0, SUB]]
    send[QUARTER_ROWS + 20 :, :] = jnp.zeros((1, LANES), jnp.float32)


def coarse_kernel(coef, idx, lanes, same, other, field, doubled, corrected, one, two, norms):
    groups = ((8, 8, LANES))
    lane3 = iota(groups, 2)
    side3 = iota(groups, 1)

    def sent(r):
        return jnp.concatenate(
            [ref[pl.ds(r, CHIPS, stride=SENT_ROWS), :] for ref in (same, other)], axis=0
        )

    square = (LANES, LANES)
    row, column = iota(square, 0), iota(square, 1)

    def block_at(x):
        return 2 * (x & 31) + (((x >> 5) & 1) ^ idx[0, CORE])

    alike = (row >> 6) == (column >> 6)
    beyond = jnp.broadcast_to(lanes[0:1, :], square)
    beyond_of_row = beyond.T
    at_row, at_column = block_at(row).astype(jnp.float32), block_at(column).astype(jnp.float32)
    from_down = jnp.where(alike & (beyond_of_row == at_column), 1.0, 0.0)
    from_up = jnp.where(alike & (at_row == beyond), 1.0, 0.0)
    code_up = jnp.broadcast_to(lanes[1:2, :], (8, LANES))
    code_down = dot(code_up, from_down)

    code_up = (code_up + 0.5).astype(jnp.int32)
    code_down = (code_down + 0.5).astype(jnp.int32)

    def flip_planes(x, code):
        side = iota((8, LANES), 0)
        out_planes = []
        for pair in x:
            turned = []
            for p in pair:
                q = pltpu.roll(p, 4, 0)
                q = jnp.where((side & 2) != 0, pltpu.roll(q, 2, 0), pltpu.roll(q, 6, 0))
                q = jnp.where((side & 1) != 0, pltpu.roll(q, 1, 0), pltpu.roll(q, 7, 0))
                turned.append(jnp.where((code & 1) == 1, q, p))
            swapped = [pltpu.roll(p, 64, 1) for p in turned[::-1]]
            out_planes.append(
                [jnp.where((code & 2) == 2, s, p) for s, p in zip(swapped, turned)]
            )
        return out_planes

    def mapped(planes, chosen, code):
        got = dot(planes, chosen)
        pairs = [
            [got[16 * a + 8 * p : 16 * a + 8 * p + 8] for p in range(2)] for a in range(NV)
        ]
        return flip_planes(pairs, code)

    source = []
    for a in range(NV):
        both = jnp.concatenate([sent(a), sent(NV + a)], axis=0)
        turned = both.T.reshape(8, 2, 8, LANES)
        source.append([turned[:, 0], turned[:, 1]])
    totals = sent(TOTAL_ROW)
    low_lane = iota(totals.shape, 1) < 64
    total_zero = jnp.where(low_lane, totals, 0.0)
    total_one = jnp.where(low_lane, 0.0, totals)
    def pairwise(terms, start):
        out_pairs = [[None, None] for _ in range(NV)]
        for p in range(2):
            got = [x[p] for x in start]
            for place_of, values in terms:
                got = times(coef, place_of, [x[p] for x in values], got)
            for a in range(NV):
                out_pairs[a][p] = got[a]
        return out_pairs

    def beside_coarse(values):
        low = [[jnp.where(side3 > 0, pltpu.roll(x, 1, 1), 0.0) for x in pair] for pair in values]
        high = [[jnp.where(side3 < 7, pltpu.roll(x, 7, 1), 0.0) for x in pair] for pair in values]
        left = [
            [jnp.where(lane3 >= 64, pltpu.roll(pair[1], 64, 2), 0.0), pair[0]] for pair in values
        ]
        right = [
            [pair[1], jnp.where(lane3 < 64, pltpu.roll(pair[0], 64, 2), 0.0)] for pair in values
        ]
        return [low, high, left, right]

    def combined(f, *fields):
        return [[f(*(x[a][p] for x in fields)) for p in range(2)] for a in range(NV)]

    def with_ends(values, coef_of, low_at, low, high_at, high):
        out_pairs = [[None, None] for _ in range(NV)]
        for p in range(2):
            under = times(coef_of, low_at, [x[p] for x in low])
            over = times(coef_of, high_at, [x[p] for x in high])
            for a in range(NV):
                x = values[a][p]
                out_pairs[a][p] = jnp.concatenate(
                    [x[:1] + under[a][None], x[1:7], x[7:] + over[a][None]], axis=0
                )
        return out_pairs

    def sides_coarse(place_of, values, start):
        return pairwise([(place_of + n, x) for n, x in enumerate(beside_coarse(values))], start)

    def carried(values, forward):
        place_of = FORWARD if forward else BACKWARD
        out_pairs = [[None, None] for _ in range(NV)]
        for p in range(2):
            before = None
            planes = [None] * 8
            for k in range(8) if forward else range(7, -1, -1):
                own = [x[p][k] for x in values]
                before = own if before is None else times(coef, place_of, before, own)
                planes[k] = before
            for a in range(NV):
                out_pairs[a][p] = jnp.stack([planes[k][a] for k in range(8)], axis=0)
        return out_pairs

    def edge(values, k):
        return jnp.concatenate([x[p][k] for x in values for p in range(2)], axis=0)

    def neighbours(values):
        below = mapped(edge(values, 7), from_down, code_down)
        above = mapped(edge(values, 0), from_up, code_up)
        return below, above

    empty = [[jnp.zeros(groups, jnp.float32)] * 2 for _ in range(NV)]
    first = carried(pairwise([(CINV, source)], empty), True)
    change = values = carried(sides_coarse(SIDE, first, first), False)
    rest = combined(jnp.subtract, values, first)
    for _ in range(3):
        below, above = neighbours(change)
        drive = sides_coarse(SIDE, rest, rest)
        first = carried(with_ends(drive, coef, FORWARD, below, BACKWARD, above), True)
        start = combined(jnp.subtract, first, drive)
        change = carried(sides_coarse(SIDE, first, start), False)
        values = combined(jnp.add, values, change)
        rest = combined(lambda x, y, z: x + (z - y), rest, first, change)

    below, above = neighbours(change)
    zero_plane = jnp.zeros((1, 8, LANES), jnp.float32)
    lifted = combined(lambda x: jnp.concatenate([zero_plane, x[:7]], axis=0), rest)
    left = sides_coarse(LATERAL, rest, pairwise([(BELOW, lifted)], empty))
    left = with_ends(left, coef, BELOW, below, ABOVE, above)
    total_two = None
    for pair in left:
        for x in pair:
            part = jnp.sum(x * x, axis=0)
            total_two = part if total_two is None else total_two + part

    lane = iota((8, LANES), 1)
    result = jnp.zeros((8, LANES), jnp.float32)
    sizes = (NV * 64 * 32 * 512, NV * 64 * 16 * 128, NV * 64 * 8 * 32)
    for level, total in enumerate((total_zero, total_one, total_two)):
        total = jnp.sum(jnp.sum(total, axis=0, keepdims=True), axis=1, keepdims=True)
        root = jnp.sqrt(jnp.broadcast_to(total, (8, LANES)) / float(sizes[level]))
        result = jnp.where(lane == level, root, result)
    norms[...] = result[:1, :3]

    which = iota((8, LANES), 0)
    wanted = jnp.where(
        which < 2,
        jnp.full((8, LANES), idx[0, POS_OWN], jnp.int32),
        jnp.where(
            which < 4,
            jnp.full((8, LANES), idx[0, POS_ONE], jnp.int32),
            jnp.full((8, LANES), idx[0, POS_TWO], jnp.int32),
        ),
    )
    chosen = jnp.where(lane == wanted + 64 * (which & 1), 1.0, 0.0)
    out = []
    for a in range(NV):
        laid = jnp.stack(values[a], axis=1).reshape(LANES, LANES)
        out.append(dot_nt(chosen, laid))

    s = idx[0, SUB]
    row = iota((2 * LANES, LANES), 0)
    cell = iota((2 * LANES, LANES), 1)
    half, inner_j, inner_i = row >> 7, (row >> 3) & 1, row & 7
    fits = (inner_i == (cell >> 4)) & (2 * half + inner_j == ((cell & 7) >> 1))
    to_mid = jnp.where(fits, 1.0, 0.0)
    fits = (inner_i == (cell >> 2)) & (2 * half + inner_j == (cell & 3)) & (cell < 32)
    to_cells = jnp.where(fits, 1.0, 0.0)

    def laid(which, count, shift):
        parts = []
        shape = (count, 2 * LANES)
        plane = (iota(shape, 1) >> 4) & 7
        wanted = 2 * s + (iota(shape, 0) >> shift)
        for a in range(NV):
            pair = jnp.concatenate(
                [out[a][2 * which : 2 * which + 1], out[a][2 * which + 1 : 2 * which + 2]], axis=1
            )
            parts.append(jnp.where(plane == wanted, jnp.broadcast_to(pair, shape), 0.0))
        return parts

    x_one = doubled[s] + dot(jnp.concatenate(laid(0, 8, 2), axis=0), to_mid)
    mid, fine = iota((LANES, 512), 0), iota((LANES, 512), 1)
    fits = ((fine >> 5) == (mid >> 3)) & (((fine & 15) >> 1) == (mid & 7))
    spread = dot(x_one, jnp.where(fits, 1.0, 0.0))
    for a in range(NV):
        corrected[a] = field[s, a] + spread[8 * a : 8 * a + 8]
    at = pl.ds(pl.multiple_of(idx[0, CHIP_ONE] * SENT_ROWS, 8), SENT_ROWS)
    held = jnp.where(jnp.full((SENT_ROWS, LANES), idx[0, REL_ONE], jnp.int32) == 0, same[at, :], other[at, :])
    held = held[QUARTER_ROWS : QUARTER_ROWS + 20]
    for a, part in enumerate(laid(1, 8, 1)):
        got = dot(part, to_mid)
        one[a] = held[4 * a : 4 * a + 4] + got[:4]
    for a, part in enumerate(laid(2, 8, 0)):
        two[a] = dot(part, to_cells)[:2, :32]


def product(a, b):
    return jnp.einsum("...ab,...bc->...ac", a, b, precision=PRECISE)


def coefficients(couple):
    center = couple[:, 0]
    identity = jnp.broadcast_to(jnp.eye(NV, dtype=jnp.float32), center.shape)
    inverse = identity
    for _ in range(6):
        inverse = product(inverse, 2.0 * identity - product(center, inverse))
    scaled = product(inverse[:, None], couple[:, 1:])
    powers = [scaled[:, 4:]]
    for _ in range(3):
        powers.append(product(powers[-1], powers[-1]))
    powers = jnp.stack(powers, axis=2).reshape(3, 8, NV, NV)
    listed = jnp.concatenate([inverse[:, None], scaled[:, :4], powers, couple], axis=1)
    return listed.reshape(3, MATRICES * 25)


def gathered(payload):
    copies = jnp.broadcast_to(payload, (CHIPS, *payload.shape))
    same = lax.all_to_all(copies, CHIP, split_axis=0, concat_axis=0, tiled=True)
    other = lax.ppermute(same, "blk_2", [(0, 1), (1, 0)])
    return same, other


def around(piece):
    moves = [[((i + d) % 4, i) for i in range(4)] for d in range(1, 4)]
    return [piece] + [lax.ppermute(piece, "sub", move) for move in moves]


def shards(solution, right_side, couple, partner, orient, owner_one, owner_two):
    core = lax.axis_index("blk_2")

    pieces = around(jnp.concatenate([solution[:, 0], right_side[:, 0]], axis=0))

    lanes = jnp.stack([partner, orient]).reshape(2, CHIPS, 2).transpose(0, 2, 1)
    lanes = jnp.where(core == 0, lanes, lanes[:, ::-1]).reshape(2, 64).astype(jnp.float32)
    lanes = jnp.concatenate([lanes, lanes], axis=1)
    idx = pl.pallas_call(
        index_kernel,
        out_shape=jax.ShapeDtypeStruct((1, LANES), jnp.int32),
        in_specs=[SMEM] * 4,
        out_specs=VMEM,
    )(partner, orient, owner_one, owner_two)
    coef = coefficients(couple)

    whole_shape = (4, NV, 8, 512)
    mid_shape = (NV, 16, LANES)
    def picked(sent, kernel, count):
        (rows,) = call(kernel, [(count, LANES)], [SMEM] + [VMEM] * 2)(idx, *gathered(sent))
        return around(rows)

    local, gap, own, sent = call(
        local_kernel,
        [whole_shape, whole_shape, (4, 24, LANES), (24, LANES)],
        [SMEM] * 2 + [VMEM] * 4,
        [pltpu.VMEM(whole_shape, jnp.float32)] * 2,
    )(coef[0], idx, *pieces)
    field, edges, total, mid, mid_gap, own, sent = call(
        fine_kernel,
        [whole_shape, (16, 512), (8, LANES), mid_shape, mid_shape, (4, 16, LANES), (16, LANES)],
        [SMEM] * 3 + [VMEM] * 7,
        [pltpu.VMEM((4, 32, LANES), jnp.float32)],
    )(coef[0], coef[1], idx, *picked(sent, pick_kernel, 32), own, local, gap)
    doubled, sent = call(
        mid_kernel,
        [(4, 40, LANES), (SENT_ROWS, LANES)],
        [SMEM] * 3 + [VMEM] * 9,
        [pltpu.VMEM((4, rows, LANES), jnp.float32) for rows in (20, 64)],
    )(coef[0], coef[1], idx, *picked(sent, pick_mid_kernel, 64), own, edges, total, mid, mid_gap)
    got = gathered(sent)
    corrected, one, two, norms = call(
        coarse_kernel,
        [(NV, 8, 512), (NV, 4, LANES), (NV, 2, 32), (1, 3)],
        [SMEM] * 2 + [VMEM] * 5,
    )(coef[2], idx, lanes, *[x.reshape(CHIPS * SENT_ROWS, LANES) for x in got], field, doubled)
    return (corrected[:, None], one[:, None], two[:, None], norms.reshape(3))


def solution(mesh):
    torus = Mesh(
        mesh.devices.reshape(4, 8, 2, mesh.shape["sub"]), ("blk_0", "blk_1", "blk_2", "sub")
    )
    split = P(None, BLK, "sub", None)
    return jax.shard_map(
        shards,
        mesh=torus,
        in_specs=(split, split, P(), P(), P(), P(), P()),
        out_specs=(split, split, split, P()),
        check_vma=False,
    )
```

```python
import jax
import jax.numpy as jnp
from jax import lax
from jax.experimental import pallas as pl
from jax.experimental.pallas import tpu as pltpu
from jax.sharding import Mesh
from jax.sharding import PartitionSpec as P

NV = 5
LANES = 128
CHIPS = 32
BLK = ("blk_0", "blk_1", "blk_2")
CHIP = ("blk_0", "blk_1")
PRECISE = lax.Precision.HIGHEST

POWERS, RAW, SUMS, TOPS, LONG = 1, 5, 7, 8, 9
PLACE_OF = (
    [(0, 0)]
    + [(1 + n, POWERS) for n in range(4)]
    + [(row, POWERS + n) for row in (5, 6) for n in range(4)]
    + [(1 + n, RAW) for n in range(6)]
    + [(n, group) for group in (SUMS, TOPS) for n in range(5)]
    + [(0, LONG)]
)
CINV, SIDE, FORWARD, BACKWARD, LATERAL, BELOW, ABOVE, SUM, TOP, LAST_POWER = 0, 1, 5, 9, 13, 17, 18, 19, 24, 29

SUB, CORE, POS_OWN, POS_ONE, POS_TWO, CHIP_ONE, REL_ONE = range(7)
DOWN, UP, DOWN_TWO, UP_TWO, DOWN_THREE, UP_THREE = 8, 11, 14, 17, 20, 23

TOTAL_ROW, QUARTER_ROWS, SENT_ROWS = 10, 11, 32

VMEM = pl.BlockSpec(memory_space=pltpu.VMEM)
SMEM = pl.BlockSpec(memory_space=pltpu.SMEM)


def call(kernel, out_shapes, in_specs, scratch=()):
    return pl.pallas_call(
        kernel,
        out_shape=tuple(jax.ShapeDtypeStruct(shape, jnp.float32) for shape in out_shapes),
        in_specs=in_specs,
        out_specs=tuple(VMEM for _ in out_shapes),
        scratch_shapes=list(scratch),
        compiler_params=pltpu.CompilerParams(vmem_limit_bytes=40 * 1024 * 1024),
    )


def iota(shape, dim):
    return lax.broadcasted_iota(jnp.int32, shape, dim)


def parts_of(x):
    high = x.astype(jnp.bfloat16)
    rest = x - high.astype(jnp.float32)
    middle = rest.astype(jnp.bfloat16)
    return high, middle, (rest - middle.astype(jnp.float32)).astype(jnp.bfloat16)


def contracted(a, b, dims):
    return lax.dot_general(a, b, (dims, ((), ())), preferred_element_type=jnp.float32)


def dot(values, exact):
    exact = exact.astype(jnp.bfloat16)
    high, middle, low = (contracted(x, exact, ((1,), (0,))) for x in parts_of(values))
    return high + (middle + low)


def dot_left(exact, values):
    exact = exact.astype(jnp.bfloat16)
    high, middle, low = (contracted(exact, x, ((1,), (0,))) for x in parts_of(values))
    return high + (middle + low)


def dot_nt(exact, values):
    exact = exact.astype(jnp.bfloat16)
    high, middle, low = (contracted(exact, x, ((1,), (1,))) for x in parts_of(values))
    return high + (middle + low)


def times(coef, place, values, start=None):
    out = list(start) if start is not None else [None] * NV
    row, group = PLACE_OF[place]
    for a in range(NV):
        for b in range(NV):
            term = coef[row, group * 25 + a * NV + b] * values[b]
            out[a] = term if out[a] is None else out[a] + term
    return out


def summed(coef, terms, start):
    width = start[0].shape[1]
    parts = []
    for at in range(0, width, LANES):
        out = [x[:, at : at + LANES] for x in start]
        for place, values in terms:
            out = times(coef, place, [x[:, at : at + LANES] for x in values], out)
        parts.append(out)
    if len(parts) == 1:
        return parts[0]
    return [jnp.concatenate([part[a] for part in parts], axis=1) for a in range(NV)]


def beside(values, columns, cells):
    shape = values[0].shape
    width = shape[1]
    cell = iota(shape, 1) & (cells - 1)
    column = cell & (columns - 1)
    cases = (
        (columns, cell >= columns),
        (width - columns, cell < cells - columns),
        (1, column != 0),
        (width - 1, column != columns - 1),
    )
    return [
        [jnp.where(mask, pltpu.roll(x, shift, 1), 0.0) for x in values] for shift, mask in cases
    ]


def moved_up(x, by):
    return jnp.where(iota(x.shape, 0) >= by, pltpu.roll(x, by, 0), 0.0)


def moved_down(x, by):
    count = x.shape[0]
    return jnp.where(iota(x.shape, 0) < count - by, pltpu.roll(x, count - by, 0), 0.0)


def tiles_of(values):
    return [[x[at : at + 8] for x in values] for at in range(0, values[0].shape[0], 8)]


def joined(tiles):
    return [jnp.concatenate([tile[a] for tile in tiles], axis=0) for a in range(NV)]


def recurrence(coef, values, forward):
    place = FORWARD if forward else BACKWARD
    move = moved_up if forward else moved_down
    for n in range(3):
        values = summed(coef, [(place + n, [move(x, 1 << n) for x in values])], values)
    tiles = tiles_of(values)
    count = len(tiles)
    for n in range(1, count):
        at, before = (n, n - 1) if forward else (count - 1 - n, count - n)
        tiles[at] = summed(coef, [(place + 3, tiles[before])], tiles[at])
    return joined(tiles)


def response(coef, low, high, count, columns, kept):
    width = low[0].shape[1]
    row = iota((8, width), 0)
    tile = [jnp.where(row == 0, jnp.broadcast_to(x, (8, width)), 0.0) for x in low]
    for n in range(3):
        tile = summed(coef, [(FORWARD + n, [moved_up(x, 1 << n) for x in tile])], tile)
    tiles = [tile]
    for _ in range(1, count // 8):
        tiles.append(summed(coef, [(FORWARD + 3, tiles[-1])], zeros_like(tile)))
    tiles[-1] = [
        x + jnp.where(row == 7, jnp.broadcast_to(h, (8, width)), 0.0)
        for x, h in zip(tiles[-1], high)
    ]
    if kept == "last":
        end = sides(coef, SIDE, tiles[-1], columns, width, tiles[-1])
        return [x[7:] for x in end]
    first = joined(tiles)
    source = sides(coef, SIDE, first, columns, width, first)
    if kept == "all":
        second = recurrence(coef, source, False)
        return second, [z - y for z, y in zip(second, first)]
    tiles = tiles_of(source)
    end = tiles[-1]
    for tile in tiles[-2::-1]:
        end = summed(coef, [(BACKWARD + 3, end)], tile)
    for n in range(3):
        end = summed(coef, [(BACKWARD + n, [moved_down(x, 1 << n) for x in end])], end)
    return [x[:1] for x in end]


def at_ends(low, high, count):
    out = []
    for a, b in zip(low, high):
        shape = (count, a.shape[1])
        row = iota(shape, 0)
        out.append(
            jnp.where(
                row == 0,
                jnp.broadcast_to(a, shape),
                jnp.where(row == count - 1, jnp.broadcast_to(b, shape), 0.0),
            )
        )
    return out


def sides(coef, place, values, columns, cells, start):
    return summed(coef, [(place + n, x) for n, x in enumerate(beside(values, columns, cells))], start)


def sweep(coef, scaled, values, columns, cells):
    source = scaled
    if values is not None:
        source = summed(coef, [(BACKWARD, [moved_down(x, 1) for x in values])], scaled)
        source = sides(coef, SIDE, values, columns, cells, source)
    first = recurrence(coef, source, True)
    start = first
    if values is not None:
        start = [g + (y - s) for g, y, s in zip(scaled, first, source)]
    second = recurrence(coef, sides(coef, SIDE, first, columns, cells, start), False)
    return second, [z - y for z, y in zip(second, first)]


def next_sweep(coef, gap, low, high, columns, cells):
    drive = sides(coef, SIDE, gap, columns, cells, gap)
    begin = drive
    if low is not None:
        begin = [x + e for x, e in zip(drive, at_ends(low, high, gap[0].shape[0]))]
    first = recurrence(coef, begin, True)
    start = [x - q for x, q in zip(first, drive)]
    return first, recurrence(coef, sides(coef, SIDE, first, columns, cells, start), False)


def zeros_like(values):
    return [jnp.zeros_like(x) for x in values]


def scaled_source(coef, source):
    return summed(coef, [(CINV, source)], zeros_like(source))


def residual(coef, gap, ends, columns, cells):
    low = times(coef, BELOW, listed_rows(ends[0]))
    high = times(coef, ABOVE, listed_rows(ends[1]))
    start = summed(coef, [(BELOW, [moved_up(x, 1) for x in gap])], at_ends(low, high, gap[0].shape[0]))
    return sides(coef, LATERAL, gap, columns, cells, start)


def lanes_crossed(x, bits):
    width, dim = x.shape[-1], x.ndim - 1
    lane = iota(x.shape, dim)
    for bit in bits:
        step = 1 << bit
        x = jnp.where(
            (lane & step) != 0, pltpu.roll(x, step, dim), pltpu.roll(x, width - step, dim)
        )
    return x


def flipped(x, code, columns):
    code = jnp.broadcast_to(code, x.shape) if getattr(code, "ndim", 0) else jnp.full(x.shape, code, jnp.int32)
    width = x.shape[-1]
    along_j = columns.bit_length() - 1
    x = jnp.where((code & 1) == 1, lanes_crossed(x, range(along_j, width.bit_length() - 1)), x)
    return jnp.where((code & 2) == 2, lanes_crossed(x, range(along_j)), x)


def block_of(same, other, chip, rel):
    a, b = same[chip], other[chip]
    return jnp.where(jnp.full(a.shape, rel, jnp.int32) == 0, a, b)


def sent_by(idx, same, other, place):
    return block_of(same, other, idx[0, place], idx[0, place + 1])


def listed_rows(x):
    return [x[a : a + 1] for a in range(NV)]


def plane_of(ref, row):
    return jnp.concatenate([ref[c, row : row + NV, :] for c in range(4)], axis=1)


def ordered(idx, pieces, ref):
    for d, piece in enumerate(pieces):
        ref[(idx[0, SUB] + d) & 3] = piece[...]


def near_planes(idx, found, own):
    down, up, down_two, up_two = (idx[0, place + 2] for place in (DOWN, UP, DOWN_TWO, UP_TWO))
    first, last = plane_of(own, 0), plane_of(own, NV)
    return (
        ((plane_of(found, 5), down), (plane_of(found, 0), up)),
        ((last, up), (plane_of(found, 10), up_two)),
        ((plane_of(found, 15), down_two), (first, down)),
    )


def store_end_chunks(out, values, at):
    count = values[0].shape[0]
    for c in range(4):
        for a in range(NV):
            line = values[a][:, c * LANES : (c + 1) * LANES]
            out[c, at + a : at + a + 1, :] = line[:1]
            out[c, at + NV + a : at + NV + a + 1, :] = line[count - 1 :]


def whole(ref):
    return [jnp.concatenate([ref[q, a] for q in range(4)], axis=0) for a in range(NV)]


def store_whole(ref, values):
    for a in range(NV):
        for q in range(4):
            ref[q, a] = values[a][8 * q : 8 * q + 8]


def squares(values):
    total = None
    for x in values:
        for at in range(0, x.shape[1], LANES):
            part = x[:, at : at + LANES] * x[:, at : at + LANES]
            total = part if total is None else total + part
    return jnp.sum(total, axis=0, keepdims=True)


def coefficients(couple, held, outs):
    square = (LANES, LANES)
    lane = iota(square, 1)
    base = jnp.where(lane < 7, 0, jnp.where(lane < 14, 7, 14))
    row = iota(square, 0)

    def entries(x, group=0):
        return [x[group * 25 + e : group * 25 + e + 1] for e in range(25)]

    def product(x, y):
        out = []
        for a in range(NV):
            for b in range(NV):
                total = x[a * NV] * y[b]
                for k in range(1, NV):
                    total = total + x[a * NV + k] * y[k * NV + b]
                out.append(total)
        return out

    def keep(group, values):
        for e, x in enumerate(values):
            held[group * 25 + e : group * 25 + e + 1, :] = x

    given = couple[...].T
    raw = entries(given)
    center = entries(dot(given, jnp.where(row == base, 1.0, 0.0)))
    identity = [jnp.full((1, LANES), 1.0 if e % 6 == 0 else 0.0, jnp.float32) for e in range(25)]

    def twice_less(x):
        return [2.0 * i - y for i, y in zip(identity, x)]

    inverse = twice_less(center)
    for _ in range(5):
        inverse = product(inverse, twice_less(product(center, inverse)))
    held[...] = jnp.zeros((256, LANES), jnp.float32)
    keep(0, inverse)
    power = scaled = product(inverse, raw)
    for n in range(4):
        keep(POWERS + n, power)
        power = product(power, power)
    keep(RAW, raw)
    keep(6, power)
    powers = held[...]
    groups = (1, 2, 3, 4, 6)
    forward = dot(powers, jnp.where(row == base + 5, 1.0, 0.0))
    backward = dot(powers, jnp.where(row == base + 6, 1.0, 0.0))
    first = (lane == base)[:1]
    sums = tops = [jnp.where(first, i, x) for i, x in zip(identity, scaled)]
    long = identity
    for group in groups:
        f, b = entries(forward, group), entries(backward, group)
        sums = [x + y for x, y in zip(sums, product(product(b, sums), f))]
        tops = product(b, tops)
        long = product(long, f)
    keep(SUMS, sums)
    keep(TOPS, tops)
    keep(LONG, long)
    turned = held[...].T
    for level, out in enumerate(outs):
        out[...] = turned[7 * level : 7 * level + 8]


def far_ends(coef, low, high, kept, columns, cells):
    if kept == "last":
        end = times(coef, LAST_POWER, low, high)
        return sides(coef, SIDE, end, columns, cells, end)
    out = sides(coef, SUM + 1, low, columns, cells, times(coef, SUM, low))
    return sides(coef, TOP + 1, high, columns, cells, times(coef, TOP, high, out))


def setup_kernel(partner, orient, owner_one, owner_two, couple, out, begin, fine, mid, coarse, held):
    coefficients(couple, held, (fine, mid, coarse))
    begin[...] = fine[...]
    device = lax.axis_index(BLK)
    core = lax.axis_index("blk_2")
    idx = {SUB: lax.axis_index("sub"), CORE: core}

    def find(j, found):
        down, one, two = found
        return (
            jnp.where(partner[j] == device, j, down),
            jnp.where(owner_one[j] == device, j, one),
            jnp.where(owner_two[j] == device, j, two),
        )

    zero = jnp.int32(0)
    down, one, two = lax.fori_loop(0, 64, find, (zero, zero, zero), unroll=8)

    def below_of(block):
        return lax.fori_loop(
            0, 64, lambda j, found: jnp.where(partner[j] == block, j, found), zero, unroll=8
        )

    down_two = below_of(down)
    down_three = below_of(down_two)
    up = partner[device]
    up_two = partner[up]
    up_three = partner[up_two]
    for place, block in ((POS_OWN, device), (POS_ONE, one), (POS_TWO, two)):
        idx[place] = ((block & 1) ^ core) * CHIPS + (block >> 1)
    idx[CHIP_ONE] = one >> 1
    idx[REL_ONE] = (one & 1) ^ core
    places = ((DOWN, down, down), (UP, up, device), (DOWN_TWO, down_two, down_two), (UP_TWO, up_two, up))
    places += ((DOWN_THREE, down_three, down_three), (UP_THREE, up_three, up_two))
    for place, block, crossing in places:
        idx[place] = block >> 1
        idx[place + 1] = (block & 1) ^ core
        idx[place + 2] = orient[crossing]
    lane = iota((1, LANES), 1)
    listed = jnp.zeros((1, LANES), jnp.int32)
    for place, value in idx.items():
        listed = jnp.where(lane == place, jnp.full((1, LANES), value, jnp.int32), listed)
    out[...] = listed


def pick_kernel(idx, same, other, out):
    up, down = sent_by(idx, same, other, UP), sent_by(idx, same, other, DOWN)
    out[0:5, :] = up[0:5]
    out[5:10, :] = down[5:10]
    out[10:15, :] = sent_by(idx, same, other, UP_TWO)[0:5]
    out[15:20, :] = sent_by(idx, same, other, DOWN_TWO)[5:10]
    out[20:25, :] = up[10:15]
    out[25:30, :] = down[15:20]
    out[30:32, :] = jnp.zeros((2, LANES), jnp.float32)


def pick_mid_kernel(idx, same, other, out):
    up, down = sent_by(idx, same, other, UP), sent_by(idx, same, other, DOWN)
    up_two, down_two = sent_by(idx, same, other, UP_TWO), sent_by(idx, same, other, DOWN_TWO)
    out[0:5, :] = up[0:5]
    out[5:10, :] = down[5:10]
    out[10:15, :] = up_two[0:5]
    out[15:20, :] = down_two[5:10]
    for n, block in enumerate((up, down, up_two, down_two)):
        out[20 + 5 * n : 25 + 5 * n, :] = block[10:15]
    out[40:45, :] = up[5:10]
    out[45:50, :] = down[0:5]
    out[50:55, :] = sent_by(idx, same, other, UP_THREE)[0:5]
    out[55:60, :] = sent_by(idx, same, other, DOWN_THREE)[5:10]
    out[60:64, :] = jnp.zeros((4, LANES), jnp.float32)


def local_kernel(coef, p0, p1, p2, p3, local, gap, own, send, field, source):
    sub = lax.axis_index("sub")
    for d, piece in enumerate((p0, p1, p2, p3)):
        q = (sub + d) & 3
        for a in range(NV):
            field[q, a] = piece[a]
            source[q, a] = piece[NV + a]
    given = whole(field)
    own[...] = jnp.zeros(own.shape, jnp.float32)
    store_end_chunks(own, given, 0)
    values, rest = sweep(coef, scaled_source(coef, whole(source)), given, 16, 512)
    store_whole(local, values)
    store_whole(gap, rest)
    store_end_chunks(own, values, 10)
    send[...] = own[sub]


def plane_mean():
    cell, coarse = iota((512, LANES), 0), iota((512, LANES), 1)
    match = ((cell >> 5) == (coarse >> 3)) & (((cell & 15) >> 1) == (coarse & 7))
    return jnp.where(match, 0.25, 0.0)


def fine_kernel(
    coef, coef_mid, idx, e0, e1, e2, e3, own, local, gap, out, edges, total, mid, mid_gap, own_ends, send, found
):
    ordered(idx, (e0, e1, e2, e3), found)
    replies, before = [], None
    for kept, pair in zip(("all", "first", "last"), near_planes(idx, found, own)):
        below, above = (flipped(plane, code, 16) for plane, code in pair)
        before = (below, above) if before is None else before
        low = times(coef, FORWARD, listed_rows(below))
        high = times(coef, BACKWARD, listed_rows(above))
        if kept == "all":
            replies.append(response(coef, low, high, 32, 16, kept))
        else:
            replies.append(far_ends(coef, low, high, kept, 16, 512))
    above = plane_of(found, 20) + jnp.concatenate(replies[1], axis=0)
    below = plane_of(found, 25) + jnp.concatenate(replies[2], axis=0)
    below, above = flipped(below, idx[0, DOWN + 2], 16), flipped(above, idx[0, UP + 2], 16)
    low = times(coef, FORWARD, listed_rows(below - before[0]))
    high = times(coef, BACKWARD, listed_rows(above - before[1]))
    rest = [x + y for x, y in zip(whole(gap), replies[0][1])]
    first, second = next_sweep(coef, rest, low, high, 16, 512)
    values = [x + y + z for x, y, z in zip(whole(local), replies[0][0], second)]
    store_whole(out, values)
    rest = [x + (z - y) for x, y, z in zip(rest, first, second)]
    left = residual(coef, rest, (-below, -above), 16, 512)
    edges[...] = jnp.zeros((16, 512), jnp.float32)
    for a in range(NV):
        edges[a : a + 1, :] = left[a][:1]
        edges[8 + a : 9 + a, :] = left[a][31:]
    row = iota((32, 512), 0)
    inner = (row > 0) & (row < 31)
    total[...] = jnp.broadcast_to(squares([jnp.where(inner, x, 0.0) for x in left]), (8, LANES))
    pair = jnp.where((iota((16, 32), 1) >> 1) == iota((16, 32), 0), 0.5, 0.0)
    mean = dot(jnp.concatenate(left, axis=0), plane_mean())
    source_mid = [dot_left(pair, mean[32 * a : 32 * a + 32]) for a in range(NV)]
    reply, rest = sweep(coef_mid, scaled_source(coef_mid, source_mid), None, 8, LANES)
    twice = next_sweep(coef_mid, rest, None, None, 8, LANES)[1]
    twice = [x + y for x, y in zip(reply, twice)]
    own_ends[...] = jnp.zeros(own_ends.shape, jnp.float32)
    store_end_chunks(own_ends, values, 0)
    for a in range(NV):
        mid[a] = reply[a]
        mid_gap[a] = rest[a]
        lines = (reply[a][:1], reply[a][15:], twice[a][:1], twice[a][15:])
        for c, line in enumerate(lines):
            own_ends[c, 10 + a : 11 + a, :] = line
    send[...] = own_ends[idx[0, SUB]]


def mid_kernel(
    coef_fine, coef, idx, e0, e1, e2, e3, own, edges, total, mid, mid_gap, lanes, doubled, send, lanes_out, quarter, found
):
    ordered(idx, (e0, e1, e2, e3), found)
    pairs = list(near_planes(idx, found, own))
    below, above = (flipped(plane, code, 16) for plane, code in pairs[0])
    up_two, down_two = idx[0, UP_TWO + 2], idx[0, DOWN_TWO + 2]
    pairs.append(((plane_of(found, 40), up_two), (plane_of(found, 50), idx[0, UP_THREE + 2])))
    pairs.append(((plane_of(found, 55), idx[0, DOWN_THREE + 2]), (plane_of(found, 45), down_two)))

    low = times(coef_fine, BELOW, listed_rows(below), [edges[a : a + 1, :] for a in range(NV)])
    high = times(coef_fine, ABOVE, listed_rows(above), [edges[8 + a : 9 + a, :] for a in range(NV)])
    total_zero = total[:1] + squares(low) + squares(high)

    gap = jnp.zeros((3, 512), jnp.float32)
    stacked = jnp.concatenate([part for pair in pairs for plane, _ in pair for part in (plane, gap)], axis=0)
    mean = dot(stacked, plane_mean())
    replies = []
    for n, (kept, pair) in enumerate(zip(("all", "all", "all", "first", "last"), pairs)):
        planes = [
            flipped(0.5 * mean[8 * m : 8 * m + NV], code, 8)
            for m, (_, code) in zip((2 * n, 2 * n + 1), pair)
        ]
        low = times(coef_fine, BELOW, listed_rows(planes[0]))
        high = times(coef_fine, ABOVE, listed_rows(planes[1]))
        low, high = times(coef, CINV, low), times(coef, CINV, high)
        replies.append(response(coef, low, high, 16, 8, kept))
    (own_reply, own_gap), (up_reply, up_gap), (down_reply, down_gap) = replies[:3]

    def row_of(values, k):
        return jnp.concatenate([x[k : k + 1] for x in values], axis=0)

    def driven(gap, below, above):
        low = times(coef, FORWARD, listed_rows(below))
        return next_sweep(coef, gap, low, times(coef, BACKWARD, listed_rows(above)), 8, LANES)

    down, up = idx[0, DOWN + 2], idx[0, UP + 2]
    field = [mid[a] + own_reply[a] for a in range(NV)]
    below = flipped(found[1, 25:30, :] + row_of(down_reply, 15), down, 8)
    above = flipped(found[0, 20:25, :] + row_of(up_reply, 0), up, 8)
    above_up = flipped(found[0, 30:35, :] + jnp.concatenate(replies[3], axis=0), up_two, 8)
    below_down = flipped(found[1, 35:40, :] + jnp.concatenate(replies[4], axis=0), down_two, 8)
    rest = [mid_gap[a] + own_gap[a] for a in range(NV)]
    first, second = driven(rest, below, above)
    values = [x + y for x, y in zip(field, second)]
    rest = [x + (z - y) for x, y, z in zip(rest, first, second)]
    up_second = driven(up_gap, flipped(row_of(field, 15), up, 8), above_up)[1]
    down_second = driven(down_gap, below_down, flipped(row_of(field, 0), down, 8))[1]
    new_above = found[2, 20:25, :] + row_of(up_reply, 0) + row_of(up_second, 0)
    new_below = found[3, 25:30, :] + row_of(down_reply, 15) + row_of(down_second, 15)
    change = (flipped(new_below, down, 8) - below, flipped(new_above, up, 8) - above)
    left = residual(coef, rest, change, 8, LANES)
    pair = jnp.where((iota((8, 16), 1) >> 1) == iota((8, 16), 0), 0.5, 0.0)
    mean = jnp.concatenate([dot_left(pair, x) for x in left], axis=0)
    cell, place = iota((LANES, LANES), 0), iota((LANES, LANES), 1)
    match_i = (cell >> 4) == (place & 7)
    column = (cell & 7) >> 1
    own_plane = (iota((8, LANES), 1) >> 4) == iota((8, LANES), 0)
    for half in range(2):
        match = match_i & (column == 2 * half + ((place >> 3) & 1))
        spread = dot(mean, jnp.where(match, 0.25, 0.0))
        for a in range(NV):
            kept = jnp.where(own_plane, spread[8 * a : 8 * a + 8], 0.0)
            at = half * NV + a
            send[at : at + 1, :] = jnp.sum(kept, axis=0, keepdims=True)
    total_one = squares(left)
    lanes_out[...] = lanes[...]
    total_zero = total_zero + pltpu.roll(total_zero, 64, 1)
    total_one = total_one + pltpu.roll(total_one, 64, 1)
    send[TOTAL_ROW : TOTAL_ROW + 1, :] = jnp.where(iota((1, LANES), 1) < 64, total_zero, total_one)
    for a in range(NV):
        for k in range(16):
            line = values[a][k : k + 1]
            quarter[k // 4, a * 4 + k % 4 : a * 4 + k % 4 + 1, :] = line
            at = a * 8 + 2 * (k % 4)
            doubled[k // 4, at : at + 1, :] = line
            doubled[k // 4, at + 1 : at + 2, :] = line
    send[QUARTER_ROWS : QUARTER_ROWS + 20, :] = quarter[idx[0, SUB]]
    send[QUARTER_ROWS + 20 :, :] = jnp.zeros((1, LANES), jnp.float32)


def coarse_kernel(coef, idx, lanes, same, other, field, doubled, corrected, one, two, norms):
    groups = ((8, 8, LANES))
    lane3 = iota(groups, 2)
    side3 = iota(groups, 1)

    def sent(r):
        return jnp.concatenate(
            [ref[pl.ds(r, CHIPS, stride=SENT_ROWS), :] for ref in (same, other)], axis=0
        )

    square = (LANES, LANES)
    row, column = iota(square, 0), iota(square, 1)

    def block_at(x):
        return 2 * (x & 31) + (((x >> 5) & 1) ^ idx[0, CORE])

    alike = (row >> 6) == (column >> 6)
    beyond = jnp.broadcast_to(lanes[0:1, :], square)
    beyond_of_row = beyond.T
    at_row, at_column = block_at(row).astype(jnp.float32), block_at(column).astype(jnp.float32)
    from_down = jnp.where(alike & (beyond_of_row == at_column), 1.0, 0.0)
    from_up = jnp.where(alike & (at_row == beyond), 1.0, 0.0)
    code_up = jnp.broadcast_to(lanes[1:2, :], (8, LANES))
    code_down = dot(code_up, from_down)

    code_up = (code_up + 0.5).astype(jnp.int32)
    code_down = (code_down + 0.5).astype(jnp.int32)

    def flip_planes(x, code):
        side = iota((8, LANES), 0)
        out_planes = []
        for pair in x:
            turned = []
            for p in pair:
                q = pltpu.roll(p, 4, 0)
                q = jnp.where((side & 2) != 0, pltpu.roll(q, 2, 0), pltpu.roll(q, 6, 0))
                q = jnp.where((side & 1) != 0, pltpu.roll(q, 1, 0), pltpu.roll(q, 7, 0))
                turned.append(jnp.where((code & 1) == 1, q, p))
            swapped = [pltpu.roll(p, 64, 1) for p in turned[::-1]]
            out_planes.append(
                [jnp.where((code & 2) == 2, s, p) for s, p in zip(swapped, turned)]
            )
        return out_planes

    def mapped(planes, chosen, code):
        got = dot(planes, chosen)
        pairs = [
            [got[16 * a + 8 * p : 16 * a + 8 * p + 8] for p in range(2)] for a in range(NV)
        ]
        return flip_planes(pairs, code)

    source = []
    for a in range(NV):
        both = jnp.concatenate([sent(a), sent(NV + a)], axis=0)
        turned = both.T.reshape(8, 2, 8, LANES)
        source.append([turned[:, 0], turned[:, 1]])
    totals = sent(TOTAL_ROW)
    low_lane = iota(totals.shape, 1) < 64
    total_zero = jnp.where(low_lane, totals, 0.0)
    total_one = jnp.where(low_lane, 0.0, totals)
    def pairwise(terms, start):
        out_pairs = [[None, None] for _ in range(NV)]
        for p in range(2):
            got = [x[p] for x in start]
            for place_of, values in terms:
                got = times(coef, place_of, [x[p] for x in values], got)
            for a in range(NV):
                out_pairs[a][p] = got[a]
        return out_pairs

    def beside_coarse(values):
        low = [[jnp.where(side3 > 0, pltpu.roll(x, 1, 1), 0.0) for x in pair] for pair in values]
        high = [[jnp.where(side3 < 7, pltpu.roll(x, 7, 1), 0.0) for x in pair] for pair in values]
        left = [
            [jnp.where(lane3 >= 64, pltpu.roll(pair[1], 64, 2), 0.0), pair[0]] for pair in values
        ]
        right = [
            [pair[1], jnp.where(lane3 < 64, pltpu.roll(pair[0], 64, 2), 0.0)] for pair in values
        ]
        return [low, high, left, right]

    def combined(f, *fields):
        return [[f(*(x[a][p] for x in fields)) for p in range(2)] for a in range(NV)]

    def with_ends(values, coef_of, low_at, low, high_at, high):
        out_pairs = [[None, None] for _ in range(NV)]
        for p in range(2):
            under = times(coef_of, low_at, [x[p] for x in low])
            over = times(coef_of, high_at, [x[p] for x in high])
            for a in range(NV):
                x = values[a][p]
                out_pairs[a][p] = jnp.concatenate(
                    [x[:1] + under[a][None], x[1:7], x[7:] + over[a][None]], axis=0
                )
        return out_pairs

    def sides_coarse(place_of, values, start):
        return pairwise([(place_of + n, x) for n, x in enumerate(beside_coarse(values))], start)

    def carried(values, forward):
        place_of = FORWARD if forward else BACKWARD
        out_pairs = [[None, None] for _ in range(NV)]
        for p in range(2):
            before = None
            planes = [None] * 8
            for k in range(8) if forward else range(7, -1, -1):
                own = [x[p][k] for x in values]
                before = own if before is None else times(coef, place_of, before, own)
                planes[k] = before
            for a in range(NV):
                out_pairs[a][p] = jnp.stack([planes[k][a] for k in range(8)], axis=0)
        return out_pairs

    def edge(values, k):
        return jnp.concatenate([x[p][k] for x in values for p in range(2)], axis=0)

    def neighbours(values):
        below = mapped(edge(values, 7), from_down, code_down)
        above = mapped(edge(values, 0), from_up, code_up)
        return below, above

    empty = [[jnp.zeros(groups, jnp.float32)] * 2 for _ in range(NV)]
    first = carried(pairwise([(CINV, source)], empty), True)
    change = values = carried(sides_coarse(SIDE, first, first), False)
    rest = combined(jnp.subtract, values, first)
    for _ in range(3):
        below, above = neighbours(change)
        drive = sides_coarse(SIDE, rest, rest)
        first = carried(with_ends(drive, coef, FORWARD, below, BACKWARD, above), True)
        start = combined(jnp.subtract, first, drive)
        change = carried(sides_coarse(SIDE, first, start), False)
        values = combined(jnp.add, values, change)
        rest = combined(lambda x, y, z: x + (z - y), rest, first, change)

    below, above = neighbours(change)
    zero_plane = jnp.zeros((1, 8, LANES), jnp.float32)
    lifted = combined(lambda x: jnp.concatenate([zero_plane, x[:7]], axis=0), rest)
    left = sides_coarse(LATERAL, rest, pairwise([(BELOW, lifted)], empty))
    left = with_ends(left, coef, BELOW, below, ABOVE, above)
    total_two = None
    for pair in left:
        for x in pair:
            part = jnp.sum(x * x, axis=0)
            total_two = part if total_two is None else total_two + part

    lane = iota((8, LANES), 1)
    result = jnp.zeros((8, LANES), jnp.float32)
    sizes = (NV * 64 * 32 * 512, NV * 64 * 16 * 128, NV * 64 * 8 * 32)
    for level, total in enumerate((total_zero, total_one, total_two)):
        total = jnp.sum(jnp.sum(total, axis=0, keepdims=True), axis=1, keepdims=True)
        root = jnp.sqrt(jnp.broadcast_to(total, (8, LANES)) / float(sizes[level]))
        result = jnp.where(lane == level, root, result)
    norms[...] = result[:1, :3]

    which = iota((8, LANES), 0)
    wanted = jnp.where(
        which < 2,
        jnp.full((8, LANES), idx[0, POS_OWN], jnp.int32),
        jnp.where(
            which < 4,
            jnp.full((8, LANES), idx[0, POS_ONE], jnp.int32),
            jnp.full((8, LANES), idx[0, POS_TWO], jnp.int32),
        ),
    )
    chosen = jnp.where(lane == wanted + 64 * (which & 1), 1.0, 0.0)
    out = []
    for a in range(NV):
        laid = jnp.stack(values[a], axis=1).reshape(LANES, LANES)
        out.append(dot_nt(chosen, laid))

    s = idx[0, SUB]
    row = iota((2 * LANES, LANES), 0)
    cell = iota((2 * LANES, LANES), 1)
    half, inner_j, inner_i = row >> 7, (row >> 3) & 1, row & 7
    fits = (inner_i == (cell >> 4)) & (2 * half + inner_j == ((cell & 7) >> 1))
    to_mid = jnp.where(fits, 1.0, 0.0)
    fits = (inner_i == (cell >> 2)) & (2 * half + inner_j == (cell & 3)) & (cell < 32)
    to_cells = jnp.where(fits, 1.0, 0.0)

    def laid(which, count, shift):
        parts = []
        shape = (count, 2 * LANES)
        plane = (iota(shape, 1) >> 4) & 7
        wanted = 2 * s + (iota(shape, 0) >> shift)
        for a in range(NV):
            pair = jnp.concatenate(
                [out[a][2 * which : 2 * which + 1], out[a][2 * which + 1 : 2 * which + 2]], axis=1
            )
            parts.append(jnp.where(plane == wanted, jnp.broadcast_to(pair, shape), 0.0))
        return parts

    x_one = doubled[s] + dot(jnp.concatenate(laid(0, 8, 2), axis=0), to_mid)
    mid, fine = iota((LANES, 512), 0), iota((LANES, 512), 1)
    fits = ((fine >> 5) == (mid >> 3)) & (((fine & 15) >> 1) == (mid & 7))
    spread = dot(x_one, jnp.where(fits, 1.0, 0.0))
    for a in range(NV):
        corrected[a] = field[s, a] + spread[8 * a : 8 * a + 8]
    at = pl.ds(pl.multiple_of(idx[0, CHIP_ONE] * SENT_ROWS, 8), SENT_ROWS)
    held = jnp.where(jnp.full((SENT_ROWS, LANES), idx[0, REL_ONE], jnp.int32) == 0, same[at, :], other[at, :])
    held = held[QUARTER_ROWS : QUARTER_ROWS + 20]
    for a, part in enumerate(laid(1, 8, 1)):
        got = dot(part, to_mid)
        one[a] = held[4 * a : 4 * a + 4] + got[:4]
    for a, part in enumerate(laid(2, 8, 0)):
        two[a] = dot(part, to_cells)[:2, :32]


def gathered(payload):
    copies = jnp.broadcast_to(payload, (CHIPS, *payload.shape))
    same = lax.all_to_all(copies, CHIP, split_axis=0, concat_axis=0, tiled=True)
    other = lax.ppermute(same, "blk_2", [(0, 1), (1, 0)])
    return same, other


def around(piece):
    moves = [[((i + d) % 4, i) for i in range(4)] for d in range(1, 4)]
    return [piece] + [lax.ppermute(piece, "sub", move) for move in moves]


def shards(solution, right_side, couple, partner, orient, owner_one, owner_two):
    core = lax.axis_index("blk_2")

    pieces = around(jnp.concatenate([solution[:, 0], right_side[:, 0]], axis=0))

    idx, begin, *coef = pl.pallas_call(
        setup_kernel,
        out_shape=(jax.ShapeDtypeStruct((1, LANES), jnp.int32),)
        + tuple(jax.ShapeDtypeStruct((8, 256), jnp.float32) for _ in range(4)),
        in_specs=[SMEM] * 4 + [VMEM],
        out_specs=(VMEM,) * 5,
        scratch_shapes=[pltpu.VMEM((256, LANES), jnp.float32)],
    )(
        partner,
        orient,
        owner_one,
        owner_two,
        jnp.pad(couple.reshape(21, 25), ((0, LANES - 21), (0, LANES - 25))),
    )

    whole_shape = (4, NV, 8, 512)
    mid_shape = (NV, 16, LANES)

    def picked(sent, kernel, count):
        (rows,) = call(kernel, [(count, LANES)], [SMEM] + [VMEM] * 2)(idx, *gathered(sent))
        return rows

    local, gap, own, sent = call(
        local_kernel,
        [whole_shape, whole_shape, (4, 24, LANES), (24, LANES)],
        [SMEM] + [VMEM] * 4,
        [pltpu.VMEM(whole_shape, jnp.float32)] * 2,
    )(begin, *pieces)
    field, edges, total, mid, mid_gap, own, sent = call(
        fine_kernel,
        [whole_shape, (16, 512), (8, LANES), mid_shape, mid_shape, (4, 16, LANES), (16, LANES)],
        [SMEM] * 3 + [VMEM] * 7,
        [pltpu.VMEM((4, 32, LANES), jnp.float32)],
    )(coef[0], coef[1], idx, *around(picked(sent, pick_kernel, 32)), own, local, gap)
    rows = picked(sent, pick_mid_kernel, 64)
    rows, partner, orient = lax.optimization_barrier((rows, partner, orient))
    lanes = jnp.stack([partner, orient]).reshape(2, CHIPS, 2).transpose(0, 2, 1)
    lanes = jnp.where(core == 0, lanes, lanes[:, ::-1]).reshape(2, 64).astype(jnp.float32)
    lanes = jnp.concatenate([lanes, lanes], axis=1)
    doubled, sent, lanes = call(
        mid_kernel,
        [(4, 40, LANES), (SENT_ROWS, LANES), (2, LANES)],
        [SMEM] * 3 + [VMEM] * 10,
        [pltpu.VMEM((4, count, LANES), jnp.float32) for count in (20, 64)],
    )(coef[0], coef[1], idx, *around(rows), own, edges, total, mid, mid_gap, lanes)
    got = gathered(sent)
    corrected, one, two, norms = call(
        coarse_kernel,
        [(NV, 8, 512), (NV, 4, LANES), (NV, 2, 32), (1, 3)],
        [SMEM] * 2 + [VMEM] * 5,
    )(coef[2], idx, lanes, *[x.reshape(CHIPS * SENT_ROWS, LANES) for x in got], field, doubled)
    return (corrected[:, None], one[:, None], two[:, None], norms.reshape(3))


def solution(mesh):
    torus = Mesh(
        mesh.devices.reshape(4, 8, 2, mesh.shape["sub"]), ("blk_0", "blk_1", "blk_2", "sub")
    )
    split = P(None, BLK, "sub", None)
    return jax.shard_map(
        shards,
        mesh=torus,
        in_specs=(split, split, P(), P(), P(), P(), P()),
        out_specs=(split, split, split, P()),
        check_vma=False,
    )
```

```python
import jax
import jax.numpy as jnp
from jax import lax
from jax.experimental import pallas as pl
from jax.experimental.pallas import tpu as pltpu
from jax.sharding import Mesh
from jax.sharding import PartitionSpec as P

NV = 5
LANES = 128
CHIPS = 32
BLK = ("blk_0", "blk_1", "blk_2")
CHIP = ("blk_0", "blk_1")
PRECISE = lax.Precision.HIGHEST

POWERS, RAW, SUMS, TOPS, LONG = 1, 5, 7, 8, 9
PLACE_OF = (
    [(0, 0)]
    + [(1 + n, POWERS) for n in range(4)]
    + [(row, POWERS + n) for row in (5, 6) for n in range(4)]
    + [(1 + n, RAW) for n in range(6)]
    + [(n, group) for group in (SUMS, TOPS) for n in range(5)]
    + [(0, LONG)]
)
CINV, SIDE, FORWARD, BACKWARD, LATERAL, BELOW, ABOVE, SUM, TOP, LAST_POWER = 0, 1, 5, 9, 13, 17, 18, 19, 24, 29

SUB, CORE, POS_OWN, POS_ONE, POS_TWO, CHIP_ONE, REL_ONE = range(7)
DOWN, UP, DOWN_TWO, UP_TWO, DOWN_THREE, UP_THREE = 8, 11, 14, 17, 20, 23

TOTAL_ROW, QUARTER_ROWS, SENT_ROWS = 10, 11, 32

VMEM = pl.BlockSpec(memory_space=pltpu.VMEM)
SMEM = pl.BlockSpec(memory_space=pltpu.SMEM)


def call(kernel, out_shapes, in_specs, scratch=()):
    return pl.pallas_call(
        kernel,
        out_shape=tuple(jax.ShapeDtypeStruct(shape, jnp.float32) for shape in out_shapes),
        in_specs=in_specs,
        out_specs=tuple(VMEM for _ in out_shapes),
        scratch_shapes=list(scratch),
        compiler_params=pltpu.CompilerParams(vmem_limit_bytes=40 * 1024 * 1024),
    )


def iota(shape, dim):
    return lax.broadcasted_iota(jnp.int32, shape, dim)


def parts_of(x):
    high = x.astype(jnp.bfloat16)
    rest = x - high.astype(jnp.float32)
    middle = rest.astype(jnp.bfloat16)
    return high, middle, (rest - middle.astype(jnp.float32)).astype(jnp.bfloat16)


def contracted(a, b, dims):
    return lax.dot_general(a, b, (dims, ((), ())), preferred_element_type=jnp.float32)


def dot(values, exact):
    exact = exact.astype(jnp.bfloat16)
    high, middle, low = (contracted(x, exact, ((1,), (0,))) for x in parts_of(values))
    return high + (middle + low)


def dot_left(exact, values):
    exact = exact.astype(jnp.bfloat16)
    high, middle, low = (contracted(exact, x, ((1,), (0,))) for x in parts_of(values))
    return high + (middle + low)


def dot_nt(exact, values):
    exact = exact.astype(jnp.bfloat16)
    high, middle, low = (contracted(exact, x, ((1,), (1,))) for x in parts_of(values))
    return high + (middle + low)


def times(coef, place, values, start=None):
    out = list(start) if start is not None else [None] * NV
    row, group = PLACE_OF[place]
    for a in range(NV):
        for b in range(NV):
            term = coef[row, group * 25 + a * NV + b] * values[b]
            out[a] = term if out[a] is None else out[a] + term
    return out


def summed(coef, terms, start):
    width = start[0].shape[1]
    parts = []
    for at in range(0, width, LANES):
        out = [x[:, at : at + LANES] for x in start]
        for place, values in terms:
            out = times(coef, place, [x[:, at : at + LANES] for x in values], out)
        parts.append(out)
    if len(parts) == 1:
        return parts[0]
    return [jnp.concatenate([part[a] for part in parts], axis=1) for a in range(NV)]


def beside(values, columns, cells):
    shape = values[0].shape
    width = shape[1]
    cell = iota(shape, 1) & (cells - 1)
    column = cell & (columns - 1)
    cases = (
        (columns, cell >= columns),
        (width - columns, cell < cells - columns),
        (1, column != 0),
        (width - 1, column != columns - 1),
    )
    return [
        [jnp.where(mask, pltpu.roll(x, shift, 1), 0.0) for x in values] for shift, mask in cases
    ]


def moved_up(x, by):
    return jnp.where(iota(x.shape, 0) >= by, pltpu.roll(x, by, 0), 0.0)


def moved_down(x, by):
    count = x.shape[0]
    return jnp.where(iota(x.shape, 0) < count - by, pltpu.roll(x, count - by, 0), 0.0)


def tiles_of(values):
    return [[x[at : at + 8] for x in values] for at in range(0, values[0].shape[0], 8)]


def joined(tiles):
    return [jnp.concatenate([tile[a] for tile in tiles], axis=0) for a in range(NV)]


def recurrence(coef, values, forward):
    place = FORWARD if forward else BACKWARD
    move = moved_up if forward else moved_down
    for n in range(3):
        values = summed(coef, [(place + n, [move(x, 1 << n) for x in values])], values)
    tiles = tiles_of(values)
    count = len(tiles)
    for n in range(1, count):
        at, before = (n, n - 1) if forward else (count - 1 - n, count - n)
        tiles[at] = summed(coef, [(place + 3, tiles[before])], tiles[at])
    return joined(tiles)


def response(coef, low, high, count, columns, kept):
    width = low[0].shape[1]
    row = iota((8, width), 0)
    tile = [jnp.where(row == 0, jnp.broadcast_to(x, (8, width)), 0.0) for x in low]
    for n in range(3):
        tile = summed(coef, [(FORWARD + n, [moved_up(x, 1 << n) for x in tile])], tile)
    tiles = [tile]
    for _ in range(1, count // 8):
        tiles.append(summed(coef, [(FORWARD + 3, tiles[-1])], zeros_like(tile)))
    tiles[-1] = [
        x + jnp.where(row == 7, jnp.broadcast_to(h, (8, width)), 0.0)
        for x, h in zip(tiles[-1], high)
    ]
    if kept == "last":
        end = sides(coef, SIDE, tiles[-1], columns, width, tiles[-1])
        return [x[7:] for x in end]
    first = joined(tiles)
    source = sides(coef, SIDE, first, columns, width, first)
    if kept == "all":
        second = recurrence(coef, source, False)
        return second, [z - y for z, y in zip(second, first)]
    tiles = tiles_of(source)
    end = tiles[-1]
    for tile in tiles[-2::-1]:
        end = summed(coef, [(BACKWARD + 3, end)], tile)
    for n in range(3):
        end = summed(coef, [(BACKWARD + n, [moved_down(x, 1 << n) for x in end])], end)
    return [x[:1] for x in end]


def at_ends(low, high, count):
    out = []
    for a, b in zip(low, high):
        shape = (count, a.shape[1])
        row = iota(shape, 0)
        out.append(
            jnp.where(
                row == 0,
                jnp.broadcast_to(a, shape),
                jnp.where(row == count - 1, jnp.broadcast_to(b, shape), 0.0),
            )
        )
    return out


def sides(coef, place, values, columns, cells, start):
    return summed(coef, [(place + n, x) for n, x in enumerate(beside(values, columns, cells))], start)


def sweep(coef, scaled, values, columns, cells):
    source = scaled
    if values is not None:
        source = summed(coef, [(BACKWARD, [moved_down(x, 1) for x in values])], scaled)
        source = sides(coef, SIDE, values, columns, cells, source)
    first = recurrence(coef, source, True)
    start = first
    if values is not None:
        start = [g + (y - s) for g, y, s in zip(scaled, first, source)]
    second = recurrence(coef, sides(coef, SIDE, first, columns, cells, start), False)
    return second, [z - y for z, y in zip(second, first)]


def next_sweep(coef, gap, low, high, columns, cells):
    drive = sides(coef, SIDE, gap, columns, cells, gap)
    begin = drive
    if low is not None:
        begin = [x + e for x, e in zip(drive, at_ends(low, high, gap[0].shape[0]))]
    first = recurrence(coef, begin, True)
    start = [x - q for x, q in zip(first, drive)]
    return first, recurrence(coef, sides(coef, SIDE, first, columns, cells, start), False)


def zeros_like(values):
    return [jnp.zeros_like(x) for x in values]


def scaled_source(coef, source):
    return summed(coef, [(CINV, source)], zeros_like(source))


def residual(coef, gap, ends, columns, cells):
    low = times(coef, BELOW, listed_rows(ends[0]))
    high = times(coef, ABOVE, listed_rows(ends[1]))
    start = summed(coef, [(BELOW, [moved_up(x, 1) for x in gap])], at_ends(low, high, gap[0].shape[0]))
    return sides(coef, LATERAL, gap, columns, cells, start)


def flipped(x, code, columns):
    width = x.shape[1]
    mask = (code & 1) * (width - columns) + (code >> 1) * (columns - 1)
    square = (LANES, LANES)
    source = iota(square, 1) ^ jnp.full(square, mask & (LANES - 1), jnp.int32)
    chosen = jnp.where(source == iota(square, 0), 1.0, 0.0)
    chunks = [x[:, at : at + LANES] for at in range(0, width, LANES)]
    if len(chunks) == 1:
        return dot(x, chosen)
    turned = jnp.full(chunks[0].shape, code & 1, jnp.int32) == 1
    chunks = [jnp.where(turned, other, own) for own, other in zip(chunks, chunks[::-1])]
    return jnp.concatenate([dot(chunk, chosen) for chunk in chunks], axis=1)


def block_of(same, other, chip, rel):
    a, b = same[chip], other[chip]
    return jnp.where(jnp.full(a.shape, rel, jnp.int32) == 0, a, b)


def sent_by(idx, same, other, place):
    return block_of(same, other, idx[0, place], idx[0, place + 1])


def listed_rows(x):
    return [x[a : a + 1] for a in range(NV)]


def plane_of(ref, row):
    return jnp.concatenate([ref[c, row : row + NV, :] for c in range(4)], axis=1)


def ordered(idx, pieces, ref):
    for d, piece in enumerate(pieces):
        ref[(idx[0, SUB] + d) & 3] = piece[...]


def near_planes(idx, found, own):
    down, up, down_two, up_two = (idx[0, place + 2] for place in (DOWN, UP, DOWN_TWO, UP_TWO))
    first, last = plane_of(own, 0), plane_of(own, NV)
    return (
        ((plane_of(found, 5), down), (plane_of(found, 0), up)),
        ((last, up), (plane_of(found, 10), up_two)),
        ((plane_of(found, 15), down_two), (first, down)),
    )


def store_end_chunks(out, values, at):
    count = values[0].shape[0]
    for c in range(4):
        for a in range(NV):
            line = values[a][:, c * LANES : (c + 1) * LANES]
            out[c, at + a : at + a + 1, :] = line[:1]
            out[c, at + NV + a : at + NV + a + 1, :] = line[count - 1 :]


def whole(ref):
    return [jnp.concatenate([ref[q, a] for q in range(4)], axis=0) for a in range(NV)]


def store_whole(ref, values):
    for a in range(NV):
        for q in range(4):
            ref[q, a] = values[a][8 * q : 8 * q + 8]


def squares(values):
    total = None
    for x in values:
        for at in range(0, x.shape[1], LANES):
            part = x[:, at : at + LANES] * x[:, at : at + LANES]
            total = part if total is None else total + part
    return jnp.sum(total, axis=0, keepdims=True)


def coefficients(couple, held, outs):
    square = (LANES, LANES)
    lane = iota(square, 1)
    base = jnp.where(lane < 7, 0, jnp.where(lane < 14, 7, 14))
    row = iota(square, 0)

    def entries(x, group=0):
        return [x[group * 25 + e : group * 25 + e + 1] for e in range(25)]

    def product(x, y):
        out = []
        for a in range(NV):
            for b in range(NV):
                total = x[a * NV] * y[b]
                for k in range(1, NV):
                    total = total + x[a * NV + k] * y[k * NV + b]
                out.append(total)
        return out

    def keep(group, values):
        for e, x in enumerate(values):
            held[group * 25 + e : group * 25 + e + 1, :] = x

    given = couple[...].T
    raw = entries(given)
    center = entries(dot(given, jnp.where(row == base, 1.0, 0.0)))
    identity = [jnp.full((1, LANES), 1.0 if e % 6 == 0 else 0.0, jnp.float32) for e in range(25)]

    def twice_less(x):
        return [2.0 * i - y for i, y in zip(identity, x)]

    inverse = twice_less(center)
    for _ in range(5):
        inverse = product(inverse, twice_less(product(center, inverse)))
    held[...] = jnp.zeros((256, LANES), jnp.float32)
    keep(0, inverse)
    power = scaled = product(inverse, raw)
    for n in range(4):
        keep(POWERS + n, power)
        power = product(power, power)
    keep(RAW, raw)
    keep(6, power)
    powers = held[...]
    groups = (1, 2, 3, 4, 6)
    forward = dot(powers, jnp.where(row == base + 5, 1.0, 0.0))
    backward = dot(powers, jnp.where(row == base + 6, 1.0, 0.0))
    first = (lane == base)[:1]
    sums = tops = [jnp.where(first, i, x) for i, x in zip(identity, scaled)]
    long = identity
    for group in groups:
        f, b = entries(forward, group), entries(backward, group)
        sums = [x + y for x, y in zip(sums, product(product(b, sums), f))]
        tops = product(b, tops)
        long = product(long, f)
    keep(SUMS, sums)
    keep(TOPS, tops)
    keep(LONG, long)
    turned = held[...].T
    for level, out in enumerate(outs):
        out[...] = turned[7 * level : 7 * level + 8]


def far_ends(coef, low, high, kept, columns, cells):
    if kept == "last":
        end = times(coef, LAST_POWER, low, high)
        return sides(coef, SIDE, end, columns, cells, end)
    out = sides(coef, SUM + 1, low, columns, cells, times(coef, SUM, low))
    return sides(coef, TOP + 1, high, columns, cells, times(coef, TOP, high, out))


def setup_kernel(partner, orient, owner_one, owner_two, couple, out, begin, fine, mid, coarse, held):
    coefficients(couple, held, (fine, mid, coarse))
    begin[...] = fine[...]
    device = lax.axis_index(BLK)
    core = lax.axis_index("blk_2")
    idx = {SUB: lax.axis_index("sub"), CORE: core}

    def find(j, found):
        down, one, two = found
        return (
            jnp.where(partner[j] == device, j, down),
            jnp.where(owner_one[j] == device, j, one),
            jnp.where(owner_two[j] == device, j, two),
        )

    zero = jnp.int32(0)
    down, one, two = lax.fori_loop(0, 64, find, (zero, zero, zero), unroll=8)

    def below_of(block):
        return lax.fori_loop(
            0, 64, lambda j, found: jnp.where(partner[j] == block, j, found), zero, unroll=8
        )

    down_two = below_of(down)
    down_three = below_of(down_two)
    up = partner[device]
    up_two = partner[up]
    up_three = partner[up_two]
    for place, block in ((POS_OWN, device), (POS_ONE, one), (POS_TWO, two)):
        idx[place] = ((block & 1) ^ core) * CHIPS + (block >> 1)
    idx[CHIP_ONE] = one >> 1
    idx[REL_ONE] = (one & 1) ^ core
    places = ((DOWN, down, down), (UP, up, device), (DOWN_TWO, down_two, down_two), (UP_TWO, up_two, up))
    places += ((DOWN_THREE, down_three, down_three), (UP_THREE, up_three, up_two))
    for place, block, crossing in places:
        idx[place] = block >> 1
        idx[place + 1] = (block & 1) ^ core
        idx[place + 2] = orient[crossing]
    lane = iota((1, LANES), 1)
    listed = jnp.zeros((1, LANES), jnp.int32)
    for place, value in idx.items():
        listed = jnp.where(lane == place, jnp.full((1, LANES), value, jnp.int32), listed)
    out[...] = listed


def pick_kernel(idx, same, other, out):
    up, down = sent_by(idx, same, other, UP), sent_by(idx, same, other, DOWN)
    out[0:5, :] = up[0:5]
    out[5:10, :] = down[5:10]
    out[10:15, :] = sent_by(idx, same, other, UP_TWO)[0:5]
    out[15:20, :] = sent_by(idx, same, other, DOWN_TWO)[5:10]
    out[20:25, :] = up[10:15]
    out[25:30, :] = down[15:20]
    out[30:32, :] = jnp.zeros((2, LANES), jnp.float32)


def pick_mid_kernel(idx, same, other, out):
    up, down = sent_by(idx, same, other, UP), sent_by(idx, same, other, DOWN)
    up_two, down_two = sent_by(idx, same, other, UP_TWO), sent_by(idx, same, other, DOWN_TWO)
    out[0:5, :] = up[0:5]
    out[5:10, :] = down[5:10]
    out[10:15, :] = up_two[0:5]
    out[15:20, :] = down_two[5:10]
    for n, block in enumerate((up, down, up_two, down_two)):
        out[20 + 5 * n : 25 + 5 * n, :] = block[10:15]
    out[40:45, :] = up[5:10]
    out[45:50, :] = down[0:5]
    out[50:55, :] = sent_by(idx, same, other, UP_THREE)[0:5]
    out[55:60, :] = sent_by(idx, same, other, DOWN_THREE)[5:10]
    out[60:64, :] = jnp.zeros((4, LANES), jnp.float32)


def local_kernel(coef, p0, p1, p2, p3, local, gap, own, send, field, source):
    sub = lax.axis_index("sub")
    for d, piece in enumerate((p0, p1, p2, p3)):
        q = (sub + d) & 3
        for a in range(NV):
            field[q, a] = piece[a]
            source[q, a] = piece[NV + a]
    given = whole(field)
    own[...] = jnp.zeros(own.shape, jnp.float32)
    store_end_chunks(own, given, 0)
    values, rest = sweep(coef, scaled_source(coef, whole(source)), given, 16, 512)
    store_whole(local, values)
    store_whole(gap, rest)
    store_end_chunks(own, values, 10)
    send[...] = own[sub]


def plane_mean():
    cell, coarse = iota((512, LANES), 0), iota((512, LANES), 1)
    match = ((cell >> 5) == (coarse >> 3)) & (((cell & 15) >> 1) == (coarse & 7))
    return jnp.where(match, 0.25, 0.0)


def fine_kernel(
    coef, coef_mid, idx, e0, e1, e2, e3, own, local, gap, out, edges, total, mid, mid_gap, own_ends, send, found
):
    ordered(idx, (e0, e1, e2, e3), found)
    replies, before = [], None
    for kept, pair in zip(("all", "first", "last"), near_planes(idx, found, own)):
        below, above = (flipped(plane, code, 16) for plane, code in pair)
        before = (below, above) if before is None else before
        low = times(coef, FORWARD, listed_rows(below))
        high = times(coef, BACKWARD, listed_rows(above))
        if kept == "all":
            replies.append(response(coef, low, high, 32, 16, kept))
        else:
            replies.append(far_ends(coef, low, high, kept, 16, 512))
    above = plane_of(found, 20) + jnp.concatenate(replies[1], axis=0)
    below = plane_of(found, 25) + jnp.concatenate(replies[2], axis=0)
    below, above = flipped(below, idx[0, DOWN + 2], 16), flipped(above, idx[0, UP + 2], 16)
    low = times(coef, FORWARD, listed_rows(below - before[0]))
    high = times(coef, BACKWARD, listed_rows(above - before[1]))
    rest = [x + y for x, y in zip(whole(gap), replies[0][1])]
    first, second = next_sweep(coef, rest, low, high, 16, 512)
    values = [x + y + z for x, y, z in zip(whole(local), replies[0][0], second)]
    store_whole(out, values)
    rest = [x + (z - y) for x, y, z in zip(rest, first, second)]
    left = residual(coef, rest, (-below, -above), 16, 512)
    edges[...] = jnp.zeros((16, 512), jnp.float32)
    for a in range(NV):
        edges[a : a + 1, :] = left[a][:1]
        edges[8 + a : 9 + a, :] = left[a][31:]
    row = iota((32, 512), 0)
    inner = (row > 0) & (row < 31)
    total[...] = jnp.broadcast_to(squares([jnp.where(inner, x, 0.0) for x in left]), (8, LANES))
    pair = jnp.where((iota((16, 32), 1) >> 1) == iota((16, 32), 0), 0.5, 0.0)
    mean = dot(jnp.concatenate(left, axis=0), plane_mean())
    source_mid = [dot_left(pair, mean[32 * a : 32 * a + 32]) for a in range(NV)]
    reply, rest = sweep(coef_mid, scaled_source(coef_mid, source_mid), None, 8, LANES)
    twice = next_sweep(coef_mid, rest, None, None, 8, LANES)[1]
    twice = [x + y for x, y in zip(reply, twice)]
    own_ends[...] = jnp.zeros(own_ends.shape, jnp.float32)
    store_end_chunks(own_ends, values, 0)
    for a in range(NV):
        mid[a] = reply[a]
        mid_gap[a] = rest[a]
        lines = (reply[a][:1], reply[a][15:], twice[a][:1], twice[a][15:])
        for c, line in enumerate(lines):
            own_ends[c, 10 + a : 11 + a, :] = line
    send[...] = own_ends[idx[0, SUB]]


def mid_kernel(
    coef_fine, coef, idx, e0, e1, e2, e3, own, edges, total, mid, mid_gap, lanes, doubled, send, lanes_out, quarter, found
):
    ordered(idx, (e0, e1, e2, e3), found)
    pairs = list(near_planes(idx, found, own))
    below, above = (flipped(plane, code, 16) for plane, code in pairs[0])
    up_two, down_two = idx[0, UP_TWO + 2], idx[0, DOWN_TWO + 2]
    pairs.append(((plane_of(found, 40), up_two), (plane_of(found, 50), idx[0, UP_THREE + 2])))
    pairs.append(((plane_of(found, 55), idx[0, DOWN_THREE + 2]), (plane_of(found, 45), down_two)))

    low = times(coef_fine, BELOW, listed_rows(below), [edges[a : a + 1, :] for a in range(NV)])
    high = times(coef_fine, ABOVE, listed_rows(above), [edges[8 + a : 9 + a, :] for a in range(NV)])
    total_zero = total[:1] + squares(low) + squares(high)

    gap = jnp.zeros((3, 512), jnp.float32)
    stacked = jnp.concatenate([part for pair in pairs for plane, _ in pair for part in (plane, gap)], axis=0)
    mean = dot(stacked, plane_mean())
    replies = []
    for n, (kept, pair) in enumerate(zip(("all", "all", "all", "first", "last"), pairs)):
        planes = [
            flipped(0.5 * mean[8 * m : 8 * m + NV], code, 8)
            for m, (_, code) in zip((2 * n, 2 * n + 1), pair)
        ]
        low = times(coef_fine, BELOW, listed_rows(planes[0]))
        high = times(coef_fine, ABOVE, listed_rows(planes[1]))
        low, high = times(coef, CINV, low), times(coef, CINV, high)
        replies.append(response(coef, low, high, 16, 8, kept))
    (own_reply, own_gap), (up_reply, up_gap), (down_reply, down_gap) = replies[:3]

    def row_of(values, k):
        return jnp.concatenate([x[k : k + 1] for x in values], axis=0)

    def driven(gap, below, above):
        low = times(coef, FORWARD, listed_rows(below))
        return next_sweep(coef, gap, low, times(coef, BACKWARD, listed_rows(above)), 8, LANES)

    down, up = idx[0, DOWN + 2], idx[0, UP + 2]
    field = [mid[a] + own_reply[a] for a in range(NV)]
    below = flipped(found[1, 25:30, :] + row_of(down_reply, 15), down, 8)
    above = flipped(found[0, 20:25, :] + row_of(up_reply, 0), up, 8)
    above_up = flipped(found[0, 30:35, :] + jnp.concatenate(replies[3], axis=0), up_two, 8)
    below_down = flipped(found[1, 35:40, :] + jnp.concatenate(replies[4], axis=0), down_two, 8)
    rest = [mid_gap[a] + own_gap[a] for a in range(NV)]
    first, second = driven(rest, below, above)
    values = [x + y for x, y in zip(field, second)]
    rest = [x + (z - y) for x, y, z in zip(rest, first, second)]
    up_second = driven(up_gap, flipped(row_of(field, 15), up, 8), above_up)[1]
    down_second = driven(down_gap, below_down, flipped(row_of(field, 0), down, 8))[1]
    new_above = found[2, 20:25, :] + row_of(up_reply, 0) + row_of(up_second, 0)
    new_below = found[3, 25:30, :] + row_of(down_reply, 15) + row_of(down_second, 15)
    change = (flipped(new_below, down, 8) - below, flipped(new_above, up, 8) - above)
    left = residual(coef, rest, change, 8, LANES)
    pair = jnp.where((iota((8, 16), 1) >> 1) == iota((8, 16), 0), 0.5, 0.0)
    mean = jnp.concatenate([dot_left(pair, x) for x in left], axis=0)
    cell, place = iota((LANES, LANES), 0), iota((LANES, LANES), 1)
    match_i = (cell >> 4) == (place & 7)
    column = (cell & 7) >> 1
    own_plane = (iota((8, LANES), 1) >> 4) == iota((8, LANES), 0)
    for half in range(2):
        match = match_i & (column == 2 * half + ((place >> 3) & 1))
        spread = dot(mean, jnp.where(match, 0.25, 0.0))
        for a in range(NV):
            kept = jnp.where(own_plane, spread[8 * a : 8 * a + 8], 0.0)
            at = half * NV + a
            send[at : at + 1, :] = jnp.sum(kept, axis=0, keepdims=True)
    total_one = squares(left)
    lanes_out[...] = lanes[...]
    total_zero = total_zero + pltpu.roll(total_zero, 64, 1)
    total_one = total_one + pltpu.roll(total_one, 64, 1)
    send[TOTAL_ROW : TOTAL_ROW + 1, :] = jnp.where(iota((1, LANES), 1) < 64, total_zero, total_one)
    for a in range(NV):
        for k in range(16):
            line = values[a][k : k + 1]
            quarter[k // 4, a * 4 + k % 4 : a * 4 + k % 4 + 1, :] = line
            at = a * 8 + 2 * (k % 4)
            doubled[k // 4, at : at + 1, :] = line
            doubled[k // 4, at + 1 : at + 2, :] = line
    send[QUARTER_ROWS : QUARTER_ROWS + 20, :] = quarter[idx[0, SUB]]
    send[QUARTER_ROWS + 20 :, :] = jnp.zeros((1, LANES), jnp.float32)


def coarse_kernel(coef, idx, lanes, same, other, field, doubled, corrected, one, two, norms):
    groups = ((8, 8, LANES))
    lane3 = iota(groups, 2)
    side3 = iota(groups, 1)

    def sent(r):
        return jnp.concatenate(
            [ref[pl.ds(r, CHIPS, stride=SENT_ROWS), :] for ref in (same, other)], axis=0
        )

    square = (LANES, LANES)
    row, column = iota(square, 0), iota(square, 1)

    def block_at(x):
        return 2 * (x & 31) + (((x >> 5) & 1) ^ idx[0, CORE])

    alike = (row >> 6) == (column >> 6)
    beyond = jnp.broadcast_to(lanes[0:1, :], square)
    beyond_of_row = beyond.T
    at_row, at_column = block_at(row).astype(jnp.float32), block_at(column).astype(jnp.float32)
    from_down = jnp.where(alike & (beyond_of_row == at_column), 1.0, 0.0)
    from_up = jnp.where(alike & (at_row == beyond), 1.0, 0.0)
    code_up = jnp.broadcast_to(lanes[1:2, :], (8, LANES))
    code_down = dot(code_up, from_down)

    code_up = (code_up + 0.5).astype(jnp.int32)
    code_down = (code_down + 0.5).astype(jnp.int32)

    def flip_planes(x, code):
        side = iota((8, LANES), 0)
        out_planes = []
        for pair in x:
            turned = []
            for p in pair:
                q = pltpu.roll(p, 4, 0)
                q = jnp.where((side & 2) != 0, pltpu.roll(q, 2, 0), pltpu.roll(q, 6, 0))
                q = jnp.where((side & 1) != 0, pltpu.roll(q, 1, 0), pltpu.roll(q, 7, 0))
                turned.append(jnp.where((code & 1) == 1, q, p))
            swapped = [pltpu.roll(p, 64, 1) for p in turned[::-1]]
            out_planes.append(
                [jnp.where((code & 2) == 2, s, p) for s, p in zip(swapped, turned)]
            )
        return out_planes

    def mapped(planes, chosen, code):
        got = dot(planes, chosen)
        pairs = [
            [got[16 * a + 8 * p : 16 * a + 8 * p + 8] for p in range(2)] for a in range(NV)
        ]
        return flip_planes(pairs, code)

    source = []
    for a in range(NV):
        both = jnp.concatenate([sent(a), sent(NV + a)], axis=0)
        turned = both.T.reshape(8, 2, 8, LANES)
        source.append([turned[:, 0], turned[:, 1]])
    totals = sent(TOTAL_ROW)
    low_lane = iota(totals.shape, 1) < 64
    total_zero = jnp.where(low_lane, totals, 0.0)
    total_one = jnp.where(low_lane, 0.0, totals)
    def pairwise(terms, start):
        out_pairs = [[None, None] for _ in range(NV)]
        for p in range(2):
            got = [x[p] for x in start]
            for place_of, values in terms:
                got = times(coef, place_of, [x[p] for x in values], got)
            for a in range(NV):
                out_pairs[a][p] = got[a]
        return out_pairs

    def beside_coarse(values):
        low = [[jnp.where(side3 > 0, pltpu.roll(x, 1, 1), 0.0) for x in pair] for pair in values]
        high = [[jnp.where(side3 < 7, pltpu.roll(x, 7, 1), 0.0) for x in pair] for pair in values]
        left = [
            [jnp.where(lane3 >= 64, pltpu.roll(pair[1], 64, 2), 0.0), pair[0]] for pair in values
        ]
        right = [
            [pair[1], jnp.where(lane3 < 64, pltpu.roll(pair[0], 64, 2), 0.0)] for pair in values
        ]
        return [low, high, left, right]

    def combined(f, *fields):
        return [[f(*(x[a][p] for x in fields)) for p in range(2)] for a in range(NV)]

    def with_ends(values, coef_of, low_at, low, high_at, high):
        out_pairs = [[None, None] for _ in range(NV)]
        for p in range(2):
            under = times(coef_of, low_at, [x[p] for x in low])
            over = times(coef_of, high_at, [x[p] for x in high])
            for a in range(NV):
                x = values[a][p]
                out_pairs[a][p] = jnp.concatenate(
                    [x[:1] + under[a][None], x[1:7], x[7:] + over[a][None]], axis=0
                )
        return out_pairs

    def sides_coarse(place_of, values, start):
        return pairwise([(place_of + n, x) for n, x in enumerate(beside_coarse(values))], start)

    def carried(values, forward):
        place_of = FORWARD if forward else BACKWARD
        out_pairs = [[None, None] for _ in range(NV)]
        for p in range(2):
            before = None
            planes = [None] * 8
            for k in range(8) if forward else range(7, -1, -1):
                own = [x[p][k] for x in values]
                before = own if before is None else times(coef, place_of, before, own)
                planes[k] = before
            for a in range(NV):
                out_pairs[a][p] = jnp.stack([planes[k][a] for k in range(8)], axis=0)
        return out_pairs

    def edge(values, k):
        return jnp.concatenate([x[p][k] for x in values for p in range(2)], axis=0)

    def neighbours(values):
        below = mapped(edge(values, 7), from_down, code_down)
        above = mapped(edge(values, 0), from_up, code_up)
        return below, above

    empty = [[jnp.zeros(groups, jnp.float32)] * 2 for _ in range(NV)]
    first = carried(pairwise([(CINV, source)], empty), True)
    change = values = carried(sides_coarse(SIDE, first, first), False)
    rest = combined(jnp.subtract, values, first)
    for _ in range(3):
        below, above = neighbours(change)
        drive = sides_coarse(SIDE, rest, rest)
        first = carried(with_ends(drive, coef, FORWARD, below, BACKWARD, above), True)
        start = combined(jnp.subtract, first, drive)
        change = carried(sides_coarse(SIDE, first, start), False)
        values = combined(jnp.add, values, change)
        rest = combined(lambda x, y, z: x + (z - y), rest, first, change)

    below, above = neighbours(change)
    zero_plane = jnp.zeros((1, 8, LANES), jnp.float32)
    lifted = combined(lambda x: jnp.concatenate([zero_plane, x[:7]], axis=0), rest)
    left = sides_coarse(LATERAL, rest, pairwise([(BELOW, lifted)], empty))
    left = with_ends(left, coef, BELOW, below, ABOVE, above)
    total_two = None
    for pair in left:
        for x in pair:
            part = jnp.sum(x * x, axis=0)
            total_two = part if total_two is None else total_two + part

    lane = iota((8, LANES), 1)
    result = jnp.zeros((8, LANES), jnp.float32)
    sizes = (NV * 64 * 32 * 512, NV * 64 * 16 * 128, NV * 64 * 8 * 32)
    for level, total in enumerate((total_zero, total_one, total_two)):
        total = jnp.sum(jnp.sum(total, axis=0, keepdims=True), axis=1, keepdims=True)
        root = jnp.sqrt(jnp.broadcast_to(total, (8, LANES)) / float(sizes[level]))
        result = jnp.where(lane == level, root, result)
    norms[...] = result[:1, :3]

    which = iota((8, LANES), 0)
    wanted = jnp.where(
        which < 2,
        jnp.full((8, LANES), idx[0, POS_OWN], jnp.int32),
        jnp.where(
            which < 4,
            jnp.full((8, LANES), idx[0, POS_ONE], jnp.int32),
            jnp.full((8, LANES), idx[0, POS_TWO], jnp.int32),
        ),
    )
    chosen = jnp.where(lane == wanted + 64 * (which & 1), 1.0, 0.0)
    out = []
    for a in range(NV):
        laid = jnp.stack(values[a], axis=1).reshape(LANES, LANES)
        out.append(dot_nt(chosen, laid))

    s = idx[0, SUB]
    row = iota((2 * LANES, LANES), 0)
    cell = iota((2 * LANES, LANES), 1)
    half, inner_j, inner_i = row >> 7, (row >> 3) & 1, row & 7
    fits = (inner_i == (cell >> 4)) & (2 * half + inner_j == ((cell & 7) >> 1))
    to_mid = jnp.where(fits, 1.0, 0.0)
    fits = (inner_i == (cell >> 2)) & (2 * half + inner_j == (cell & 3)) & (cell < 32)
    to_cells = jnp.where(fits, 1.0, 0.0)

    def laid(which, count, shift):
        parts = []
        shape = (count, 2 * LANES)
        plane = (iota(shape, 1) >> 4) & 7
        wanted = 2 * s + (iota(shape, 0) >> shift)
        for a in range(NV):
            pair = jnp.concatenate(
                [out[a][2 * which : 2 * which + 1], out[a][2 * which + 1 : 2 * which + 2]], axis=1
            )
            parts.append(jnp.where(plane == wanted, jnp.broadcast_to(pair, shape), 0.0))
        return parts

    x_one = doubled[s] + dot(jnp.concatenate(laid(0, 8, 2), axis=0), to_mid)
    mid, fine = iota((LANES, 512), 0), iota((LANES, 512), 1)
    fits = ((fine >> 5) == (mid >> 3)) & (((fine & 15) >> 1) == (mid & 7))
    spread = dot(x_one, jnp.where(fits, 1.0, 0.0))
    for a in range(NV):
        corrected[a] = field[s, a] + spread[8 * a : 8 * a + 8]
    at = pl.ds(pl.multiple_of(idx[0, CHIP_ONE] * SENT_ROWS, 8), SENT_ROWS)
    held = jnp.where(jnp.full((SENT_ROWS, LANES), idx[0, REL_ONE], jnp.int32) == 0, same[at, :], other[at, :])
    held = held[QUARTER_ROWS : QUARTER_ROWS + 20]
    for a, part in enumerate(laid(1, 8, 1)):
        got = dot(part, to_mid)
        one[a] = held[4 * a : 4 * a + 4] + got[:4]
    for a, part in enumerate(laid(2, 8, 0)):
        two[a] = dot(part, to_cells)[:2, :32]


def gathered(payload):
    copies = jnp.broadcast_to(payload, (CHIPS, *payload.shape))
    same = lax.all_to_all(copies, CHIP, split_axis=0, concat_axis=0, tiled=True)
    other = lax.ppermute(same, "blk_2", [(0, 1), (1, 0)])
    return same, other


def around(piece):
    moves = [[((i + d) % 4, i) for i in range(4)] for d in range(1, 4)]
    return [piece] + [lax.ppermute(piece, "sub", move) for move in moves]


def shards(solution, right_side, couple, partner, orient, owner_one, owner_two):
    core = lax.axis_index("blk_2")

    pieces = around(jnp.concatenate([solution[:, 0], right_side[:, 0]], axis=0))

    idx, begin, *coef = pl.pallas_call(
        setup_kernel,
        out_shape=(jax.ShapeDtypeStruct((1, LANES), jnp.int32),)
        + tuple(jax.ShapeDtypeStruct((8, 256), jnp.float32) for _ in range(4)),
        in_specs=[SMEM] * 4 + [VMEM],
        out_specs=(VMEM,) * 5,
        scratch_shapes=[pltpu.VMEM((256, LANES), jnp.float32)],
    )(
        partner,
        orient,
        owner_one,
        owner_two,
        jnp.pad(couple.reshape(21, 25), ((0, LANES - 21), (0, LANES - 25))),
    )

    whole_shape = (4, NV, 8, 512)
    mid_shape = (NV, 16, LANES)

    def picked(sent, kernel, count):
        (rows,) = call(kernel, [(count, LANES)], [SMEM] + [VMEM] * 2)(idx, *gathered(sent))
        return rows

    local, gap, own, sent = call(
        local_kernel,
        [whole_shape, whole_shape, (4, 24, LANES), (24, LANES)],
        [SMEM] + [VMEM] * 4,
        [pltpu.VMEM(whole_shape, jnp.float32)] * 2,
    )(begin, *pieces)
    field, edges, total, mid, mid_gap, own, sent = call(
        fine_kernel,
        [whole_shape, (16, 512), (8, LANES), mid_shape, mid_shape, (4, 16, LANES), (16, LANES)],
        [SMEM] * 3 + [VMEM] * 7,
        [pltpu.VMEM((4, 32, LANES), jnp.float32)],
    )(coef[0], coef[1], idx, *around(picked(sent, pick_kernel, 32)), own, local, gap)
    rows = picked(sent, pick_mid_kernel, 64)
    rows, partner, orient = lax.optimization_barrier((rows, partner, orient))
    lanes = jnp.stack([partner, orient]).reshape(2, CHIPS, 2).transpose(0, 2, 1)
    lanes = jnp.where(core == 0, lanes, lanes[:, ::-1]).reshape(2, 64).astype(jnp.float32)
    lanes = jnp.concatenate([lanes, lanes], axis=1)
    doubled, sent, lanes = call(
        mid_kernel,
        [(4, 40, LANES), (SENT_ROWS, LANES), (2, LANES)],
        [SMEM] * 3 + [VMEM] * 10,
        [pltpu.VMEM((4, count, LANES), jnp.float32) for count in (20, 64)],
    )(coef[0], coef[1], idx, *around(rows), own, edges, total, mid, mid_gap, lanes)
    got = gathered(sent)
    corrected, one, two, norms = call(
        coarse_kernel,
        [(NV, 8, 512), (NV, 4, LANES), (NV, 2, 32), (1, 3)],
        [SMEM] * 2 + [VMEM] * 5,
    )(coef[2], idx, lanes, *[x.reshape(CHIPS * SENT_ROWS, LANES) for x in got], field, doubled)
    return (corrected[:, None], one[:, None], two[:, None], norms.reshape(3))


def solution(mesh):
    torus = Mesh(
        mesh.devices.reshape(4, 8, 2, mesh.shape["sub"]), ("blk_0", "blk_1", "blk_2", "sub")
    )
    split = P(None, BLK, "sub", None)
    return jax.shard_map(
        shards,
        mesh=torus,
        in_specs=(split, split, P(), P(), P(), P(), P()),
        out_specs=(split, split, split, P()),
        check_vma=False,
    )
```
